32 devices in a mesh: dp: 4 (over z), seq: 8 (over y, x, core).
Axes of the slice: x: 2, y: 2, z: 4, core: 2. Of those that a mesh axis runs over, the one named last changes fastest.
Arguments:
- inputs: bfloat16 [4, 6144, 768], P('dp', 'seq'), may hold values from -6 to 6
- lengths: int32 [4, 784], P('dp'), may hold values from 0 to 256, as said below
- w_query: bfloat16 [768, 768], replicated, may hold values from -0.21875 to 0.21875
- b_query: float32 [768], replicated, may hold values from -3 to 3
- w_key: bfloat16 [768, 768], replicated, may hold values from -0.21875 to 0.21875
- w_value: bfloat16 [768, 768], replicated, may hold values from -0.21875 to 0.21875
- b_value: float32 [768], replicated, may hold values from -3 to 3
- w_out: bfloat16 [768, 768], replicated, may hold values from -0.875 to 0.875
- b_out: float32 [768], replicated, may hold values from -3 to 3
- gain_one: float32 [768], replicated, may hold values from 0.5 to 1.5
- shift_one: float32 [768], replicated, may hold values from -1.2 to 1.2
- w_up: bfloat16 [768, 3072], replicated, may hold values from -0.21875 to 0.21875
- b_up: float32 [3072], replicated, may hold values from -3 to 3
- w_down: bfloat16 [3072, 768], replicated, may hold values from -0.109375 to 0.109375
- b_down: float32 [768], replicated, may hold values from -3 to 3
- gain_two: float32 [768], replicated, may hold values from 0.5 to 1.5
- shift_two: float32 [768], replicated, may hold values from -1.2 to 1.2
- d_output: bfloat16 [4, 6144, 768], P('dp', 'seq'), may hold values from -6 to 6
Outputs:
- output: bfloat16 [4, 6144, 768], P('dp', 'seq')
- d_inputs: float32 [4, 6144, 768], P('dp', 'seq')
- g_w_query: float32 [768, 768], replicated
- g_b_query: float32 [768], replicated
- g_w_key: float32 [768, 768], replicated
- g_w_value: float32 [768, 768], replicated
- g_b_value: float32 [768], replicated
- g_w_out: float32 [768, 768], replicated
- g_b_out: float32 [768], replicated
- g_gain_one: float32 [768], replicated
- g_shift_one: float32 [768], replicated
- g_w_up: float32 [768, 3072], replicated
- g_b_up: float32 [3072], replicated
- g_w_down: float32 [3072, 768], replicated
- g_b_down: float32 [768], replicated
- g_gain_two: float32 [768], replicated
- g_shift_two: float32 [768], replicated
The draws below stay inside these ranges and needn't reach their ends.
Inputs may be any that keep to these rules, and one draw needn't show every extreme that they name: `lengths`: every item has at most 256 tokens and each row has one of exactly 256; a zero length is an empty slot; each row ends with some padding.
All inputs are finite; a program needn't handle non-finite values.
Results may differ from the reference program's by a relative error of at most 0.014.
Values may be sent and summed in bfloat16 or wider, within the bound.
No kernel may reach another device: no remote copies, remote signals or barrier semaphores. Data moves between devices by JAX's collectives and lax.ppermute only.
A program may use at most 192 MiB of HBM per device.

```python
import math
import jax
import jax.numpy as jnp
from jax import lax

D = 768
HEADS = 12
HEAD_DIM = 64
FF = 3072
TOK_DEV = 768
ITEM_MOST = 256
SHORT_MOST = 32
SHORT_LEAST = 8
SLOTS_DEV = 98
ROW = 6144
BATCH = 4
N_SEQ = 8


def draw_lengths(key, part):
    key = jax.random.fold_in(key, 7)
    keys = jax.random.split(key, 5)
    per_dev = SLOTS_DEV - 1
    device_ids = jnp.arange(N_SEQ, dtype=jnp.int32)[None, :]
    cross = jax.random.randint(keys[0], (BATCH, N_SEQ), 2, ITEM_MOST + 1, dtype=jnp.int32)
    chosen = jax.random.randint(keys[1], (BATCH, 1), 0, N_SEQ - 1, dtype=jnp.int32)
    cross = jnp.where(device_ids == chosen, ITEM_MOST, cross)
    head = jax.random.randint(keys[2], (BATCH, N_SEQ), 1, cross, dtype=jnp.int32)
    padding = jax.random.randint(keys[3], (BATCH, 1), 1, TOK_DEV // 4 + 1, dtype=jnp.int32)
    last = device_ids == N_SEQ - 1
    cross = jnp.where(last, 0, cross)
    head = jnp.where(last, padding, head)
    tail = cross - head
    tail_before = jnp.concatenate([jnp.zeros((BATCH, 1), jnp.int32), tail[:, :-1]], axis=1)
    room = TOK_DEV - tail_before - head
    raw = jax.random.randint(keys[4], (BATCH, N_SEQ, per_dev), SHORT_LEAST, SHORT_MOST + 1, dtype=jnp.int32)
    earlier = jnp.cumsum(raw, axis=2) - raw
    shorts = jnp.clip(room[:, :, None] - earlier, 0, raw)
    lengths = jnp.concatenate([shorts, cross[:, :, None]], axis=2)
    return lengths.reshape(BATCH, N_SEQ * SLOTS_DEV).astype(jnp.int32)


def block_scale(key, extent, cuts, low, top_value):
    def one(dim, parts):
        steps = jax.random.uniform(jax.random.fold_in(jax.random.fold_in(key, 6), dim), (parts,), jnp.float32, low / len(cuts), top_value / len(cuts))
        return jnp.repeat(jnp.exp(steps), extent[dim] // parts).reshape((-1,) + (1,) * (len(extent) - dim - 1))

    loudness = one(*cuts[0])
    for cut in cuts[1:]:
        loudness = loudness * one(*cut)
    return loudness


def gaussian(own_key, shape, scale, most, cuts=(), held_as=jnp.bfloat16):
    level = block_scale(own_key, shape, cuts, -0.22, 0.18) if cuts else 1.0
    entries = jax.random.normal(own_key, shape, jnp.float32) * scale * level
    return jnp.minimum(jnp.maximum(entries, -most), most).astype(held_as)


def setup_inputs(seed: int = 0) -> dict:
    key_of = jax.random.split(jax.random.key(seed), 19)
    return {
        "inputs": gaussian(key_of[0], (BATCH, ROW, D), 1.0, 6.0, ((0, 4), (1, 8))),
        "lengths": draw_lengths(jax.random.fold_in(key_of[18], 71), 0),
        "w_query": gaussian(key_of[2], (D, D), D ** -0.5, 0.21875),
        "b_query": gaussian(key_of[3], (D,), 0.5, 3.0, (), jnp.float32),
        "w_key": gaussian(key_of[4], (D, D), D ** -0.5, 0.21875),
        "w_value": gaussian(key_of[5], (D, D), D ** -0.5, 0.21875),
        "b_value": gaussian(key_of[6], (D,), 0.5, 3.0, (), jnp.float32),
        "w_out": gaussian(key_of[7], (D, D), (D // 16) ** -0.5, 0.875),
        "b_out": gaussian(key_of[8], (D,), 0.5, 3.0, (), jnp.float32),
        "gain_one": jnp.clip(1.0 + 0.1 * jax.random.normal(key_of[9], (D,), jnp.float32), 0.5, 1.5),
        "shift_one": gaussian(key_of[10], (D,), 0.2, 1.2, (), jnp.float32),
        "w_up": gaussian(key_of[11], (D, FF), D ** -0.5, 0.21875),
        "b_up": gaussian(key_of[12], (FF,), 0.5, 3.0, (), jnp.float32),
        "w_down": gaussian(key_of[13], (FF, D), FF ** -0.5, 0.109375),
        "b_down": gaussian(key_of[14], (D,), 0.5, 3.0, (), jnp.float32),
        "gain_two": jnp.clip(1.0 + 0.1 * jax.random.normal(key_of[15], (D,), jnp.float32), 0.5, 1.5),
        "shift_two": gaussian(key_of[16], (D,), 0.2, 1.2, (), jnp.float32),
        "d_output": gaussian(key_of[17], (BATCH, ROW, D), 1.0, 6.0, ((0, 4), (1, 8))),
    }


@jax.custom_vjp
def low(v):
    return lax.optimization_barrier(v.astype(jnp.bfloat16)).astype(jnp.float32)

@jax.custom_vjp
def low_back(v):
    return v

def low_keep(v):
    return (low(v), None)

def low_pass(kept, grad):
    return (grad,)

def back_keep(v):
    return (v, None)

def back_low(kept, grad):
    return (low(grad),)
low.defvjp(low_keep, low_pass)
low_back.defvjp(back_keep, back_low)

def matmul(left, right):
    return jnp.dot(left, right, precision=lax.Precision.HIGHEST)

def norm_apply(hidden, gain, shift):
    mean = lax.optimization_barrier(jnp.mean(hidden, axis=-1, keepdims=True))
    centered = hidden - mean
    rstd = lax.rsqrt(lax.optimization_barrier(jnp.mean(centered * centered, axis=-1, keepdims=True)) + 1e-12)
    return centered * rstd * gain + shift

def attention_row(query, key, value, seg):
    count = query.shape[0]
    qblock = math.gcd(count, 512)
    reach = ITEM_MOST
    span = qblock + 2 * reach
    query_blocks = query.reshape(count // qblock, qblock, HEADS, HEAD_DIM)
    seg_blocks = seg.reshape(count // qblock, qblock)
    key_pad = jnp.pad(key, ((reach, reach), (0, 0))).reshape(count + 2 * reach, HEADS, HEAD_DIM)
    value_pad = jnp.pad(value, ((reach, reach), (0, 0))).reshape(count + 2 * reach, HEADS, HEAD_DIM)
    seg_pad = jnp.pad(seg, (reach, reach), constant_values=-1).astype(jnp.int32)
    starts = (jnp.arange(count // qblock) * qblock).astype(jnp.int32)

    def block(args):
        query_blk, seg_blk, start = args
        key_win = lax.dynamic_slice_in_dim(key_pad, start, span, 0)
        value_win = lax.dynamic_slice_in_dim(value_pad, start, span, 0)
        seg_win = lax.dynamic_slice_in_dim(seg_pad, start, span, 0)
        scores = jnp.einsum('qhd,khd->hqk', query_blk, key_win, precision=lax.Precision.HIGHEST) * 0.125
        scores = low_back(scores)
        allowed = seg_blk[:, None] == seg_win[None, :]
        scores = jnp.where(allowed[None], scores, -1e+30)
        probs = low(jax.nn.softmax(scores, axis=-1))
        return jnp.einsum('hqk,khd->qhd', probs, value_win, precision=lax.Precision.HIGHEST)
    result = lax.map(jax.checkpoint(block), (query_blocks, seg_blocks, starts))
    return result.reshape(count, HEADS * HEAD_DIM)

def row_forward(inputs, params, seg, valid):
    w_query, b_query, w_key, w_value, b_value, w_out, b_out, gain_one, shift_one, w_up, b_up, w_down, b_down, gain_two, shift_two = params
    query = low(low_back(matmul(inputs, w_query) + b_query))
    key = low(low_back(matmul(inputs, w_key)))
    value = low(low_back(matmul(inputs, w_value) + b_value))
    attn = low(low_back(attention_row(query, key, value, seg)))
    branch = low_back(matmul(attn, w_out) + b_out)
    mid = norm_apply(inputs + branch, gain_one, shift_one)
    mid_low = low(mid)
    up = low_back(matmul(mid_low, w_up) + b_up)
    act = low(jax.nn.gelu(up, approximate=False))
    down = low_back(matmul(act, w_down) + b_down)
    return norm_apply(mid + down, gain_two, shift_two) * valid[:, None]

def reference(inputs, lengths, w_query, b_query, w_key, w_value, b_value, w_out, b_out, gain_one, shift_one, w_up, b_up, w_down, b_down, gain_two, shift_two, d_output):
    params = tuple((p.astype(jnp.float32) for p in (w_query, b_query, w_key, w_value, b_value, w_out, b_out, gain_one, shift_one, w_up, b_up, w_down, b_down, gain_two, shift_two)))
    positions = jnp.arange(ROW, dtype=jnp.int32)
    zeros = tuple((jnp.zeros_like(p) for p in params))

    def per_row(totals, item):
        row_inputs, row_lengths, row_cotangent = item
        ends = jnp.cumsum(row_lengths).astype(jnp.int32)
        seg = jnp.searchsorted(ends, positions, side='right').astype(jnp.int32)
        valid = (positions < ends[-1]).astype(jnp.float32)

        def forward(values, weights):
            return row_forward(values, weights, seg, valid)
        result, back = jax.vjp(forward, row_inputs.astype(jnp.float32), params)
        d_row, d_params = back(row_cotangent.astype(jnp.float32))
        totals = tuple((a + b for a, b in zip(totals, d_params)))
        return (totals, (result.astype(jnp.bfloat16), d_row))
    totals, (output, d_inputs) = lax.scan(per_row, zeros, (inputs, lengths, d_output))
    return (output, d_inputs, totals[0], totals[1], totals[2], totals[3], totals[4], totals[5], totals[6], totals[7], totals[8], totals[9], totals[10], totals[11], totals[12], totals[13], totals[14])
```

```python
import functools

import jax
import jax.numpy as jnp
from jax import lax
from jax.experimental import pallas as pl
from jax.experimental.pallas import tpu as pltpu
from jax.sharding import PartitionSpec as P

HEADS = 12
HEAD_DIM = 64
ITEM_MOST = 256
EPS = 1e-12
SCALE = 0.125
MASKED = -1e30
FAR = 1e9
TILE = 128
PAIR = 2 * HEAD_DIM
WIDTHS = (256, 384, 640)
ROWS = 256
PARTS = 8
VMEM_MOST = 60 * 1024 * 1024

bf16 = jnp.bfloat16
f32 = jnp.float32
i32 = jnp.int32
ANY = pl.BlockSpec(memory_space=pl.ANY)
SMEM = pl.BlockSpec(memory_space=pltpu.SMEM)
VMEM = pl.BlockSpec(memory_space=pltpu.VMEM)


def params(**kw):
    return pltpu.CompilerParams(vmem_limit_bytes=VMEM_MOST, **kw)


def cost(flops, nbytes, trans=0):
    return pl.CostEstimate(flops=int(flops), bytes_accessed=int(nbytes), transcendentals=int(trans))


def mm(a, b):
    return lax.dot_general(a, b, (((1,), (0,)), ((), ())), preferred_element_type=f32)


def mm_nt(a, b):
    return lax.dot_general(a, b, (((1,), (1,)), ((), ())), preferred_element_type=f32)


def mm_tn(a, b):
    return lax.dot_general(a, b, (((0,), (0,)), ((), ())), preferred_element_type=f32)


def front_kernel(place, lengths, x, wq, wk, wv, bq, bv, q, k, v, se, spans, wbuf, sems):
    copies = [
        pltpu.make_async_copy(w, wbuf.at[i], sems.at[i]) for i, w in enumerate((wq, wk, wv))
    ]
    for c in copies:
        c.start()
    slots = lengths.shape[1]
    tokens = x.shape[0]
    ext = se.shape[1]
    reach = (ext - tokens) // 2
    step = max(d for d in range(8, 129, 8) if slots % d == 0)
    start = place[0] - reach
    pos = (lax.broadcasted_iota(i32, (1, ext), 1) + start).astype(f32)
    sizes = lengths[...].astype(f32)

    def scan(c, state):
        low, high = state
        index = lax.broadcasted_iota(i32, (step, slots), 0) + c * step
        upto = lax.broadcasted_iota(i32, (step, slots), 1) <= index
        ends = jnp.sum(jnp.where(upto, sizes, 0.0), axis=1, keepdims=True)
        before = ends <= pos
        low = jnp.maximum(low, jnp.max(jnp.where(before, ends, 0.0), axis=0, keepdims=True))
        high = jnp.minimum(high, jnp.min(jnp.where(before, FAR, ends), axis=0, keepdims=True))
        return low, high

    low, high = lax.fori_loop(
        0, slots // step, scan, (jnp.zeros((1, ext), f32), jnp.full((1, ext), FAR, f32))
    )
    real = (pos >= 0.0) & (high < FAR)
    local = lax.broadcasted_iota(i32, (1, ext), 1).astype(f32)
    offset = start.astype(f32)
    own = (local >= reach) & (local < reach + tokens)
    low_e = jnp.where(real, low - offset, local)
    high_e = jnp.where(real, high - offset, local + 1.0)
    shared = real & (
        ((local < reach) & (high_e > reach)) | ((local >= reach + tokens) & (low_e < reach + tokens))
    )
    used = own | shared
    low_e = jnp.where(used, low_e, 0.0)
    high_e = jnp.where(used, high_e, 0.0)
    se[0:1, :] = low_e
    se[1:2, :] = high_e
    spans[0] = jnp.sum(sizes).astype(i32)
    for t in range(ext // TILE):
        sl = slice(t * TILE, (t + 1) * TILE)
        some = high_e[:, sl] > low_e[:, sl]
        first = jnp.min(jnp.where(some, low_e[:, sl], FAR)).astype(i32)
        last = jnp.max(jnp.where(some, high_e[:, sl], -1.0)).astype(i32)
        at = first & ~15
        span = last - at
        kind = jnp.where(span <= WIDTHS[0], 1, jnp.where(span <= WIDTHS[1], 2, 3))
        wide = min(max(t * TILE - reach, 0), ext - WIDTHS[2])
        at = jnp.where(
            kind == 1,
            jnp.minimum(at, ext - WIDTHS[0]),
            jnp.where(kind == 2, jnp.minimum(at, ext - WIDTHS[1]), wide),
        )
        spans[8 + 2 * t] = jnp.where(last < 0, 0, kind)
        spans[9 + 2 * t] = at

    for i, (w, b, out) in enumerate(((wq, bq, q), (wk, None, k), (wv, bv, v))):
        copies[i].wait()

        def rows(r, _, i=i, b=b, out=out):
            at = pl.ds(pl.multiple_of(r * ROWS, ROWS), ROWS)
            y = mm(x[at, :], wbuf[i])
            if b is not None:
                y = y + b[...]
            y = y.astype(bf16)
            if out is q:
                y = y * bf16(SCALE)
            out[at, :] = y
            return 0

        lax.fori_loop(0, tokens // ROWS, rows, 0)


def front(place, lengths, x, wq, wk, wv, bq, bv, reach):
    tokens, width = x.shape
    ext = tokens + 2 * reach
    out = jax.ShapeDtypeStruct((tokens, width), bf16)
    return pl.pallas_call(
        front_kernel,
        out_shape=(
            out,
            out,
            out,
            jax.ShapeDtypeStruct((8, ext), f32),
            jax.ShapeDtypeStruct((8 + 2 * (ext // TILE),), i32),
        ),
        in_specs=[SMEM, VMEM, VMEM, ANY, ANY, ANY, VMEM, VMEM],
        out_specs=(VMEM, VMEM, VMEM, VMEM, SMEM),
        scratch_shapes=[pltpu.VMEM((3, width, width), bf16), pltpu.SemaphoreType.DMA((3,))],
        compiler_params=params(),
        cost_estimate=cost(6 * tokens * width * width, 8 * tokens * width),
        name="front",
    )(place, lengths, x, wq, wk, wv, bq, bv)


def tile_bias(se, t, at, width):
    base = pl.multiple_of(t * TILE, TILE)
    low = se[0:1, pl.ds(base, TILE)]
    high = se[1:2, pl.ds(base, TILE)]
    key = (lax.broadcasted_iota(i32, (width, TILE), 0) + at).astype(f32)
    one = jnp.where((key >= low) & (key < high), 0.0, MASKED)
    some = jnp.where(high > low, 1.0, 0.0)
    return jnp.concatenate([one, one], axis=1), jnp.concatenate([some, some], axis=1)


def stacked(pair):
    lane = lax.broadcasted_iota(i32, pair.shape, 1)
    zero = jnp.zeros_like(pair)
    return jnp.concatenate(
        [jnp.where(lane < HEAD_DIM, pair, zero), jnp.where(lane < HEAD_DIM, zero, pair)], axis=0
    )


def unstacked(both):
    own = jnp.concatenate([both[:HEAD_DIM, :TILE], both[HEAD_DIM:, TILE:]], axis=0)
    return own.T


def attend_kernel(spans, se, q, k, v, xl, xr, wk, wv, bv, attn, kh, vh, kx, vx, wbuf, sems):
    tokens, width = q.shape
    reach = xl.shape[0]
    copies = [
        pltpu.make_async_copy(wk, wbuf.at[0], sems.at[0]),
        pltpu.make_async_copy(wv, wbuf.at[1], sems.at[1]),
        pltpu.make_async_copy(k, kx.at[pl.ds(reach, tokens)], sems.at[2]),
        pltpu.make_async_copy(v, vx.at[pl.ds(reach, tokens)], sems.at[3]),
    ]
    for c in copies:
        c.start()
    copies[0].wait()
    for part, at in ((xl, 0), (xr, reach + tokens)):
        y = mm(part[...], wbuf[0]).astype(bf16)
        kx[at : at + reach, :] = y
        kh[(0 if at == 0 else reach) : (reach if at == 0 else 2 * reach), :] = y
    copies[1].wait()
    for part, at in ((xl, 0), (xr, reach + tokens)):
        y = (mm(part[...], wbuf[1]) + bv[...]).astype(bf16)
        vx[at : at + reach, :] = y
        vh[(0 if at == 0 else reach) : (reach if at == 0 else 2 * reach), :] = y
    copies[2].wait()
    copies[3].wait()

    def tile(t, at, span):
        bias, _ = tile_bias(se, t, at, span)
        rows = pl.ds(pl.multiple_of(t * TILE - reach, TILE), TILE)
        window = pl.ds(pl.multiple_of(at, 16), span)
        for p in range(width // PAIR):
            lanes = slice(p * PAIR, (p + 1) * PAIR)
            scores = mm_nt(kx[window, lanes], stacked(q[rows, lanes])) + bias
            top = jnp.max(scores, axis=0, keepdims=True)
            weights = jnp.exp(scores - top)
            total = jnp.sum(weights, axis=0, keepdims=True)
            both = mm_tn(vx[window, lanes], weights.astype(bf16)) / total
            attn[rows, lanes] = unstacked(both).astype(bf16)

    def each(t, _):
        kind, at = spans[8 + 2 * t], spans[9 + 2 * t]
        for i, span in enumerate(WIDTHS):
            pl.when(kind == i + 1)(functools.partial(tile, t, at, span))
        return 0

    lax.fori_loop(reach // TILE, (reach + tokens) // TILE, each, 0)


def attend(spans, se, q, k, v, xl, xr, wk, wv, bv):
    tokens, width = q.shape
    reach = xl.shape[0]
    ext = tokens + 2 * reach
    halo = jax.ShapeDtypeStruct((2 * reach, width), bf16)
    return pl.pallas_call(
        attend_kernel,
        out_shape=(jax.ShapeDtypeStruct((tokens, width), bf16), halo, halo),
        in_specs=[SMEM, VMEM, VMEM, ANY, ANY, VMEM, VMEM, ANY, ANY, VMEM],
        out_specs=(VMEM, VMEM, VMEM),
        scratch_shapes=[
            pltpu.VMEM((ext, width), bf16),
            pltpu.VMEM((ext, width), bf16),
            pltpu.VMEM((2, width, width), bf16),
            pltpu.SemaphoreType.DMA((4,)),
        ],
        compiler_params=params(),
        cost_estimate=cost(8e9, 12 * tokens * width),
        name="attend",
    )(spans, se, q, k, v, xl, xr, wk, wv, bv)


def attend_back_kernel(
    spans, se, q, k, v, do, kh, vh, xl, xr, dl, dr, wq, bq, dq, dk, dv, qx, kx, vx, dox, dkx, dvx, wbuf, sems
):
    tokens, width = q.shape
    reach = xl.shape[0]
    ext = kx.shape[0]
    own, low, high = pl.ds(reach, tokens), pl.ds(0, reach), pl.ds(reach + tokens, reach)
    pairs = [
        (wq, wbuf),
        (q, qx.at[own]),
        (k, kx.at[own]),
        (v, vx.at[own]),
        (do, dox.at[own]),
        (kh.at[pl.ds(0, reach)], kx.at[low]),
        (kh.at[pl.ds(reach, reach)], kx.at[high]),
        (vh.at[pl.ds(0, reach)], vx.at[low]),
        (vh.at[pl.ds(reach, reach)], vx.at[high]),
        (dl, dox.at[low]),
        (dr, dox.at[high]),
    ]
    copies = [pltpu.make_async_copy(a, b, sems.at[i]) for i, (a, b) in enumerate(pairs)]
    for c in copies:
        c.start()
    dkx[...] = jnp.zeros_like(dkx)
    dvx[...] = jnp.zeros_like(dvx)
    copies[0].wait()
    for part, at in ((xl, 0), (xr, reach + tokens)):
        y = (mm(part[...], wbuf[...]) + bq[...]).astype(bf16)
        qx[at : at + reach, :] = y * bf16(SCALE)
    for c in copies[1:]:
        c.wait()

    def tile(t, at, span):
        bias, some = tile_bias(se, t, at, span)
        rows = pl.ds(pl.multiple_of(t * TILE, TILE), TILE)
        window = pl.ds(pl.multiple_of(at, 16), span)
        inside = (t >= reach // TILE) & (t < (reach + tokens) // TILE)
        for p in range(width // PAIR):
            lanes = slice(p * PAIR, (p + 1) * PAIR)
            key, value = kx[window, lanes], vx[window, lanes]
            query, dout = stacked(qx[rows, lanes]), stacked(dox[rows, lanes])
            scores = mm_nt(key, query) + bias
            top = jnp.max(scores, axis=0, keepdims=True)
            weights = jnp.exp(scores - top)
            total = jnp.sum(weights, axis=0, keepdims=True)
            probs = weights * (some / total)
            dprob = mm_nt(value, dout)
            delta = jnp.sum(probs * dprob, axis=0, keepdims=True)
            dscore = (probs * (dprob - delta)).astype(bf16)
            dvx[window, lanes] += mm(probs.astype(bf16), dout)
            dkx[window, lanes] += mm(dscore, query)

            @pl.when(inside)
            def _(key=key, dscore=dscore, lanes=lanes):
                here = pl.ds(pl.multiple_of(t * TILE - reach, TILE), TILE)
                dq[here, lanes] = (unstacked(mm_tn(key, dscore)) * SCALE).astype(bf16)

    def each(t, _):
        kind, at = spans[8 + 2 * t], spans[9 + 2 * t]
        for i, span in enumerate(WIDTHS):
            pl.when(kind == i + 1)(functools.partial(tile, t, at, span))
        return 0

    lax.fori_loop(0, ext // TILE, each, 0)
    dk[...] = dkx[reach : reach + tokens, :].astype(bf16)
    dv[...] = dvx[reach : reach + tokens, :].astype(bf16)


def attend_back(spans, se, q, k, v, do, kh, vh, xl, xr, dl, dr, wq, bq):
    tokens, width = q.shape
    reach = xl.shape[0]
    ext = tokens + 2 * reach
    out = jax.ShapeDtypeStruct((tokens, width), bf16)
    return pl.pallas_call(
        attend_back_kernel,
        out_shape=(out, out, out),
        in_specs=[SMEM, VMEM] + [ANY] * 6 + [VMEM, VMEM] + [ANY] * 3 + [VMEM],
        out_specs=(VMEM, VMEM, VMEM),
        scratch_shapes=[pltpu.VMEM((ext, width), bf16)] * 4
        + [pltpu.VMEM((ext, width), f32)] * 2
        + [pltpu.VMEM((width, width), bf16), pltpu.SemaphoreType.DMA((11,))],
        compiler_params=params(),
        cost_estimate=cost(16e9, 20 * tokens * width),
        name="attend_back",
    )(spans, se, q, k, v, do, kh, vh, xl, xr, dl, dr, wq, bq)


def write_group(block, send, keep, buf, sems, place):
    here, layer = place[1], place[2]
    half = buf.shape[1] // 2
    layers = place_layers(half)
    chunk = half // layers

    def copies(slot, x, y, out):
        return (
            pltpu.make_async_copy(
                buf.at[slot, pl.ds(0, half)],
                out.at[pl.ds(pl.multiple_of((2 * x + y) * half, half), half)],
                sems.at[slot, 0],
            ),
            pltpu.make_async_copy(
                buf.at[slot, pl.ds(half, half)],
                out.at[pl.ds(pl.multiple_of((4 + 2 * y + x) * half, half), half)],
                sems.at[slot, 1],
            ),
        )

    for core, out in ((1, send), (0, keep)):

        def step(j, _, core=core, out=out):
            x, y = j & 1, j >> 1
            part = (core + 2 * x + 4 * y) ^ here
            slot = j & 1
            value = block(part).astype(bf16)

            def free():
                for c in copies(slot, x, y, out):
                    c.wait()

            if core == 1:
                pl.when(j >= 2)(free)
            else:
                free()
            for z in range(layers):
                to = (z ^ layer) * chunk
                buf[slot, pl.ds(pl.multiple_of(to, chunk), chunk), :] = value[z * chunk : (z + 1) * chunk]
                buf[slot, pl.ds(pl.multiple_of(half + to, chunk), chunk), :] = value[
                    half + z * chunk : half + (z + 1) * chunk
                ]
            for c in copies(slot, x, y, out):
                c.start()
            return 0

        lax.fori_loop(0, PARTS // 2, step, 0)
    for slot in range(2):
        for c in copies(slot, 0, 0, keep):
            c.wait()


LAYERS = [4]


def place_layers(half):
    return LAYERS[0]


def group_shapes(rows, width):
    return (jax.ShapeDtypeStruct((rows // 2, width), bf16),) * 2


def group_scratch(rows, width):
    return [pltpu.VMEM((2, rows // PARTS, width), bf16), pltpu.SemaphoreType.DMA((2, 2))]


def gelu_both(z):
    u = jnp.abs(z) * 0.7071067811865476
    t = 1.0 / (1.0 + 0.3275911 * u)
    bell = jnp.exp(-0.5 * z * z)
    poly = t * (
        0.5 * 0.254829592
        + t * (0.5 * -0.284496736 + t * (0.5 * 1.421413741 + t * (0.5 * -1.453152027 + t * (0.5 * 1.061405429))))
    )
    tail = poly * bell
    cdf = jnp.where(z >= 0.0, 1.0 - tail, tail)
    return z * cdf, cdf + z * bell * 0.3989422804014327


def center(v):
    mean = jnp.mean(v, axis=1, keepdims=True)
    c = v - mean
    rstd = lax.rsqrt(jnp.mean(c * c, axis=1, keepdims=True) + EPS)
    return c * rstd, rstd


def center_back(e, xhat, rstd):
    return rstd * (
        e - jnp.mean(e, axis=1, keepdims=True) - xhat * jnp.mean(e * xhat, axis=1, keepdims=True)
    )


def colsum(v):
    return jnp.sum(v, axis=0, keepdims=True)


def chain_kernel(
    place, spans, attn, x, dy, wo, wu, wd, bo, g1, s1, bu, bd, g2, s2,
    out, slope, mid_low, xhat1, rstd1, d_two, d_down, vec, send, keep,
    wo_b, wu_b, wd_b, act, dd, buf, wsems, gsems,
):
    i = pl.program_id(0)
    ff = wu.shape[1]
    width = x.shape[1]
    copies = [
        pltpu.make_async_copy(a, b, wsems.at[n]) for n, (a, b) in enumerate(((wo, wo_b), (wu, wu_b), (wd, wd_b)))
    ]

    @pl.when(i == 0)
    def _():
        for c in copies:
            c.start()
        vec[...] = jnp.zeros_like(vec)
        copies[0].wait()

    one = x[...].astype(f32) + mm(attn[...], wo_b[...]) + bo[...]
    xh1, r1 = center(one)
    mid = xh1 * g1[...] + s1[...]
    low = mid.astype(bf16)
    xhat1[...] = xh1
    rstd1[...] = jnp.broadcast_to(r1, rstd1.shape)
    mid_low[...] = low

    @pl.when(i == 0)
    def _():
        copies[1].wait()
        copies[2].wait()

    rows = pl.ds(pl.multiple_of(i * ROWS, ROWS), ROWS)
    two = mid + bd[...]
    step = 512
    for c in range(ff // step):
        cols = slice(c * step, (c + 1) * step)
        a, s = gelu_both(mm(low, wu_b[:, cols]) + bu[:, cols])
        a = a.astype(bf16)
        act[rows, cols] = a
        slope[:, cols] = s.astype(bf16)
        two = two + mm(a, wd_b[cols, :])
    xh2, r2 = center(two)
    token = place[0] + i * ROWS + lax.broadcasted_iota(i32, (ROWS, 1), 0)
    valid = jnp.where(token < spans[0], 1.0, 0.0)
    out[...] = ((xh2 * g2[...] + s2[...]) * valid).astype(bf16)
    d = dy[...].astype(f32) * valid
    vec[1:2, :] += colsum(d * xh2)
    vec[2:3, :] += colsum(d)
    d2 = center_back(d * g2[...], xh2, r2)
    d_two[...] = d2
    d2 = d2.astype(bf16)
    d_down[...] = d2
    dd[rows, :] = d2
    vec[0:1, :] += colsum(d2.astype(f32))

    @pl.when(i == pl.num_programs(0) - 1)
    def _():
        size = ff // PARTS

        def block(part):
            return mm_tn(act[:, pl.ds(pl.multiple_of(part * size, size), size)], dd[...])

        write_group(block, send, keep, buf, gsems, place)


def chain(place, spans, attn, x, dy, wo, wu, wd, bo, g1, s1, bu, bd, g2, s2):
    tokens, width = x.shape
    ff = wu.shape[1]
    tok = lambda n: pl.BlockSpec((ROWS, n), lambda i: (i, 0))
    row = lambda n: pl.BlockSpec((1, n), lambda i: (0, 0))
    shape = lambda n, t: jax.ShapeDtypeStruct((tokens, n), t)
    return pl.pallas_call(
        chain_kernel,
        grid=(tokens // ROWS,),
        out_shape=(
            shape(width, bf16),
            shape(ff, bf16),
            shape(width, bf16),
            shape(width, f32),
            shape(128, f32),
            shape(width, f32),
            shape(width, bf16),
            jax.ShapeDtypeStruct((8, width), f32),
        )
        + group_shapes(ff, width),
        in_specs=[SMEM, SMEM, tok(width), tok(width), tok(width), ANY, ANY, ANY]
        + [row(width), row(width), row(width), row(ff), row(width), row(width), row(width)],
        out_specs=(
            tok(width),
            tok(ff),
            tok(width),
            tok(width),
            tok(128),
            tok(width),
            tok(width),
            pl.BlockSpec((8, width), lambda i: (0, 0)),
            ANY,
            ANY,
        ),
        scratch_shapes=[
            pltpu.VMEM((width, width), bf16),
            pltpu.VMEM((width, ff), bf16),
            pltpu.VMEM((ff, width), bf16),
            pltpu.VMEM((tokens, ff), bf16),
            pltpu.VMEM((tokens, width), bf16),
        ]
        + group_scratch(ff, width)[:1]
        + [pltpu.SemaphoreType.DMA((3,))]
        + group_scratch(ff, width)[1:],
        compiler_params=params(dimension_semantics=("arbitrary",)),
        cost_estimate=cost(2 * tokens * width * (width + 3 * ff), 30 * tokens * width, 2 * tokens * ff),
        name="chain",
    )(place, spans, attn, x, dy, wo, wu, wd, bo, g1, s1, bu, bd, g2, s2)


def back_kernel(
    d_two, d_down, slope, xhat1, rstd1, wd, wu, wo, g1,
    d_up, d_one, d_branch, d_attn, vec, wd_b, wu_b, wo_b, wsems,
):
    i = pl.program_id(0)
    ff = wu.shape[1]
    width = d_two.shape[1]
    copies = [
        pltpu.make_async_copy(a, b, wsems.at[n]) for n, (a, b) in enumerate(((wd, wd_b), (wu, wu_b), (wo, wo_b)))
    ]

    @pl.when(i == 0)
    def _():
        for c in copies:
            c.start()
        vec[...] = jnp.zeros_like(vec)
        for c in copies:
            c.wait()

    d_mid = d_two[...]
    dd = d_down[...]
    step = width
    for c in range(ff // step):
        cols = slice(c * step, (c + 1) * step)
        du = (slope[:, cols].astype(f32) * mm_nt(dd, wd_b[cols, :])).astype(bf16)
        d_up[:, cols] = du
        vec[3 + c : 4 + c, :] += colsum(du.astype(f32))
        d_mid = d_mid + mm_nt(du, wu_b[:, cols])
    xh = xhat1[...]
    vec[0:1, :] += colsum(d_mid * xh)
    vec[1:2, :] += colsum(d_mid)
    d1 = center_back(d_mid * g1[...], xh, rstd1[:, 0:1])
    d_one[...] = d1
    d1 = d1.astype(bf16)
    d_branch[...] = d1
    vec[2:3, :] += colsum(d1.astype(f32))
    d_attn[...] = mm_nt(d1, wo_b[...]).astype(bf16)


def back(d_two, d_down, slope, xhat1, rstd1, wd, wu, wo, g1):
    tokens, width = d_two.shape
    ff = wu.shape[1]
    tok = lambda n: pl.BlockSpec((ROWS, n), lambda i: (i, 0))
    shape = lambda n, t: jax.ShapeDtypeStruct((tokens, n), t)
    return pl.pallas_call(
        back_kernel,
        grid=(tokens // ROWS,),
        out_shape=(
            shape(ff, bf16),
            shape(width, f32),
            shape(width, bf16),
            shape(width, bf16),
            jax.ShapeDtypeStruct((8, width), f32),
        ),
        in_specs=[tok(width), tok(width), tok(ff), tok(width), tok(128), ANY, ANY, ANY]
        + [pl.BlockSpec((1, width), lambda i: (0, 0))],
        out_specs=(tok(ff), tok(width), tok(width), tok(width), pl.BlockSpec((8, width), lambda i: (0, 0))),
        scratch_shapes=[
            pltpu.VMEM((ff, width), bf16),
            pltpu.VMEM((width, ff), bf16),
            pltpu.VMEM((width, width), bf16),
            pltpu.SemaphoreType.DMA((3,)),
        ],
        compiler_params=params(dimension_semantics=("arbitrary",)),
        cost_estimate=cost(2 * tokens * width * (width + 2 * ff), 30 * tokens * width),
        name="back",
    )(d_two, d_down, slope, xhat1, rstd1, wd, wu, wo, g1)


def up_grad_kernel(place, mid_low, d_up, send, keep, buf, gsems):
    tokens, width = mid_low.shape
    size = width // 2

    def block(part):
        a = mid_low[:, pl.ds(pl.multiple_of((part & 1) * size, size), size)]
        b = d_up[:, pl.ds(pl.multiple_of((part >> 1) * width, width), width)]
        return mm_tn(a, b)

    write_group(block, send, keep, buf, gsems, place)


def up_grad(place, mid_low, d_up):
    tokens, width = mid_low.shape
    ff = d_up.shape[1]
    return pl.pallas_call(
        up_grad_kernel,
        out_shape=group_shapes(ff, width),
        in_specs=[SMEM, VMEM, VMEM],
        out_specs=(ANY, ANY),
        scratch_shapes=group_scratch(ff, width),
        compiler_params=params(),
        cost_estimate=cost(2 * tokens * width * ff, 14 * tokens * width),
        name="up_grad",
    )(place, mid_low, d_up)


def rest_grad_kernel(place, attn, x, d_branch, dq, dk, dv, vec, send, keep, lhs, rhs, buf, gsems, sems):
    tokens, width = x.shape
    size = width // 2
    pairs = [(attn, lhs.at[0]), (d_branch, rhs.at[0]), (x, lhs.at[1]), (dq, rhs.at[1]), (dk, rhs.at[2]), (dv, rhs.at[3])]
    copies = [pltpu.make_async_copy(a, b, sems.at[i]) for i, (a, b) in enumerate(pairs)]
    for c in copies:
        c.start()
    for c in copies:
        c.wait()
    ones = jnp.ones((8, tokens), bf16)
    vec[0:1, :] = mm(ones, rhs[1])[0:1]
    vec[1:2, :] = mm(ones, rhs[3])[0:1]
    vec[2:8, :] = jnp.zeros((6, width), f32)

    def block(part):
        which = part >> 1
        a = lhs[jnp.minimum(which, 1), :, pl.ds(pl.multiple_of((part & 1) * size, size), size)]
        return mm_tn(a, rhs[which])

    write_group(block, send, keep, buf, gsems, place)


def rest_grad(place, attn, x, d_branch, dq, dk, dv):
    tokens, width = x.shape
    rows = 4 * width
    return pl.pallas_call(
        rest_grad_kernel,
        out_shape=(jax.ShapeDtypeStruct((8, width), f32),) + group_shapes(rows, width),
        in_specs=[SMEM] + [ANY] * 6,
        out_specs=(VMEM, ANY, ANY),
        scratch_shapes=[pltpu.VMEM((2, tokens, width), bf16), pltpu.VMEM((4, tokens, width), bf16)]
        + group_scratch(rows, width)
        + [pltpu.SemaphoreType.DMA((6,))],
        compiler_params=params(),
        cost_estimate=cost(8 * tokens * width * width, 20 * tokens * width),
        name="rest_grad",
    )(place, attn, x, d_branch, dq, dk, dv)


def inputs_grad_kernel(d_one, dq, dk, dv, wq, wk, wv, out):
    out[...] = d_one[...] + mm_nt(dq[...], wq[...]) + mm_nt(dk[...], wk[...]) + mm_nt(dv[...], wv[...])


def inputs_grad(d_one, dq, dk, dv, wq, wk, wv):
    tokens, width = d_one.shape
    tok = pl.BlockSpec((ROWS, width), lambda i: (i, 0))
    full = pl.BlockSpec((width, width), lambda i: (0, 0))
    return pl.pallas_call(
        inputs_grad_kernel,
        grid=(tokens // ROWS,),
        out_shape=jax.ShapeDtypeStruct((tokens, width), f32),
        in_specs=[tok] * 4 + [full] * 3,
        out_specs=tok,
        compiler_params=params(dimension_semantics=("arbitrary",)),
        cost_estimate=cost(6 * tokens * width * width, 20 * tokens * width),
        name="inputs_grad",
    )(d_one, dq, dk, dv, wq, wk, wv)


def swap(value, axis, bit):
    count = lax.axis_size(axis)
    return lax.ppermute(value, axis, [(i, i ^ bit) for i in range(count)])


def plus(a, b):
    return (a.astype(f32) + b.astype(f32)).astype(bf16)


def layer_bits():
    return list(range(1, lax.axis_size("dp")))


def far_bits():
    bit, bits = PARTS, []
    while bit < lax.axis_size("seq"):
        bits.append(bit)
        bit *= 2
    return bits


def scatter_sum(send, keep):
    width = send.shape[-1]
    layers = lax.axis_size("dp")
    shape = (2, 2, 2, layers, send.shape[0] // (8 * layers), width)
    got = swap(send, "seq", 1)
    both = plus(keep, got).reshape(shape)
    a, b = both[0], both[1]
    ra, rb = swap(a[1], "seq", 2), swap(b[1], "seq", 4)
    a, b = plus(a[0], ra), plus(b[0], rb)
    ra, rb = swap(a[1], "seq", 4), swap(b[1], "seq", 2)
    a, b = plus(a[0], ra), plus(b[0], rb)
    both = jnp.stack([a, b], axis=1)
    terms = [both[0].astype(f32)] + [swap(both[d], "dp", d).astype(f32) for d in layer_bits()]
    while len(terms) > 1:
        terms = [terms[i] + terms[i + 1] for i in range(0, len(terms), 2)]
    total = terms[0].astype(bf16)
    for bit in far_bits():
        total = plus(total, swap(total, "seq", bit))
    return total


def gather_all(total):
    both = jnp.stack([total] + [swap(total, "dp", d) for d in layer_bits()], axis=0)
    a, b = both[:, 0], both[:, 1]
    a, b = jnp.stack([a, swap(a, "seq", 4)]), jnp.stack([b, swap(b, "seq", 2)])
    a, b = jnp.stack([a, swap(a, "seq", 2)]), jnp.stack([b, swap(b, "seq", 4)])
    mine = jnp.stack([a, b])
    mine = mine.reshape(8, -1, mine.shape[-1])
    return mine, swap(mine, "seq", 1)


def spread_kernel(kind, place, ma, mb, oa, ob, *refs):
    outs, (buf, sems) = refs[:-2], refs[-2:]
    j = pl.program_id(0)
    here, layer = place[1], place[2]
    half = ma.shape[1]
    size = 2 * half
    layers = LAYERS[0]
    chunk = half // layers
    width = ma.shape[2]

    def copies(step):
        part = step ^ here
        slot = step & 1
        src = buf.at[slot]
        if kind == "down":
            return [(None, pltpu.make_async_copy(src, outs[0].at[pl.ds(pl.multiple_of(part * size, size), size)], sems.at[slot]))]
        at = pl.ds(pl.multiple_of((part & 1) * size, size), size)
        which = part >> 1
        if kind == "up":
            cols = pl.ds(pl.multiple_of(which * width, width), width)
            return [(None, pltpu.make_async_copy(src, outs[0].at[at, cols], sems.at[slot]))]
        return [(which == n, pltpu.make_async_copy(src, o.at[at], sems.at[slot])) for n, o in enumerate(outs)]

    def start(step):
        for cond, c in copies(step):
            if cond is None:
                c.start()
            else:
                pl.when(cond)(c.start)

    def wait(step):
        copies(step)[0][1].wait()

    pl.when(j >= 2)(lambda: wait(j - 2))
    slot = j & 1

    def fill(a, b):
        for z in range(layers):
            to = (z ^ layer) * chunk
            rows = slice(z * chunk, (z + 1) * chunk)
            buf[slot, pl.ds(pl.multiple_of(to, chunk), chunk), :] = a[0, rows, :].astype(f32)
            buf[slot, pl.ds(pl.multiple_of(half + to, chunk), chunk), :] = b[0, rows, :].astype(f32)

    pl.when((j & 1) == 0)(lambda: fill(ma, mb))
    pl.when((j & 1) == 1)(lambda: fill(oa, ob))
    start(j)

    @pl.when(j == PARTS - 1)
    def _():
        wait(j - 1)
        wait(j)


def spread(kind, place, mine, other):
    half, width = mine.shape[1:]
    rows = 2 * half * PARTS
    a = pl.BlockSpec((1, half, width), lambda j: (2 * ((j >> 1) & 1) + (j >> 2), 0, 0))
    b = pl.BlockSpec((1, half, width), lambda j: (4 + 2 * (j >> 2) + ((j >> 1) & 1), 0, 0))
    if kind == "down":
        shapes = [(rows, width)]
    elif kind == "up":
        shapes = [(width, rows)]
    else:
        shapes = [(width, width)] * 4
    return pl.pallas_call(
        functools.partial(spread_kernel, kind),
        grid=(PARTS,),
        out_shape=[jax.ShapeDtypeStruct(s, f32) for s in shapes],
        in_specs=[SMEM, a, b, a, b],
        out_specs=[ANY] * len(shapes),
        scratch_shapes=[pltpu.VMEM((2, 2 * half, width), f32), pltpu.SemaphoreType.DMA((2,))],
        compiler_params=params(dimension_semantics=("arbitrary",)),
        cost_estimate=cost(rows * width, 6 * rows * width),
        name="spread_" + kind,
    )(place, mine, mine, other, other)


def sum_small(vec):
    for axis in ("seq", "dp"):
        bit = 1
        while bit < lax.axis_size(axis):
            vec = vec + swap(vec, axis, bit)
            bit *= 2
    return vec


def neighbours(value, reach):
    count = lax.axis_size("seq")
    up = [(i, i + 1) for i in range(count - 1)]
    low = lax.ppermute(value[-reach:], "seq", up)
    high = lax.ppermute(value[:reach], "seq", [(b, a) for a, b in up])
    return low, high


def body(
    inputs, lengths, w_query, b_query, w_key, w_value, b_value, w_out, b_out, gain_one, shift_one,
    w_up, b_up, w_down, b_down, gain_two, shift_two, d_output,
):
    rows, tokens, width = inputs.shape
    reach = ITEM_MOST
    LAYERS[0] = lax.axis_size("dp")
    here = lax.axis_index("seq")
    place = jnp.stack([here * tokens, here & (PARTS - 1), lax.axis_index("dp")]).astype(i32)
    x = inputs.reshape(tokens, width)
    dy = d_output.reshape(tokens, width)
    line = lambda v: v.reshape(1, -1)

    xl, xr = neighbours(x, reach)
    q, k, v, se, spans = front(place, lengths, x, w_query, w_key, w_value, line(b_query), line(b_value), reach)
    attn, kh, vh = attend(spans, se, q, k, v, xl, xr, w_key, w_value, line(b_value))
    output, slope, mid_low, xhat1, rstd1, d_two, d_down, vec_a, send1, keep1 = chain(
        place, spans, attn, x, dy, w_out, w_up, w_down, line(b_out), line(gain_one), line(shift_one),
        line(b_up), line(b_down), line(gain_two), line(shift_two),
    )
    d_up, d_one, d_branch, d_attn, vec_b = back(
        d_two, d_down, slope, xhat1, rstd1, w_down, w_up, w_out, line(gain_one)
    )
    dl, dr = neighbours(d_attn, reach)
    send2, keep2 = up_grad(place, mid_low, d_up)
    dq, dk, dv = attend_back(spans, se, q, k, v, d_attn, kh, vh, xl, xr, dl, dr, w_query, line(b_query))
    vec_c, send3, keep3 = rest_grad(place, attn, x, d_branch, dq, dk, dv)
    d_inputs = inputs_grad(d_one, dq, dk, dv, w_query, w_key, w_value)

    (g_w_down,) = spread("down", place, *gather_all(scatter_sum(send1, keep1)))
    (g_w_up,) = spread("up", place, *gather_all(scatter_sum(send2, keep2)))
    g_w_out, g_w_query, g_w_key, g_w_value = spread("rest", place, *gather_all(scatter_sum(send3, keep3)))
    small = sum_small(jnp.concatenate([vec_a, vec_b, vec_c], axis=0))
    ff = w_up.shape[1]
    many = ff // width
    return (
        output.reshape(rows, tokens, width),
        d_inputs.reshape(rows, tokens, width),
        g_w_query,
        small[16],
        g_w_key,
        g_w_value,
        small[17],
        g_w_out,
        small[10],
        small[8],
        small[9],
        g_w_up,
        small[11 : 11 + many].reshape(ff),
        g_w_down,
        small[0],
        small[1],
        small[2],
    )


def solution(mesh):
    split, whole = P("dp", "seq", None), P()
    return jax.shard_map(
        body,
        mesh=mesh,
        in_specs=(split, P("dp", None)) + (whole,) * 15 + (split,),
        out_specs=(split, split) + (whole,) * 15,
        check_vma=False,
    )
```

```python
import functools

import jax
import jax.numpy as jnp
from jax import lax
from jax.experimental import pallas as pl
from jax.experimental.pallas import tpu as pltpu
from jax.sharding import PartitionSpec as P

HEADS = 12
HEAD_DIM = 64
ITEM_MOST = 256
EPS = 1e-12
SCALE = 0.125
MASKED = -1e30
FAR = 1e9
TILE = 128
PAIR = 2 * HEAD_DIM
WIDTHS = (256, 384, 640)
ROWS = 256
SMALL = 32
ORDER = (23, 1, 2, 1, 3, 2, 1, 3, 2, 1, 3, 2, 3, 1, 2, 3, 1, -1, 3, 2, 2, 3, -2, 3, 3, -3)
HALVES = 2
PARTS = 8
CHUNK = 512

bf16 = jnp.bfloat16
f32 = jnp.float32
i32 = jnp.int32
ANY = pl.BlockSpec(memory_space=pl.ANY)
HBM = pl.BlockSpec(memory_space=pltpu.HBM)
SMEM = pl.BlockSpec(memory_space=pltpu.SMEM)
VMEM = pl.BlockSpec(memory_space=pltpu.VMEM)


def params(mib, **kw):
    return pltpu.CompilerParams(vmem_limit_bytes=mib * 1024 * 1024, **kw)


def cost(flops, nbytes, trans=0):
    return pl.CostEstimate(flops=int(flops), bytes_accessed=int(nbytes), transcendentals=int(trans))


def mm(a, b):
    return lax.dot_general(a, b, (((1,), (0,)), ((), ())), preferred_element_type=f32)


def mm_nt(a, b):
    return lax.dot_general(a, b, (((1,), (1,)), ((), ())), preferred_element_type=f32)


def mm_tn(a, b):
    return lax.dot_general(a, b, (((0,), (0,)), ((), ())), preferred_element_type=f32)


def large(a):
    return a.size * a.dtype.itemsize > 512 * 1024


def call(kernel, out_shape, in_specs, out_specs, after=(), **kw):
    shapes = [
        pltpu.HBM(o.shape, o.dtype) if spec is HBM or large(o) else o for o, spec in zip(out_shape, out_specs)
    ]
    count = len(in_specs)

    def plain(*refs):
        return kernel(*refs[:count], *refs[count + len(after) :])

    specs = list(in_specs) + [ANY] * len(after)
    run = pl.pallas_call(plain, out_shape=shapes, in_specs=specs, out_specs=list(out_specs), **kw)

    def apply(*args):
        args = [
            pltpu.with_memory_space_constraint(a, pltpu.HBM) if spec is HBM or large(a) else a
            for a, spec in zip(args, in_specs)
        ]
        return run(*args, *after)

    return apply


def loads(pairs, sems):
    copies = [pltpu.make_async_copy(a, b, sems.at[i]) for i, (a, b) in enumerate(pairs)]
    for c in copies:
        c.start()
    return lambda i: copies[i].wait()


def out_copy(source, target, sem):
    c = pltpu.make_async_copy(source, target, sem)
    c.start()
    return c


def row_blocks(tokens):
    return [slice(r, r + ROWS) for r in range(0, tokens, ROWS)]


def front_kernel(
    place, lengths, bq, bv, x, wq, wk, wv, se, spans, q, k, v, xb, wb, ob, sems, osems
):
    ready = loads([(x, xb), (wq, wb.at[0]), (wk, wb.at[1]), (wv, wb.at[2])], sems)
    slots = lengths.shape[1]
    tokens = x.shape[0]
    ext = se.shape[1]
    reach = (ext - tokens) // 2
    step = max(d for d in range(8, 129, 8) if slots % d == 0)
    start = place[0] - reach
    pos = (lax.broadcasted_iota(i32, (1, ext), 1) + start).astype(f32)
    sizes = lengths[...].astype(f32)

    def scan(c, state):
        low, high = state
        index = lax.broadcasted_iota(i32, (step, slots), 0) + c * step
        upto = lax.broadcasted_iota(i32, (step, slots), 1) <= index
        ends = jnp.sum(jnp.where(upto, sizes, 0.0), axis=1, keepdims=True)
        before = ends <= pos
        low = jnp.maximum(low, jnp.max(jnp.where(before, ends, 0.0), axis=0, keepdims=True))
        high = jnp.minimum(high, jnp.min(jnp.where(before, FAR, ends), axis=0, keepdims=True))
        return low, high

    low, high = lax.fori_loop(
        0, slots // step, scan, (jnp.zeros((1, ext), f32), jnp.full((1, ext), FAR, f32))
    )
    real = (pos >= 0.0) & (high < FAR)
    local = lax.broadcasted_iota(i32, (1, ext), 1).astype(f32)
    offset = start.astype(f32)
    own = (local >= reach) & (local < reach + tokens)
    low_e = jnp.where(real, low - offset, local)
    high_e = jnp.where(real, high - offset, local + 1.0)
    shared = real & (
        ((local < reach) & (high_e > reach)) | ((local >= reach + tokens) & (low_e < reach + tokens))
    )
    used = own | shared
    low_e = jnp.where(used, low_e, 0.0)
    high_e = jnp.where(used, high_e, 0.0)
    se[0:1, :] = low_e
    se[1:2, :] = high_e
    spans[0] = jnp.sum(sizes).astype(i32)
    for t in range(ext // TILE):
        sl = slice(t * TILE, (t + 1) * TILE)
        some = high_e[:, sl] > low_e[:, sl]
        first = jnp.min(jnp.where(some, low_e[:, sl], FAR)).astype(i32)
        last = jnp.max(jnp.where(some, high_e[:, sl], -1.0)).astype(i32)
        at = first & ~15
        span = last - at
        kind = jnp.where(span <= WIDTHS[0], 1, jnp.where(span <= WIDTHS[1], 2, 3))
        wide = min(max(t * TILE - reach, 0), ext - WIDTHS[2])
        at = jnp.where(
            kind == 1,
            jnp.minimum(at, ext - WIDTHS[0]),
            jnp.where(kind == 2, jnp.minimum(at, ext - WIDTHS[1]), wide),
        )
        spans[8 + 2 * t] = jnp.where(last < 0, 0, kind)
        spans[9 + 2 * t] = at

    copies = []
    ready(0)
    for i, (b, out) in enumerate(((bq, q), (None, k), (bv, v))):
        ready(i + 1)
        for r in row_blocks(tokens):
            y = mm(xb[r, :], wb[i])
            if b is not None:
                y = y + b[...]
            y = y.astype(bf16)
            ob[i, r, :] = y * bf16(SCALE) if i == 0 else y
        copies.append(out_copy(ob.at[i], out, osems.at[i]))
    for c in copies:
        c.wait()


def front(place, lengths, x, wq, wk, wv, bq, bv, reach):
    tokens, width = x.shape
    ext = tokens + 2 * reach
    out = jax.ShapeDtypeStruct((tokens, width), bf16)
    return call(
        front_kernel,
        out_shape=(
            jax.ShapeDtypeStruct((8, ext), f32),
            jax.ShapeDtypeStruct((8 + 2 * (ext // TILE),), i32),
            out,
            out,
            out,
        ),
        in_specs=[SMEM, VMEM, VMEM, VMEM] + [HBM] * 4,
        out_specs=(VMEM, SMEM, HBM, HBM, HBM),
        scratch_shapes=[
            pltpu.VMEM((tokens, width), bf16),
            pltpu.VMEM((3, width, width), bf16),
            pltpu.VMEM((3, tokens, width), bf16),
            pltpu.SemaphoreType.DMA((4,)),
            pltpu.SemaphoreType.DMA((3,)),
        ],
        compiler_params=params(20),
        cost_estimate=cost(6 * tokens * width * width, 8 * tokens * width),
        name="front",
    )(place, lengths, bq, bv, x, wq, wk, wv)


def tile_bias(se, t, at, width):
    base = pl.multiple_of(t * TILE, TILE)
    low = se[0:1, pl.ds(base, TILE)]
    high = se[1:2, pl.ds(base, TILE)]
    key = (lax.broadcasted_iota(i32, (width, TILE), 0) + at).astype(f32)
    one = jnp.where((key >= low) & (key < high), 0.0, MASKED)
    some = jnp.where(high > low, 1.0, 0.0)
    return jnp.concatenate([one, one], axis=1), jnp.concatenate([some, some], axis=1)


def stacked(pair):
    lane = lax.broadcasted_iota(i32, pair.shape, 1)
    zero = jnp.zeros_like(pair)
    return jnp.concatenate(
        [jnp.where(lane < HEAD_DIM, pair, zero), jnp.where(lane < HEAD_DIM, zero, pair)], axis=0
    )


def unstacked(both):
    own = jnp.concatenate([both[:HEAD_DIM, :TILE], both[HEAD_DIM:, TILE:]], axis=0)
    return own.T


def each_tile(spans, first, last, tile):
    def each(t, _):
        kind, at = spans[8 + 2 * t], spans[9 + 2 * t]
        for i, span in enumerate(WIDTHS):
            pl.when(kind == i + 1)(functools.partial(tile, t, at, span))
        return 0

    lax.fori_loop(first, last, each, 0)


def attend_tile(se, q, kx, vx, attn, reach, t, at, span):
    width = q.shape[1]
    bias, _ = tile_bias(se, t, at, span)
    rows = pl.ds(pl.multiple_of(t * TILE - reach, TILE), TILE)
    window = pl.ds(pl.multiple_of(at, 16), span)
    pairs = [slice(p, p + PAIR) for p in range(0, width, PAIR)]
    scores = [mm_nt(kx[window, c], stacked(q[rows, c])) for c in pairs]
    soft = []
    for s in scores:
        s = s + bias
        weights = jnp.exp(s - jnp.max(s, axis=0, keepdims=True))
        soft.append((weights.astype(bf16), jnp.sum(weights, axis=0, keepdims=True)))
    for c, (weights, total) in zip(pairs, soft):
        attn[rows, c] = unstacked(mm_tn(vx[window, c], weights) / total).astype(bf16)


def attend_back_tile(se, qx, kx, vx, dox, dkx, dvx, t, at, span):
    width = qx.shape[1]
    bias, some = tile_bias(se, t, at, span)
    rows = pl.ds(pl.multiple_of(t * TILE, TILE), TILE)
    window = pl.ds(pl.multiple_of(at, 16), span)
    pairs = [slice(p, p + PAIR) for p in range(0, width, PAIR)]
    first = []
    for c in pairs:
        query, dout = stacked(qx[rows, c]), stacked(dox[rows, c])
        first.append((query, dout, mm_nt(kx[window, c], query), mm_nt(vx[window, c], dout)))
    second = []
    for query, dout, scores, dprob in first:
        scores = scores + bias
        weights = jnp.exp(scores - jnp.max(scores, axis=0, keepdims=True))
        probs = weights * (some / jnp.sum(weights, axis=0, keepdims=True))
        delta = jnp.sum(probs * dprob, axis=0, keepdims=True)
        second.append((probs.astype(bf16), (probs * (dprob - delta)).astype(bf16)))
    for c, (query, dout, _, _), (probs, dscore) in zip(pairs, first, second):
        dvx[window, c] += mm(probs, dout)
        dkx[window, c] += mm(dscore, query)
        qx[rows, c] = (unstacked(mm_tn(kx[window, c], dscore)) * SCALE).astype(bf16)


def attend_back_kernel(
    half, spans, se, bq, q, k, v, do, kh, vh, xl, xr, dl, dr, wq,
    dq, dk, dv, qx, kx, vx, dox, dkx, dvx, dkb, dvb, wb, xb, sems, osems,
):
    tokens = q.shape[0]
    reach = xl.shape[0]
    ext, some = kx.shape
    cols = pl.ds(half * some, some)
    own, low, high = pl.ds(reach, tokens), pl.ds(0, reach), pl.ds(reach + tokens, reach)
    ready = loads(
        [
            (wq.at[:, cols], wb),
            (xl, xb.at[low]),
            (xr, xb.at[pl.ds(reach, reach)]),
            (q.at[:, cols], qx.at[own]),
            (k.at[:, cols], kx.at[own]),
            (v.at[:, cols], vx.at[own]),
            (do.at[:, cols], dox.at[own]),
            (kh.at[pl.ds(0, reach), cols], kx.at[low]),
            (kh.at[pl.ds(reach, reach), cols], kx.at[high]),
            (vh.at[pl.ds(0, reach), cols], vx.at[low]),
            (vh.at[pl.ds(reach, reach), cols], vx.at[high]),
            (dl.at[:, cols], dox.at[low]),
            (dr.at[:, cols], dox.at[high]),
        ],
        sems,
    )
    dkx[...] = jnp.zeros_like(dkx)
    dvx[...] = jnp.zeros_like(dvx)
    for i in range(3):
        ready(i)
    bias = bq[...][half * some : (half + 1) * some]
    for at, to in ((0, 0), (reach, reach + tokens)):
        y = (mm(xb[at : at + reach, :], wb[...]) + bias).astype(bf16)
        qx[to : to + reach, :] = y * bf16(SCALE)
    for i in range(3, 13):
        ready(i)
    tile = functools.partial(attend_back_tile, se, qx, kx, vx, dox, dkx, dvx)
    each_tile(spans, 0, ext // TILE, tile)
    copies = [out_copy(qx.at[own], dq, osems.at[0])]
    dkb[...] = dkx[reach : reach + tokens, :].astype(bf16)
    copies.append(out_copy(dkb, dk, osems.at[1]))
    dvb[...] = dvx[reach : reach + tokens, :].astype(bf16)
    copies.append(out_copy(dvb, dv, osems.at[2]))
    for c in copies:
        c.wait()


def attend_back(half, halves, spans, se, q, k, v, do, kh, vh, xl, xr, dl, dr, wq, bq, after=()):
    tokens, width = q.shape
    reach = xl.shape[0]
    ext = tokens + 2 * reach
    some = width // halves
    out = jax.ShapeDtypeStruct((tokens, some), bf16)
    return call(
        functools.partial(attend_back_kernel, half),
        out_shape=(out, out, out),
        in_specs=[SMEM, VMEM, VMEM] + [HBM] * 11,
        out_specs=(HBM, HBM, HBM),
        scratch_shapes=[pltpu.VMEM((ext, some), bf16)] * 4
        + [pltpu.VMEM((ext, some), f32)] * 2
        + [pltpu.VMEM((tokens, some), bf16)] * 2
        + [pltpu.VMEM((width, some), bf16), pltpu.VMEM((2 * reach, width), bf16)]
        + [pltpu.SemaphoreType.DMA((13,)), pltpu.SemaphoreType.DMA((3,))],
        after=after,
        compiler_params=params(40),
        cost_estimate=cost(16e9 / halves, 20 * tokens * some),
        name="attend_back_%d" % half,
    )(spans, se, bq, q, k, v, do, kh, vh, xl, xr, dl, dr, wq)


LAYERS = [4]


def write_group(block, send, keep, buf, sems, place):
    here, layer = place[1], place[2]
    slots, rows = buf.shape[:2]
    half = rows // 2
    layers = LAYERS[0]
    chunk = half // layers

    def copies(slot, x, y, out):
        return (
            pltpu.make_async_copy(
                buf.at[slot, pl.ds(0, half)],
                out.at[pl.ds(pl.multiple_of((2 * x + y) * half, half), half)],
                sems.at[slot, 0],
            ),
            pltpu.make_async_copy(
                buf.at[slot, pl.ds(half, half)],
                out.at[pl.ds(pl.multiple_of((4 + 2 * y + x) * half, half), half)],
                sems.at[slot, 1],
            ),
        )

    def free(slot):
        for c in copies(slot, 0, 0, keep):
            c.wait()

    for part in range(PARTS):
        to = part ^ here
        core, x, y = to & 1, (to >> 1) & 1, (to >> 2) & 1
        slot = part % slots
        value = block(part).astype(bf16)
        if part >= slots:
            free(slot)
        for z in range(layers):
            at = (z ^ layer) * chunk
            for h in (0, half):
                buf[slot, pl.ds(pl.multiple_of(h + at, chunk), chunk), :] = value[h + z * chunk : h + (z + 1) * chunk]

        def start(out, slot=slot, x=x, y=y):
            for c in copies(slot, x, y, out):
                c.start()

        pl.when(core == 1)(functools.partial(start, send))
        pl.when(core == 0)(functools.partial(start, keep))
    for slot in range(slots):
        free(slot)


def group_shapes(rows, width):
    return (jax.ShapeDtypeStruct((rows // 2, width), bf16),) * 2


def group_scratch(rows, width):
    return [pltpu.VMEM((2, rows // PARTS, width), bf16), pltpu.SemaphoreType.DMA((2, 2))]


def gelu_both(z):
    u = jnp.abs(z) * 0.7071067811865476
    t = 1.0 / (1.0 + 0.3275911 * u)
    bell = jnp.exp(-0.5 * z * z)
    poly = t * (
        0.5 * 0.254829592
        + t * (0.5 * -0.284496736 + t * (0.5 * 1.421413741 + t * (0.5 * -1.453152027 + t * (0.5 * 1.061405429))))
    )
    tail = poly * bell
    cdf = jnp.where(z >= 0.0, 1.0 - tail, tail)
    return z * cdf, cdf + z * bell * 0.3989422804014327


def center(v):
    mean = jnp.mean(v, axis=1, keepdims=True)
    c = v - mean
    rstd = lax.rsqrt(jnp.mean(c * c, axis=1, keepdims=True) + EPS)
    return c * rstd, rstd


def center_back(e, xhat, rstd):
    return rstd * (
        e - jnp.mean(e, axis=1, keepdims=True) - xhat * jnp.mean(e * xhat, axis=1, keepdims=True)
    )


def colsum(v):
    return jnp.sum(v, axis=0, keepdims=True)


def layer_kernel(
    place, spans, se, bv, bo, g1, s1, bu, bd, g2, s2, q, k, v, xl, xr, x, dy, wk, wv, wo, wu, wd,
    rstd1, vec, attn, kh, vh, out, slope, mid_low, xhat1, d_two, d_down, send, keep,
    qb, kx, vx, xlb, xrb, wkb, wvb, khb, vhb, attb, xb, dyb, wob, wub, wdb, act, slb, xhb, lowb, two, ob, ddb, buf, sems, osems, gsems,
):
    tokens, width = x.shape
    ff = wu.shape[1]
    reach = xl.shape[0]
    ready = loads(
        [
            (wk, wkb), (xl, xlb), (xr, xrb), (wv, wvb),
            (k, kx.at[pl.ds(reach, tokens)]), (v, vx.at[pl.ds(reach, tokens)]), (q, qb),
            (wo, wob), (x, xb), (wu, wub), (wd, wdb), (dy, dyb),
        ],
        sems,
    )
    copies = []

    def put(source, target):
        copies.append(out_copy(source, target, osems.at[len(copies)]))

    for i in range(3):
        ready(i)
    for part, at, to in ((xlb, 0, 0), (xrb, reach, reach + tokens)):
        y = mm(part[...], wkb[...]).astype(bf16)
        kx[to : to + reach, :] = y
        khb[at : at + reach, :] = y
    ready(3)
    for part, at, to in ((xlb, 0, 0), (xrb, reach, reach + tokens)):
        y = (mm(part[...], wvb[...]) + bv[...]).astype(bf16)
        vx[to : to + reach, :] = y
        vhb[at : at + reach, :] = y
    put(khb, kh)
    put(vhb, vh)
    for i in (4, 5, 6):
        ready(i)
    tile = functools.partial(attend_tile, se, qb, kx, vx, attb, reach)
    each_tile(spans, reach // TILE, (reach + tokens) // TILE, tile)
    put(attb, attn)

    ready(7)
    ready(8)
    blocks = row_blocks(tokens)
    branch = [mm(attb[r, :], wob[...]) for r in blocks]
    for r, b in zip(blocks, branch):
        xh1, r1 = center(xb[r, :].astype(f32) + b + bo[...])
        mid = xh1 * g1[...] + s1[...]
        xhb[r, :] = xh1
        rstd1[r, :] = jnp.broadcast_to(r1, (ROWS, rstd1.shape[1]))
        lowb[r, :] = mid.astype(bf16)
        two[r, :] = mid + bd[...]
    put(xhb, xhat1)
    put(lowb, mid_low)

    ready(9)
    ready(10)

    def ups(c):
        return [mm(lowb[r, :], wub[:, c : c + CHUNK]) for r in blocks]

    up = ups(0)
    for c in range(0, ff, CHUNK):
        cols = slice(c, c + CHUNK)
        now = up
        if c + CHUNK < ff:
            up = ups(c + CHUNK)
        for r, z in zip(blocks, now):
            a, s = gelu_both(z + bu[...][cols])
            act[r, cols] = a.astype(bf16)
            slb[r, cols] = s.astype(bf16)
        for r in blocks:
            two[r, :] += mm(act[r, cols], wdb[cols, :])
        put(slb.at[:, pl.ds(c, CHUNK)], slope.at[:, pl.ds(c, CHUNK)])

    ready(11)
    sums = [0.0, 0.0, 0.0]
    for r in blocks:
        xh2, r2 = center(two[r, :])
        token = place[0] + r.start + lax.broadcasted_iota(i32, (ROWS, 1), 0)
        valid = jnp.where(token < spans[0], 1.0, 0.0)
        ob[r, :] = ((xh2 * g2[...] + s2[...]) * valid).astype(bf16)
        d = dyb[r, :].astype(f32) * valid
        d2 = center_back(d * g2[...], xh2, r2)
        two[r, :] = d2
        d2 = d2.astype(bf16)
        ddb[r, :] = d2
        for i, term in enumerate((d2.astype(f32), d * xh2, d)):
            sums[i] = sums[i] + colsum(term)
    put(ddb, d_down)
    put(two, d_two)
    put(ob, out)
    vec[3:8, :] = jnp.zeros((5, width), f32)
    for i in range(3):
        vec[i : i + 1, :] = sums[i]

    size = ff // PARTS
    write_group(lambda p: mm_tn(act[:, p * size : (p + 1) * size], ddb[...]), send, keep, buf, gsems, place)
    for c in copies:
        c.wait()


def layer(place, spans, se, q, k, v, xl, xr, x, dy, wk, wv, wo, wu, wd, bv, bo, g1, s1, bu, bd, g2, s2):
    tokens, width = x.shape
    ff = wu.shape[1]
    reach = xl.shape[0]
    ext = tokens + 2 * reach
    shape = lambda n, t, rows=tokens: jax.ShapeDtypeStruct((rows, n), t)
    vm = lambda rows, n, t: pltpu.VMEM((rows, n), t)
    return call(
        layer_kernel,
        out_shape=(
            shape(128, f32),
            shape(width, f32, 8),
            shape(width, bf16),
            shape(width, bf16, 2 * reach),
            shape(width, bf16, 2 * reach),
            shape(width, bf16),
            shape(ff, bf16),
            shape(width, bf16),
            shape(width, f32),
            shape(width, f32),
            shape(width, bf16),
        )
        + group_shapes(ff, width),
        in_specs=[SMEM, SMEM] + [VMEM] * 9 + [HBM] * 12,
        out_specs=(VMEM, VMEM) + (HBM,) * 11,
        scratch_shapes=[
            vm(tokens, width, bf16),
            vm(ext, width, bf16),
            vm(ext, width, bf16),
            vm(reach, width, bf16),
            vm(reach, width, bf16),
            vm(width, width, bf16),
            vm(width, width, bf16),
            vm(2 * reach, width, bf16),
            vm(2 * reach, width, bf16),
            vm(tokens, width, bf16),
            vm(tokens, width, bf16),
            vm(tokens, width, bf16),
            vm(width, width, bf16),
            vm(width, ff, bf16),
            vm(ff, width, bf16),
            vm(tokens, ff, bf16),
            vm(tokens, ff, bf16),
            vm(tokens, width, f32),
            vm(tokens, width, bf16),
            vm(tokens, width, f32),
            vm(tokens, width, bf16),
            vm(tokens, width, bf16),
        ]
        + group_scratch(ff, width)[:1]
        + [pltpu.SemaphoreType.DMA((12,)), pltpu.SemaphoreType.DMA((8 + ff // CHUNK,))]
        + group_scratch(ff, width)[1:],
        compiler_params=params(56),
        cost_estimate=cost(2 * tokens * width * (width + 3 * ff) + 8e9, 40 * tokens * width, 2 * tokens * ff),
        name="layer",
    )(place, spans, se, bv, bo, g1, s1, bu, bd, g2, s2, q, k, v, xl, xr, x, dy, wk, wv, wo, wu, wd)


def back_kernel(
    g1, rstd1, dd, slope, wd, wu, d_two, xhat1, wo,
    d_up, vec, bup, d_one, d_branch, d_attn, dmid, d2b, xhb, wob, oneb, brb, atb, sems, osems,
):
    c = pl.program_id(0)
    tokens, width = dd.shape
    pairs = [(d_two, d2b), (xhat1, xhb), (wo, wob)]
    arriving = [pltpu.make_async_copy(a, b, sems.at[i]) for i, (a, b) in enumerate(pairs)]

    @pl.when(c == 0)
    def _():
        for a in arriving:
            a.start()
        dmid[...] = jnp.zeros_like(dmid)
        vec[...] = jnp.zeros_like(vec)

    blocks = row_blocks(tokens)
    d_act = [mm_nt(dd[r, :], wd[...]) for r in blocks]
    total = 0.0
    for r, d in zip(blocks, d_act):
        du = (slope[r, :].astype(f32) * d).astype(bf16)
        d_up[r, :] = du
        total = total + colsum(du.astype(f32))
    bup[pl.ds(c, 1), :] = total

    for r in blocks:
        dmid[r, :] += mm_nt(d_up[r, :], wu[...])

    @pl.when(c == pl.num_programs(0) - 1)
    def _():
        for a in arriving:
            a.wait()
        sums = [0.0, 0.0, 0.0]
        copies = []
        for i, r in enumerate(blocks):
            d_mid = dmid[r, :] + d2b[r, :]
            xh = xhb[r, :]
            d1 = center_back(d_mid * g1[...], xh, rstd1[r, 0:1])
            oneb[r, :] = d1
            d1 = d1.astype(bf16)
            brb[r, :] = d1
            for n, term in enumerate((d_mid * xh, d_mid, d1.astype(f32))):
                sums[n] = sums[n] + colsum(term)
        for i, r in enumerate(blocks):
            atb[r, :] = mm_nt(brb[r, :], wob[...]).astype(bf16)
            at = pl.ds(r.start, ROWS)
            for n, (a, b) in enumerate(((oneb, d_one), (brb, d_branch), (atb, d_attn))):
                copies.append(out_copy(a.at[at], b.at[at], osems.at[3 * i + n]))
        for n in range(3):
            vec[n : n + 1, :] = sums[n]
        for a in copies:
            a.wait()


def back(d_two, d_down, slope, xhat1, rstd1, wd, wu, wo, g1, after=()):
    tokens, width = d_two.shape
    ff = wu.shape[1]
    full = lambda a: pl.BlockSpec(a.shape, lambda c: (0,) * a.ndim)
    col = lambda rows: pl.BlockSpec((rows, CHUNK), lambda c: (0, c))
    shape = lambda n, t: jax.ShapeDtypeStruct((tokens, n), t)
    vec = jax.ShapeDtypeStruct((8, width), f32)
    bup = jax.ShapeDtypeStruct((ff // CHUNK, CHUNK), f32)
    return call(
        back_kernel,
        grid=(ff // CHUNK,),
        out_shape=(shape(ff, bf16), vec, bup, shape(width, f32), shape(width, bf16), shape(width, bf16)),
        in_specs=[full(g1), full(rstd1), full(d_down), col(tokens), pl.BlockSpec((CHUNK, width), lambda c: (c, 0)), col(width)]
        + [HBM] * 3,
        out_specs=(col(tokens), full(vec), full(bup), HBM, HBM, HBM),
        scratch_shapes=[
            pltpu.VMEM((tokens, width), f32),
            pltpu.VMEM((tokens, width), f32),
            pltpu.VMEM((tokens, width), f32),
            pltpu.VMEM((width, width), bf16),
            pltpu.VMEM((tokens, width), f32),
            pltpu.VMEM((tokens, width), bf16),
            pltpu.VMEM((tokens, width), bf16),
            pltpu.SemaphoreType.DMA((3,)),
            pltpu.SemaphoreType.DMA((3 * (tokens // ROWS),)),
        ],
        after=after,
        compiler_params=params(34, dimension_semantics=("arbitrary",)),
        cost_estimate=cost(2 * tokens * width * (width + 2 * ff), 30 * tokens * width),
        name="back",
    )(g1, rstd1, d_down, slope, wd, wu, d_two, xhat1, wo)


def up_grad_kernel(place, mid_low, d_up, send, keep, lowb, upb, buf, gsems, sems):
    width = mid_low.shape[1]
    size = width // 2
    many = d_up.shape[1] // width
    ready = loads(
        [(mid_low, lowb)] + [(d_up.at[:, pl.ds(n * width, width)], upb.at[n]) for n in range(many)], sems
    )
    ready(0)

    def block(part):
        if part % 2 == 0:
            ready(1 + part // 2)
        rows = (part % 2) * size
        return mm_tn(lowb[:, rows : rows + size], upb[part // 2])

    write_group(block, send, keep, buf, gsems, place)


def up_grad(place, mid_low, d_up, after=()):
    tokens, width = mid_low.shape
    ff = d_up.shape[1]
    return call(
        up_grad_kernel,
        out_shape=group_shapes(ff, width),
        in_specs=[SMEM, HBM, HBM],
        out_specs=(HBM, HBM),
        scratch_shapes=[pltpu.VMEM((tokens, width), bf16), pltpu.VMEM((ff // width, tokens, width), bf16)]
        + group_scratch(ff, width)
        + [pltpu.SemaphoreType.DMA((1 + ff // width,))],
        after=after,
        compiler_params=params(20),
        cost_estimate=cost(2 * tokens * width * ff, 14 * tokens * width),
        name="up_grad",
    )(place, mid_low, d_up)


def rest_grad_kernel(halves, place, vec_a, vec_b, bup, attn, x, d_branch, *refs):
    parts, (send, keep, lhs, rhs, buf, small, gsems, sems, ssems) = refs[: 3 * halves], refs[3 * halves :]
    tokens, width = x.shape
    size = width // 2
    some = width // halves
    pairs = [(attn, lhs.at[0]), (d_branch, rhs.at[0]), (x, lhs.at[1])]
    for n in range(3):
        for h in range(halves):
            pairs.append((parts[3 * h + n], rhs.at[n + 1, :, pl.ds(h * some, some)]))
    ready = loads(pairs, sems)
    ready(0)
    ready(1)

    def block(part):
        which = part // 2
        if part == 2:
            ready(2)
        if which > 0 and part % 2 == 0:
            for h in range(halves):
                ready(3 + (which - 1) * halves + h)
        rows = (part % 2) * size
        return mm_tn(lhs[min(which, 1), :, rows : rows + size], rhs[which])

    write_group(block, send, keep, buf, gsems, place)
    ones = jnp.ones((8, tokens), bf16)
    row = lax.broadcasted_iota(i32, (8, width), 0)
    sums = jnp.where(row == 0, mm(ones, rhs[1]), jnp.where(row == 1, mm(ones, rhs[3]), 0.0))
    lines = [vec_a[...], sums, vec_b[...], bup[...]]
    have = sum(v.shape[0] for v in lines)
    lines.append(jnp.zeros((SMALL - have, width), f32))
    small[...] = jnp.concatenate(lines, axis=0).astype(bf16)
    end = pl.ds(2 * width, SMALL)
    copies = [out_copy(small, o.at[end], ssems.at[i]) for i, o in enumerate((send, keep))]
    for c in copies:
        c.wait()


def rest_grad(place, attn, x, d_branch, parts, vecs, after=()):
    tokens, width = x.shape
    rows = 4 * width
    halves = len(parts)
    out = jax.ShapeDtypeStruct((rows // 2 + SMALL, width), bf16)
    return call(
        functools.partial(rest_grad_kernel, halves),
        out_shape=(out, out),
        in_specs=[SMEM, VMEM, VMEM, VMEM] + [HBM] * (3 + 3 * halves),
        out_specs=(HBM, HBM),
        scratch_shapes=[pltpu.VMEM((2, tokens, width), bf16), pltpu.VMEM((4, tokens, width), bf16)]
        + group_scratch(rows, width)[:1]
        + [pltpu.VMEM((SMALL, width), bf16)]
        + group_scratch(rows, width)[1:]
        + [pltpu.SemaphoreType.DMA((3 + 3 * halves,)), pltpu.SemaphoreType.DMA((2,))],
        after=after,
        compiler_params=params(20),
        cost_estimate=cost(8 * tokens * width * width, 20 * tokens * width),
        name="rest_grad",
    )(place, *vecs, attn, x, d_branch, *sum(map(tuple, parts), ()))


def inputs_grad_kernel(halves, d_one, *refs):
    parts, (wq, wk, wv, out) = refs[: 3 * halves], refs[3 * halves :]
    total = d_one[...]
    some = wq.shape[1] // halves
    for h in range(halves):
        for g, w in zip(parts[3 * h : 3 * h + 3], (wq, wk, wv)):
            total = total + mm_nt(g[...], w[:, h * some : (h + 1) * some])
    out[...] = total


def inputs_grad(d_one, parts, wq, wk, wv, after=()):
    tokens, width = d_one.shape
    halves = len(parts)
    tok = lambda n: pl.BlockSpec((ROWS, n), lambda i: (i, 0))
    full = pl.BlockSpec((width, width), lambda i: (0, 0))
    return call(
        functools.partial(inputs_grad_kernel, halves),
        grid=(tokens // ROWS,),
        out_shape=(jax.ShapeDtypeStruct((tokens, width), f32),),
        in_specs=[tok(width)] + [tok(width // halves)] * (3 * halves) + [full] * 3,
        out_specs=(tok(width),),
        after=after,
        compiler_params=params(16, dimension_semantics=("arbitrary",)),
        cost_estimate=cost(6 * tokens * width * width, 20 * tokens * width),
        name="inputs_grad",
    )(d_one, *sum(map(tuple, parts), ()), wq, wk, wv)


def swap(value, axis, bit):
    count = lax.axis_size(axis)
    return lax.ppermute(value, axis, [(i, i ^ bit) for i in range(count)])


def plus(a, b):
    return (a.astype(f32) + b.astype(f32)).astype(bf16)


def layer_bits():
    return list(range(1, lax.axis_size("dp")))


def far_bits():
    bit, bits = PARTS, []
    while bit < lax.axis_size("seq"):
        bits.append(bit)
        bit *= 2
    return bits


def axis_bits(axis):
    return [1 << n for n in range((lax.axis_size(axis) - 1).bit_length())]


class Sum:
    def __init__(self, send, keep, tail=0):
        self.mine, self.got, self.payload, self.tail = [keep], [], [send], tail
        self.swaps = [("seq", 1)]
        self.steps = self.run()

    def receive(self, token):
        if self.got:
            *self.got, _ = lax.optimization_barrier((*self.got, token))
            next(self.steps)

    def send(self):
        self.got = [swap(p, *s) for p, s in zip(self.payload, self.swaps)]

    def tailed(self, payloads):
        rows = [p.reshape(-1, p.shape[-1]) for p in payloads]
        if self.tail:
            rows[0] = jnp.concatenate([rows[0], self.small], axis=0)
        return rows

    def untailed(self, like):
        if self.tail:
            self.small = plus(self.small, self.got[0][-self.tail :])
            self.got[0] = self.got[0][: -self.tail]
        return [g.reshape(m.shape) for g, m in zip(self.got, like)]

    def run(self):
        keep, got = self.mine[0], self.got[0]
        width = keep.shape[-1]
        both = plus(keep, got)
        if self.tail:
            self.small, both = both[-self.tail :], both[: -self.tail]
        layers = axis_bits("dp")
        both = both.reshape((2, 2, 2) + (2,) * len(layers) + (-1, width))
        parts = [both[0], both[1]]
        for bits in ((2, 4), (4, 2)):
            keeps = [p[0] for p in parts]
            self.payload, self.swaps = self.tailed([p[1] for p in parts]), [("seq", b) for b in bits]
            yield
            parts = list(map(plus, keeps, self.untailed(keeps)))
        part = jnp.stack(parts, axis=-3)
        for bit in layers:
            axis = part.ndim - 4
            keep = lax.index_in_dim(part, 0, axis, keepdims=False)
            self.payload, self.swaps = self.tailed([lax.index_in_dim(part, 1, axis, keepdims=False)]), [("dp", bit)]
            yield
            part = plus(keep, self.untailed([keep])[0])
        for bit in far_bits():
            part = plus(part, swap(part, "seq", bit))
            if self.tail:
                self.small = plus(self.small, swap(self.small, "seq", bit))
        for bit in reversed(layers):
            self.payload, self.swaps = [part], [("dp", bit)]
            yield
            part = jnp.stack([part, self.got[0]], axis=part.ndim - 3)
        parts = [lax.index_in_dim(part, n, part.ndim - 3, keepdims=False) for n in range(2)]
        for bits in ((4, 2), (2, 4)):
            self.payload, self.swaps = parts, [("seq", b) for b in bits]
            yield
            parts = [jnp.stack(pair) for pair in zip(parts, self.got)]
        whole = jnp.stack(parts).reshape(8, -1, width)
        self.payload, self.swaps = [whole], [("seq", 1)]
        yield
        self.result = (whole, self.got[0])
        self.payload = []
        yield


def advance(token, *sums):
    for s in sums:
        s.receive(token)
    payloads = lax.optimization_barrier(tuple(p for s in sums for p in s.payload))
    at = 0
    for s in sums:
        s.payload = list(payloads[at : at + len(s.payload)])
        at += len(s.payload)
        s.send()
    return payloads[0] if payloads else token


def spread_kernel(kind, place, ma, mb, oa, ob, *refs):
    outs, (buf, sems) = refs[:-2], refs[-2:]
    j = pl.program_id(0)
    here, layer = place[1], place[2]
    half = ma.shape[1]
    size = 2 * half
    layers = LAYERS[0]
    chunk = half // layers
    width = ma.shape[2]

    def copies(step):
        part = step ^ here
        slot = step & 1
        src = buf.at[slot]
        if kind == "down":
            return [(None, pltpu.make_async_copy(src, outs[0].at[pl.ds(pl.multiple_of(part * size, size), size)], sems.at[slot]))]
        at = pl.ds(pl.multiple_of((part & 1) * size, size), size)
        which = part >> 1
        if kind == "up":
            cols = pl.ds(pl.multiple_of(which * width, width), width)
            return [(None, pltpu.make_async_copy(src, outs[0].at[at, cols], sems.at[slot]))]
        return [(which == n, pltpu.make_async_copy(src, o.at[at], sems.at[slot])) for n, o in enumerate(outs)]

    def start(step):
        for cond, c in copies(step):
            if cond is None:
                c.start()
            else:
                pl.when(cond)(c.start)

    def wait(step):
        copies(step)[0][1].wait()

    pl.when(j >= 2)(lambda: wait(j - 2))
    slot = j & 1

    def fill(a, b):
        for z in range(layers):
            to = (z ^ layer) * chunk
            rows = slice(z * chunk, (z + 1) * chunk)
            buf[slot, pl.ds(pl.multiple_of(to, chunk), chunk), :] = a[0, rows, :].astype(f32)
            buf[slot, pl.ds(pl.multiple_of(half + to, chunk), chunk), :] = b[0, rows, :].astype(f32)

    pl.when((j & 1) == 0)(lambda: fill(ma, mb))
    pl.when((j & 1) == 1)(lambda: fill(oa, ob))
    start(j)

    @pl.when(j == PARTS - 1)
    def _():
        wait(j - 1)
        wait(j)


def spread(kind, place, mine, other, after=()):
    half, width = mine.shape[1:]
    rows = 2 * half * PARTS
    a = pl.BlockSpec((1, half, width), lambda j: (2 * ((j >> 1) & 1) + (j >> 2), 0, 0))
    b = pl.BlockSpec((1, half, width), lambda j: (4 + 2 * (j >> 2) + ((j >> 1) & 1), 0, 0))
    if kind == "down":
        shapes = [(rows, width)]
    elif kind == "up":
        shapes = [(width, rows)]
    else:
        shapes = [(width, width)] * 4
    return call(
        functools.partial(spread_kernel, kind),
        grid=(PARTS,),
        out_shape=[jax.ShapeDtypeStruct(s, f32) for s in shapes],
        in_specs=[SMEM, a, b, a, b],
        out_specs=[HBM] * len(shapes),
        after=after,
        scratch_shapes=[pltpu.VMEM((2, 2 * half, width), f32), pltpu.SemaphoreType.DMA((2,))],
        compiler_params=params(12, dimension_semantics=("arbitrary",)),
        cost_estimate=cost(rows * width, 6 * rows * width),
        name="spread_" + kind,
    )(place, mine, mine, other, other)


def sum_small(vec):
    for axis in ("seq", "dp"):
        bit = 1
        while bit < lax.axis_size(axis):
            vec = vec + swap(vec, axis, bit)
            bit *= 2
    return vec


def neighbours(value, reach):
    count = lax.axis_size("seq")
    up = [(i, i + 1) for i in range(count - 1)]
    low = lax.ppermute(value[-reach:], "seq", up)
    high = lax.ppermute(value[:reach], "seq", [(b, a) for a, b in up])
    return low, high


def body(
    inputs, lengths, w_query, b_query, w_key, w_value, b_value, w_out, b_out, gain_one, shift_one,
    w_up, b_up, w_down, b_down, gain_two, shift_two, d_output,
):
    rows, tokens, width = inputs.shape
    reach = ITEM_MOST
    LAYERS[0] = lax.axis_size("dp")
    here = lax.axis_index("seq")
    place = jnp.stack([here * tokens, here & (PARTS - 1), lax.axis_index("dp")]).astype(i32)
    x = inputs.reshape(tokens, width)
    dy = d_output.reshape(tokens, width)

    xl, xr = neighbours(x, reach)
    se, spans, q, k, v = front(place, lengths, x, w_query, w_key, w_value, b_query, b_value, reach)
    rstd1, vec_a, attn, kh, vh, output, slope, mid_low, xhat1, d_two, d_down, send1, keep1 = layer(
        place, spans, se, q, k, v, xl, xr, x, dy, w_key, w_value, w_out, w_up, w_down,
        b_value, b_out, gain_one, shift_one, b_up, b_down, gain_two, shift_two,
    )
    one = Sum(send1, keep1)
    token = advance(d_two, one)
    d_up, vec_b, bup, d_one, d_branch, d_attn = back(
        d_two, d_down, slope, xhat1, rstd1, w_down, w_up, w_out, gain_one, after=[token]
    )
    token = advance(d_attn, one)
    dl, dr = neighbours(d_attn, reach)
    send2, keep2 = up_grad(place, mid_low, d_up, after=[token])
    two = Sum(send2, keep2)
    token = advance(send2, two)
    args = (HALVES, spans, se, q, k, v, d_attn, kh, vh, xl, xr, dl, dr, w_query, b_query)
    parts = [attend_back(0, *args, after=[token])]
    token = advance(parts[0][0], one, two)
    parts.append(attend_back(1, *args, after=[token]))
    token = advance(parts[1][0], one)
    send3, keep3 = rest_grad(place, attn, x, d_branch, parts, [vec_a, vec_b, bup.reshape(-1, width)], after=[token])
    three = Sum(send3, keep3, SMALL)
    token = advance(send3, one, two, three)
    (d_inputs,) = inputs_grad(d_one, parts, w_query, w_key, w_value, after=[token])
    token = d_inputs
    sums = {1: one, 2: two, 3: three}
    for event in ORDER:
        if event < 0:
            kind = ("down", "up", "rest")[-event - 1]
            grads = spread(kind, place, *sums[-event].result, after=[token])
            token = grads[0]
            if kind == "down":
                (g_w_down,) = grads
            elif kind == "up":
                (g_w_up,) = grads
            else:
                g_w_out, g_w_query, g_w_key, g_w_value = grads
        else:
            token = advance(token, *[sums[int(g)] for g in str(event)])
    small = three.small.astype(f32)
    ff = w_up.shape[1]
    many = ff // width
    return (
        output.reshape(rows, tokens, width),
        d_inputs.reshape(rows, tokens, width),
        g_w_query,
        small[8],
        g_w_key,
        g_w_value,
        small[9],
        g_w_out,
        small[18],
        small[16],
        small[17],
        g_w_up,
        small[24 : 24 + many].reshape(ff),
        g_w_down,
        small[0],
        small[1],
        small[2],
    )


def solution(mesh):
    split, whole = P("dp", "seq", None), P()
    return jax.shard_map(
        body,
        mesh=mesh,
        in_specs=(split, P("dp", None)) + (whole,) * 15 + (split,),
        out_specs=(split, split) + (whole,) * 15,
        check_vma=False,
    )
```

```python
import functools

import jax
import jax.numpy as jnp
from jax import lax
from jax.experimental import pallas as pl
from jax.experimental.pallas import tpu as pltpu
from jax.sharding import PartitionSpec as P

HEADS = 12
HEAD_DIM = 64
ITEM_MOST = 256
EPS = 1e-12
SCALE = 0.125
MASKED = -1e30
FAR = 1e9
TILE = 128
PAIR = 2 * HEAD_DIM
WIDTHS = (256, 384, 640)
ROWS = 256
SMALL = 16
ORDER = (3, 2, 1, 3, 2, 1, 3, 2, 1, 3, 2, 1, 3, 3, 2, 1, 3, 2, 1, -1, 3, 0, 2, 2, -2, 3, 3, -3)
HALVES = 2
PARTS = 8
CHUNK = 512

bf16 = jnp.bfloat16
f32 = jnp.float32
i32 = jnp.int32
ANY = pl.BlockSpec(memory_space=pl.ANY)
HBM = pl.BlockSpec(memory_space=pltpu.HBM)
KEPT = pl.BlockSpec(memory_space=pltpu.VMEM)
FREE = pl.BlockSpec(memory_space=pltpu.VMEM)
NEAR = pl.BlockSpec(memory_space=pltpu.VMEM)
SMEM = pl.BlockSpec(memory_space=pltpu.SMEM)
VMEM = pl.BlockSpec(memory_space=pltpu.VMEM)


def params(mib, **kw):
    return pltpu.CompilerParams(vmem_limit_bytes=mib * 1024 * 1024, **kw)


def cost(flops, nbytes, trans=0):
    return pl.CostEstimate(flops=int(flops), bytes_accessed=int(nbytes), transcendentals=int(trans))


def mm(a, b):
    return lax.dot_general(a, b, (((1,), (0,)), ((), ())), preferred_element_type=f32)


def mm_nt(a, b):
    return lax.dot_general(a, b, (((1,), (1,)), ((), ())), preferred_element_type=f32)


def mm_tn(a, b):
    return lax.dot_general(a, b, (((0,), (0,)), ((), ())), preferred_element_type=f32)


def large(a):
    return a.size * a.dtype.itemsize > 512 * 1024


def call(kernel, out_shape, in_specs, out_specs, after=(), **kw):
    kept = lambda a, spec: pltpu.VMEM if spec is KEPT else pltpu.HBM if spec is HBM or spec is NEAR or (large(a) and spec is not FREE and spec is not ANY) else None
    shapes = [k(o.shape, o.dtype) if (k := kept(o, spec)) else o for o, spec in zip(out_shape, out_specs)]
    count = len(in_specs)

    def plain(*refs):
        return kernel(*refs[:count], *refs[count + len(after) :])

    specs = list(in_specs) + [ANY] * len(after)
    run = pl.pallas_call(plain, out_shape=shapes, in_specs=specs, out_specs=list(out_specs), **kw)

    def apply(*args):
        args = [
            pltpu.with_memory_space_constraint(a, k) if (k := kept(a, spec)) else a
            for a, spec in zip(args, in_specs)
        ]
        return run(*args, *[pltpu.with_memory_space_constraint(a, pltpu.HBM) if a.dtype == f32 else a for a in after])

    return apply


def loads(pairs, sems):
    copies = [pltpu.make_async_copy(a, b, sems.at[i]) for i, (a, b) in enumerate(pairs)]
    for c in copies:
        c.start()
    return lambda i: copies[i].wait()


def out_copy(source, target, sem):
    c = pltpu.make_async_copy(source, target, sem)
    c.start()
    return c


def row_blocks(tokens):
    return [slice(r, r + ROWS) for r in range(0, tokens, ROWS)]


def front_kernel(
    place, lengths, bq, bv, x, wq, wk, wv,
    se, spans, se_low, spans_low, q, k, v, qv, kv, vv, xv, wkv, wvv, wqb, sems, osems,
):
    ready = loads([(x, xv), (wq, wqb), (wk, wkv), (wv, wvv)], sems)
    slots = lengths.shape[1]
    tokens = x.shape[0]
    ext = se.shape[1]
    reach = (ext - tokens) // 2
    step = max(d for d in range(8, 129, 8) if slots % d == 0)
    start = place[0] - reach
    pos = (lax.broadcasted_iota(i32, (1, ext), 1) + start).astype(f32)
    sizes = lengths[...].astype(f32)

    def scan(c, state):
        low, high = state
        index = lax.broadcasted_iota(i32, (step, slots), 0) + c * step
        upto = lax.broadcasted_iota(i32, (step, slots), 1) <= index
        ends = jnp.sum(jnp.where(upto, sizes, 0.0), axis=1, keepdims=True)
        before = ends <= pos
        low = jnp.maximum(low, jnp.max(jnp.where(before, ends, 0.0), axis=0, keepdims=True))
        high = jnp.minimum(high, jnp.min(jnp.where(before, FAR, ends), axis=0, keepdims=True))
        return low, high

    low, high = lax.fori_loop(
        0, slots // step, scan, (jnp.zeros((1, ext), f32), jnp.full((1, ext), FAR, f32))
    )
    real = (pos >= 0.0) & (high < FAR)
    local = lax.broadcasted_iota(i32, (1, ext), 1).astype(f32)
    offset = start.astype(f32)
    own = (local >= reach) & (local < reach + tokens)
    low_e = jnp.where(real, low - offset, local)
    high_e = jnp.where(real, high - offset, local + 1.0)
    shared = real & (
        ((local < reach) & (high_e > reach)) | ((local >= reach + tokens) & (low_e < reach + tokens))
    )
    used = own | shared
    low_e = jnp.where(used, low_e, 0.0)
    high_e = jnp.where(used, high_e, 0.0)
    se[0:1, :] = low_e
    se[1:2, :] = high_e
    se[2:8, :] = jnp.zeros((6, ext), f32)
    se_copy = out_copy(se, se_low, osems.at[3])

    def note(i, value):
        spans[i] = value
        spans_low[i] = value

    note(0, jnp.sum(sizes).astype(i32))
    for t in range(ext // TILE):
        sl = slice(t * TILE, (t + 1) * TILE)
        some = high_e[:, sl] > low_e[:, sl]
        first = jnp.min(jnp.where(some, low_e[:, sl], FAR)).astype(i32)
        last = jnp.max(jnp.where(some, high_e[:, sl], -1.0)).astype(i32)
        at = first & ~15
        span = last - at
        kind = jnp.where(span <= WIDTHS[0], 1, jnp.where(span <= WIDTHS[1], 2, 3))
        wide = min(max(t * TILE - reach, 0), ext - WIDTHS[2])
        at = jnp.where(
            kind == 1,
            jnp.minimum(at, ext - WIDTHS[0]),
            jnp.where(kind == 2, jnp.minimum(at, ext - WIDTHS[1]), wide),
        )
        note(8 + 2 * t, jnp.where(last < 0, 0, kind))
        note(9 + 2 * t, at)

    copies = [se_copy]
    ready(0)
    for i, (w, b, out, to) in enumerate(((wqb, bq, qv, q), (wkv, None, kv, k), (wvv, bv, vv, v))):
        ready(i + 1)
        for r in row_blocks(tokens):
            y = mm(xv[r, :], w[...])
            if b is not None:
                y = y + b[...]
            y = y.astype(bf16)
            out[r, :] = y * bf16(SCALE) if i == 0 else y
        copies.append(out_copy(out, to, osems.at[i]))
    for c in copies:
        c.wait()


def front(place, lengths, x, wq, wk, wv, bq, bv, reach):
    tokens, width = x.shape
    ext = tokens + 2 * reach
    like = lambda a: jax.ShapeDtypeStruct(a.shape, a.dtype)
    kept = [like(a) for a in (x, x, x, x, wk, wv)]
    return call(
        front_kernel,
        out_shape=(
            *[
                jax.ShapeDtypeStruct((8, ext), f32),
                jax.ShapeDtypeStruct((8 + 2 * (ext // TILE),), i32),
            ]
            * 2,
            like(x),
            like(x),
            like(x),
            *kept,
        ),
        in_specs=[SMEM, NEAR, NEAR, NEAR] + [HBM] * 4,
        out_specs=(KEPT, SMEM, HBM, SMEM, HBM, HBM, HBM) + (KEPT,) * len(kept),
        scratch_shapes=[
            pltpu.VMEM((width, width), bf16),
            pltpu.SemaphoreType.DMA((4,)),
            pltpu.SemaphoreType.DMA((4,)),
        ],
        compiler_params=params(8),
        cost_estimate=cost(6 * tokens * width * width, 8 * tokens * width),
        name="front",
    )(place, lengths, bq, bv, x, wq, wk, wv)


def tile_bias(se, t, at, width):
    base = pl.multiple_of(t * TILE, TILE)
    low = se[0:1, pl.ds(base, TILE)]
    high = se[1:2, pl.ds(base, TILE)]
    key = (lax.broadcasted_iota(i32, (width, TILE), 0) + at).astype(f32)
    one = jnp.where((key >= low) & (key < high), 0.0, MASKED)
    some = jnp.where(high > low, 1.0, 0.0)
    return jnp.concatenate([one, one], axis=1), jnp.concatenate([some, some], axis=1)


def stacked(pair):
    lane = lax.broadcasted_iota(i32, pair.shape, 1)
    zero = jnp.zeros_like(pair)
    return jnp.concatenate(
        [jnp.where(lane < HEAD_DIM, pair, zero), jnp.where(lane < HEAD_DIM, zero, pair)], axis=0
    )


def unstacked(both):
    own = jnp.concatenate([both[:HEAD_DIM, :TILE], both[HEAD_DIM:, TILE:]], axis=0)
    return own.T


def each_tile(spans, first, last, tile):
    def each(t, _):
        kind, at = spans[8 + 2 * t], spans[9 + 2 * t]
        for i, span in enumerate(WIDTHS):
            pl.when(kind == i + 1)(functools.partial(tile, t, at, span))
        return 0

    lax.fori_loop(first, last, each, 0)


def attend_tile(se, q, kx, vx, attn, reach, t, at, span):
    width = q.shape[1]
    bias, _ = tile_bias(se, t, at, span)
    rows = pl.ds(pl.multiple_of(t * TILE - reach, TILE), TILE)
    window = pl.ds(pl.multiple_of(at, 16), span)
    pairs = [slice(p, p + PAIR) for p in range(0, width, PAIR)]
    scores = [mm_nt(kx[window, c], stacked(q[rows, c])) for c in pairs]
    soft = []
    for s in scores:
        s = s + bias
        weights = jnp.exp(s - jnp.max(s, axis=0, keepdims=True))
        soft.append((weights.astype(bf16), jnp.sum(weights, axis=0, keepdims=True)))
    for c, (weights, total) in zip(pairs, soft):
        attn[rows, c] = unstacked(mm_tn(vx[window, c], weights) / total).astype(bf16)


def attend_back_tile(se, qx, kx, vx, dox, dkx, dvx, t, at, span):
    width = qx.shape[1]
    bias, some = tile_bias(se, t, at, span)
    rows = pl.ds(pl.multiple_of(t * TILE, TILE), TILE)
    window = pl.ds(pl.multiple_of(at, 16), span)
    pairs = [slice(p, p + PAIR) for p in range(0, width, PAIR)]
    first = []
    for c in pairs:
        query, dout = stacked(qx[rows, c]), stacked(dox[rows, c])
        first.append((query, dout, mm_nt(kx[window, c], query), mm_nt(vx[window, c], dout)))
    second = []
    for query, dout, scores, dprob in first:
        scores = scores + bias
        weights = jnp.exp(scores - jnp.max(scores, axis=0, keepdims=True))
        probs = weights * (some / jnp.sum(weights, axis=0, keepdims=True))
        delta = jnp.sum(probs * dprob, axis=0, keepdims=True)
        second.append((probs.astype(bf16), (probs * (dprob - delta)).astype(bf16)))
    for c, (query, dout, _, _), (probs, dscore) in zip(pairs, first, second):
        dvx[window, c] += mm(probs, dout)
        dkx[window, c] += mm(dscore, query)
        qx[rows, c] = (unstacked(mm_tn(kx[window, c], dscore)) * SCALE).astype(bf16)


def attend_back_kernel(
    half, spans, se, bq, q, k, v, do, kh, vh, xl, xr, dl, dr, wq,
    dq, dk, dv, qx, kx, vx, dox, dkx, dvx, dkb, dvb, wb, xb, sems, osems,
):
    tokens = q.shape[0]
    reach = xl.shape[0]
    ext, some = kx.shape
    cols = pl.ds(half * some, some)
    own, low, high = pl.ds(reach, tokens), pl.ds(0, reach), pl.ds(reach + tokens, reach)
    ready = loads(
        [
            (wq.at[:, cols], wb),
            (xl, xb.at[low]),
            (xr, xb.at[pl.ds(reach, reach)]),
            (q.at[:, cols], qx.at[own]),
            (k.at[:, cols], kx.at[own]),
            (v.at[:, cols], vx.at[own]),
            (do.at[:, cols], dox.at[own]),
            (kh.at[pl.ds(0, reach), cols], kx.at[low]),
            (kh.at[pl.ds(reach, reach), cols], kx.at[high]),
            (vh.at[pl.ds(0, reach), cols], vx.at[low]),
            (vh.at[pl.ds(reach, reach), cols], vx.at[high]),
            (dl.at[:, cols], dox.at[low]),
            (dr.at[:, cols], dox.at[high]),
        ],
        sems,
    )
    dkx[...] = jnp.zeros_like(dkx)
    dvx[...] = jnp.zeros_like(dvx)
    for i in range(3):
        ready(i)
    bias = bq[...][half * some : (half + 1) * some]
    for at, to in ((0, 0), (reach, reach + tokens)):
        y = (mm(xb[at : at + reach, :], wb[...]) + bias).astype(bf16)
        qx[to : to + reach, :] = y * bf16(SCALE)
    for i in range(3, 13):
        ready(i)
    tile = functools.partial(attend_back_tile, se, qx, kx, vx, dox, dkx, dvx)
    each_tile(spans, 0, ext // TILE, tile)
    copies = [out_copy(qx.at[own], dq, osems.at[0])]
    dkb[...] = dkx[reach : reach + tokens, :].astype(bf16)
    copies.append(out_copy(dkb, dk, osems.at[1]))
    dvb[...] = dvx[reach : reach + tokens, :].astype(bf16)
    copies.append(out_copy(dvb, dv, osems.at[2]))
    for c in copies:
        c.wait()


def attend_back(half, halves, spans, se, q, k, v, do, kh, vh, xl, xr, dl, dr, wq, bq, after=()):
    tokens, width = q.shape
    reach = xl.shape[0]
    ext = tokens + 2 * reach
    some = width // halves
    out = jax.ShapeDtypeStruct((tokens, some), bf16)
    return call(
        functools.partial(attend_back_kernel, half),
        out_shape=(out, out, out),
        in_specs=[SMEM, NEAR, VMEM] + [HBM] * 11,
        out_specs=(HBM, HBM, HBM),
        scratch_shapes=[pltpu.VMEM((ext, some), bf16)] * 4
        + [pltpu.VMEM((ext, some), f32)] * 2
        + [pltpu.VMEM((tokens, some), bf16)] * 2
        + [pltpu.VMEM((width, some), bf16), pltpu.VMEM((2 * reach, width), bf16)]
        + [pltpu.SemaphoreType.DMA((13,)), pltpu.SemaphoreType.DMA((3,))],
        after=after,
        compiler_params=params(20),
        cost_estimate=cost(16e9 / halves, 20 * tokens * some),
        name="attend_back_%d" % half,
    )(spans, se, bq, q, k, v, do, kh, vh, xl, xr, dl, dr, wq)


def piece_copies(part, place, source, sem, send, keep, stride, offset=0):
    to = part ^ place[1]
    core, x, y = to & 1, (to >> 1) & 1, (to >> 2) & 1
    rows = source(0).shape[0]

    def copies(out):
        return [
            pltpu.make_async_copy(
                source(n), out.at[pl.ds(pl.multiple_of(at * stride + offset, 16), rows)], sem.at[n]
            )
            for n, at in enumerate((2 * x + y, 4 + 2 * y + x))
        ]

    for here, out in ((1, send), (0, keep)):

        @pl.when(core == here)
        def _(out=out):
            for c in copies(out):
                c.start()

    def wait():
        for c in copies(keep):
            c.wait()

    return wait


def write_group(block, send, keep, buf, sems, place, stride):
    slots, rows = buf.shape[:2]
    half = rows // 2
    waits = []
    for part in range(PARTS):
        slot = part % slots
        value = block(part).astype(bf16)
        if part >= slots:
            waits[part - slots]()
        buf[slot] = value
        source = lambda n, slot=slot: buf.at[slot, pl.ds(n * half, half)]
        waits.append(piece_copies(part, place, source, sems.at[slot], send, keep, stride))
    for wait in waits[-slots:]:
        wait()


def group_shapes(stride, width, tail=0):
    return (jax.ShapeDtypeStruct((PARTS * stride + tail, width), bf16),) * 2


def group_scratch(rows, width, slots=PARTS):
    return [pltpu.VMEM((slots, rows // PARTS, width), bf16), pltpu.SemaphoreType.DMA((slots, 2))]


def gelu_both(z):
    u = jnp.abs(z) * 0.7071067811865476
    t = 1.0 / (1.0 + 0.3275911 * u)
    bell = jnp.exp2(z * (z * -0.7213475204444817))
    poly = t * (
        0.5 * 0.254829592
        + t * (0.5 * -0.284496736 + t * (0.5 * 1.421413741 + t * (0.5 * -1.453152027 + t * (0.5 * 1.061405429))))
    )
    tail = poly * bell
    cdf = jnp.where(z >= 0.0, 1.0 - tail, tail)
    return z * cdf, cdf + z * bell * 0.3989422804014327


def center(v):
    mean = jnp.mean(v, axis=1, keepdims=True)
    c = v - mean
    rstd = lax.rsqrt(jnp.mean(c * c, axis=1, keepdims=True) + EPS)
    return c * rstd, rstd


def center_back(e, xhat, rstd):
    return rstd * (
        e - jnp.mean(e, axis=1, keepdims=True) - xhat * jnp.mean(e * xhat, axis=1, keepdims=True)
    )


def colsum(v):
    return jnp.sum(v, axis=0, keepdims=True)


def layer_kernel(
    place, spans, se, bv, bo, g1, s1, bu, bd, g2, s2, xl, xr, q, k, v, x, wk, wv, wo_h, wu_h, wd_h, dy_h,
    d_up, mid_low, kh, vh, out, d_one, d_attn, d_low, d_high, send, keep,
    wo, wu, wd, dy, lsems, kx, vx, attb, act, xh, rstd, two, ob, dd, branch, datt, gout, line, small, buf, osems, gsems, hsems,
):
    tokens, width = x.shape
    ff = wu.shape[1]
    reach = xl.shape[0]
    own = slice(reach, reach + tokens)
    blocks = row_blocks(tokens)
    ready = loads([(wo_h, wo), (wu_h, wu), (wd_h, wd), (dy_h, dy)], lsems)
    copies = []

    def put(source, target):
        copies.append(out_copy(source, target, osems.at[len(copies)]))

    line[...] = jnp.zeros_like(line)
    kx[own, :] = k[...]
    vx[own, :] = v[...]
    for part, at in ((xl, 0), (xr, reach + tokens)):
        kx[at : at + reach, :] = mm(part[...], wk[...]).astype(bf16)
        vx[at : at + reach, :] = (mm(part[...], wv[...]) + bv[...]).astype(bf16)
    for n, at in enumerate((0, reach + tokens)):
        for ref, to in ((kx, kh), (vx, vh)):
            put(ref.at[pl.ds(at, reach)], to.at[pl.ds(n * reach, reach)])
    tile = functools.partial(attend_tile, se, q, kx, vx, attb, reach)
    each_tile(spans, reach // TILE, (reach + tokens) // TILE, tile)
    ready(0)
    for r, b in zip(blocks, [mm(attb[r, :], wo[...]) for r in blocks]):
        hat, rs = center(x[r, :].astype(f32) + b + bo[...])
        mid = hat * g1[...] + s1[...]
        xh[r, :] = hat
        rstd[r, :] = jnp.broadcast_to(rs, (ROWS, rstd.shape[1]))
        mid_low[r, :] = mid.astype(bf16)
        two[r, :] = mid + bd[...]

    ready(1)
    ready(2)

    def ups(c):
        return [mm(mid_low[r, :], wu[:, c : c + CHUNK]) for r in blocks]

    up = ups(0)
    for c in range(0, ff, CHUNK):
        cols = slice(c, c + CHUNK)
        now = up
        if c + CHUNK < ff:
            up = ups(c + CHUNK)
        for r, z in zip(blocks, now):
            a, s = gelu_both(z + bu[...][cols])
            act[r, cols] = a.astype(bf16)
            d_up[r, cols] = s.astype(bf16)
        for r in blocks:
            two[r, :] += mm(act[r, cols], wd[cols, :])

    ready(3)
    sums = [0.0] * 6
    for r in blocks:
        hat, rs = center(two[r, :])
        token = place[0] + r.start + lax.broadcasted_iota(i32, (ROWS, 1), 0)
        valid = jnp.where(token < spans[0], 1.0, 0.0)
        ob[r, :] = ((hat * g2[...] + s2[...]) * valid).astype(bf16)
        d = dy[r, :].astype(f32) * valid
        d2 = center_back(d * g2[...], hat, rs)
        two[r, :] = d2
        d2 = d2.astype(bf16)
        dd[r, :] = d2
        for i, term in enumerate((d2.astype(f32), d * hat, d)):
            sums[i] = sums[i] + colsum(term)
    put(ob, out)
    size = ff // PARTS
    stride = (send.shape[0] - SMALL) // PARTS
    write_group(lambda p: mm_tn(act[:, p * size : (p + 1) * size], dd[...]), send, keep, buf, gsems, place, stride)

    def downs(c):
        return [mm_nt(dd[r, :], wd[c : c + CHUNK, :]) for r in blocks]

    down = downs(0)
    for c in range(0, ff, CHUNK):
        cols = slice(c, c + CHUNK)
        now = down
        if c + CHUNK < ff:
            down = downs(c + CHUNK)
        total = 0.0
        for r, d in zip(blocks, now):
            du = (d_up[r, cols].astype(f32) * d).astype(bf16)
            d_up[r, cols] = du
            total = total + colsum(du.astype(f32))
        for half in range(0, CHUNK, CHUNK // 2):
            n, at = divmod(c + half, width)
            line[8 + n : 9 + n, at : at + CHUNK // 2] = total[:, half : half + CHUNK // 2]
        for r in blocks:
            two[r, :] += mm_nt(d_up[r, cols], wu[:, cols])
    for r in blocks:
        d_mid = two[r, :]
        hat = xh[r, :]
        d1 = center_back(d_mid * g1[...], hat, rstd[r, 0:1])
        two[r, :] = d1
        d1 = d1.astype(bf16)
        branch[r, :] = d1
        for i, term in enumerate((d_mid * hat, d_mid, d1.astype(f32))):
            sums[3 + i] = sums[3 + i] + colsum(term)
    put(two, d_one)
    for r in blocks:
        datt[r, :] = mm_nt(branch[r, :], wo[...]).astype(bf16)
        at = pl.ds(r.start, ROWS)
        put(datt.at[at], d_attn.at[at])
    put(datt.at[pl.ds(0, reach)], d_low)
    put(datt.at[pl.ds(tokens - reach, reach)], d_high)
    for r in range(0, width, width // 2):
        gout[r : r + width // 2, :] = mm_tn(attb[:, r : r + width // 2], branch[...]).astype(bf16)
    size = width // PARTS // 2
    waits = []
    for part in range(PARTS):
        source = lambda n, part=part: gout.at[pl.ds((2 * part + n) * size, size)]
        waits.append(piece_copies(part, place, source, hsems.at[part], send, keep, stride, stride - size))
    for i in range(6):
        line[i : i + 1, :] = sums[i]
    small[...] = line[...].astype(bf16)
    for to in (send, keep):
        put(small, to.at[pl.ds(PARTS * stride, SMALL)])
    for c in copies:
        c.wait()
    for wait in waits:
        wait()


def layer(place, spans, se, xl, xr, q, k, v, x, wk, wv, wo, wu, wd, dy, bv, bo, g1, s1, bu, bd, g2, s2):
    tokens, width = x.shape
    ff = wu.shape[1]
    reach = xl.shape[0]
    ext = tokens + 2 * reach
    shape = lambda n, t, rows=tokens: jax.ShapeDtypeStruct((rows, n), t)
    vm = lambda rows, n, t: pltpu.VMEM((rows, n), t)
    group = group_scratch(ff, width, 4)
    return call(
        layer_kernel,
        out_shape=(
            shape(ff, bf16),
            shape(width, bf16),
            shape(width, bf16, 2 * reach),
            shape(width, bf16, 2 * reach),
            shape(width, bf16),
            shape(width, f32),
            shape(width, bf16),
            shape(width, bf16, reach),
            shape(width, bf16, reach),
        )
        + group_shapes((ff + width) // PARTS // 2, width, SMALL),
        in_specs=[SMEM, SMEM, KEPT] + [VMEM] * 8 + [FREE, FREE] + [KEPT] * 6 + [HBM] * 4,
        out_specs=(KEPT, KEPT) + (HBM,) * 9,
        scratch_shapes=[
            vm(width, width, bf16),
            vm(width, ff, bf16),
            vm(ff, width, bf16),
            vm(tokens, width, bf16),
            pltpu.SemaphoreType.DMA((4,)),
            vm(ext, width, bf16),
            vm(ext, width, bf16),
            vm(tokens, width, bf16),
            vm(tokens, ff, bf16),
            vm(tokens, width, f32),
            vm(tokens, 128, f32),
            vm(tokens, width, f32),
            vm(tokens, width, bf16),
            vm(tokens, width, bf16),
            vm(tokens, width, bf16),
            vm(tokens, width, bf16),
            vm(width, width, bf16),
            vm(SMALL, width, f32),
            vm(SMALL, width, bf16),
            group[0],
            pltpu.SemaphoreType.DMA((10 + len(row_blocks(tokens)),)),
            group[1],
            pltpu.SemaphoreType.DMA((PARTS, 2)),
        ],
        compiler_params=params(46),
        cost_estimate=cost(4 * tokens * width * (width + 3 * ff) + 8e9, 40 * tokens * width, 2 * tokens * ff),
        name="layer",
    )(place, spans, se, bv, bo, g1, s1, bu, bd, g2, s2, xl, xr, q, k, v, x, wk, wv, wo, wu, wd, dy)


def up_grad_kernel(place, mid_low, d_up, send, keep, buf, gsems):
    width = mid_low.shape[1]
    size = width // 2

    def block(part):
        rows, cols = (part % 2) * size, (part // 2) * width
        return mm_tn(mid_low[:, rows : rows + size], d_up[:, cols : cols + width])

    write_group(block, send, keep, buf, gsems, place, size // 2)


def up_grad(place, mid_low, d_up, after=()):
    tokens, width = mid_low.shape
    ff = d_up.shape[1]
    return call(
        up_grad_kernel,
        out_shape=group_shapes(width // 4, width),
        in_specs=[SMEM, KEPT, KEPT],
        out_specs=(HBM, HBM),
        scratch_shapes=group_scratch(ff, width),
        after=after,
        compiler_params=params(12),
        cost_estimate=cost(2 * tokens * width * ff, 14 * tokens * width),
        name="up_grad",
    )(place, mid_low, d_up)


def rest_grad_kernel(halves, place, x, *refs):
    parts, (send, keep, xb, rhs, grad, small, gsems, sems, ssems) = refs[: 3 * halves], refs[3 * halves :]
    tokens, width = x.shape
    size = width // 2
    some = width // halves
    pairs = [(x, xb)]
    for n in range(3):
        for h in range(halves):
            pairs.append((parts[3 * h + n], rhs.at[n, :, pl.ds(h * some, some)]))
    ready = loads(pairs, sems)
    ready(0)
    stride = 3 * width // PARTS // 2
    waits = []
    for done in range(0, 3 * width, size):
        which = done // width
        if done % width == 0:
            for h in range(halves):
                ready(1 + which * halves + h)
        at = done % width
        grad[done : done + size, :] = mm_tn(xb[:, at : at + size], rhs[which]).astype(bf16)
        while 2 * stride * (len(waits) + 1) <= done + size:
            part = len(waits)
            source = lambda n, part=part: grad.at[pl.ds((2 * part + n) * stride, stride)]
            waits.append(piece_copies(part, place, source, gsems.at[part], send, keep, stride))
    ones = jnp.ones((8, tokens), bf16)
    row = lax.broadcasted_iota(i32, (8, width), 0)
    sums = jnp.where(row == 0, mm(ones, rhs[0]), jnp.where(row == 1, mm(ones, rhs[2]), 0.0))
    small[...] = jnp.concatenate([sums, jnp.zeros((SMALL - 8, width), f32)], axis=0).astype(bf16)
    end = pl.ds(PARTS * stride, SMALL)
    copies = [out_copy(small, o.at[end], ssems.at[i]) for i, o in enumerate((send, keep))]
    for c in copies:
        c.wait()
    for wait in waits:
        wait()


def rest_grad(place, x, parts, after=()):
    tokens, width = x.shape
    halves = len(parts)
    return call(
        functools.partial(rest_grad_kernel, halves),
        out_shape=group_shapes(3 * width // PARTS // 2, width, SMALL),
        in_specs=[SMEM] + [HBM] * (1 + 3 * halves),
        out_specs=(HBM, HBM),
        scratch_shapes=[
            pltpu.VMEM((tokens, width), bf16),
            pltpu.VMEM((3, tokens, width), bf16),
            pltpu.VMEM((3 * width, width), bf16),
            pltpu.VMEM((SMALL, width), bf16),
            pltpu.SemaphoreType.DMA((PARTS, 2)),
            pltpu.SemaphoreType.DMA((1 + 3 * halves,)),
            pltpu.SemaphoreType.DMA((2,)),
        ],
        after=after,
        compiler_params=params(20),
        cost_estimate=cost(6 * tokens * width * width, 20 * tokens * width),
        name="rest_grad",
    )(place, x, *sum(map(tuple, parts), ()))


def inputs_grad_kernel(halves, d_one, *refs):
    parts, (wq, wk, wv, out) = refs[: 3 * halves], refs[3 * halves :]
    total = d_one[...]
    some = wq.shape[1] // halves
    for h in range(halves):
        for g, w in zip(parts[3 * h : 3 * h + 3], (wq, wk, wv)):
            total = total + mm_nt(g[...], w[:, h * some : (h + 1) * some])
    out[...] = total


def inputs_grad(d_one, parts, wq, wk, wv, after=()):
    tokens, width = d_one.shape
    halves = len(parts)
    tok = lambda n: pl.BlockSpec((ROWS, n), lambda i: (i, 0))
    full = pl.BlockSpec((width, width), lambda i: (0, 0))
    return call(
        functools.partial(inputs_grad_kernel, halves),
        grid=(tokens // ROWS,),
        out_shape=(jax.ShapeDtypeStruct((tokens, width), f32),),
        in_specs=[tok(width)] + [tok(width // halves)] * (3 * halves) + [full] * 3,
        out_specs=(tok(width),),
        after=after,
        compiler_params=params(16, dimension_semantics=("arbitrary",)),
        cost_estimate=cost(6 * tokens * width * width, 20 * tokens * width),
        name="inputs_grad",
    )(d_one, *sum(map(tuple, parts), ()), wq, wk, wv)


def swap(value, axis, bit):
    count = lax.axis_size(axis)
    return lax.ppermute(value, axis, [(i, i ^ bit) for i in range(count)])


def plus(a, b):
    return (a.astype(f32) + b.astype(f32)).astype(bf16)


def layer_bits():
    return list(range(1, lax.axis_size("dp")))


def far_bits():
    bit, bits = PARTS, []
    while bit < lax.axis_size("seq"):
        bits.append(bit)
        bit *= 2
    return bits


def axis_bits(axis):
    return [1 << n for n in range((lax.axis_size(axis) - 1).bit_length())]


class Sum:
    def __init__(self, send, keep, tail=0):
        self.mine, self.got, self.payload, self.tail = [keep], [], [send], tail
        self.swaps = [("seq", 1)]
        self.steps = self.run()

    def receive(self, token):
        if self.got:
            *self.got, _ = lax.optimization_barrier((*self.got, token))
            next(self.steps)

    def send(self):
        self.got = [swap(p, *s) for p, s in zip(self.payload, self.swaps)]

    def tailed(self, payloads):
        rows = [p.reshape(-1, p.shape[-1]) for p in payloads]
        if self.tail:
            rows[0] = jnp.concatenate([rows[0], self.small], axis=0)
        return rows

    def untailed(self, like):
        if self.tail:
            self.small = plus(self.small, self.got[0][-self.tail :])
            self.got[0] = self.got[0][: -self.tail]
        return [g.reshape(m.shape) for g, m in zip(self.got, like)]

    def run(self):
        keep, got = self.mine[0], self.got[0]
        width = keep.shape[-1]
        both = plus(keep, got)
        if self.tail:
            self.small, both = both[-self.tail :], both[: -self.tail]
        both = both.reshape((2, 2, 2, -1, width))
        parts = [both[0], both[1]]
        for bits in ((2, 4), (4, 2)):
            keeps = [p[0] for p in parts]
            self.payload, self.swaps = self.tailed([p[1] for p in parts]), [("seq", b) for b in bits]
            yield
            parts = list(map(plus, keeps, self.untailed(keeps)))
        layers = axis_bits("dp")
        layer = lax.axis_index("dp")
        rows = parts[0].shape[0]
        part = jnp.stack(parts).reshape((2,) * len(layers) + (-1, width))
        for bit in layers:
            mine = (layer // bit) % 2
            keep = lax.dynamic_index_in_dim(part, mine, 0, keepdims=False)
            away = lax.dynamic_index_in_dim(part, 1 - mine, 0, keepdims=False)
            self.payload, self.swaps = self.tailed([away]), [("dp", bit)]
            yield
            part = plus(keep, self.untailed([keep])[0])
        for bit in far_bits():
            part = plus(part, swap(part, "seq", bit))
            if self.tail:
                self.small = plus(self.small, swap(self.small, "seq", bit))
        for bit in reversed(layers):
            self.payload, self.swaps = [part], [("dp", bit)]
            yield
            low = (layer // bit) % 2 == 0
            got = self.got[0]
            part = jnp.stack([jnp.where(low, part, got), jnp.where(low, got, part)])
        parts = list(part.reshape(2, rows, width))
        for bits in ((4, 2), (2, 4)):
            self.payload, self.swaps = parts, [("seq", b) for b in bits]
            yield
            parts = [jnp.stack(pair) for pair in zip(parts, self.got)]
        whole = jnp.stack(parts).reshape(8, -1, width)
        self.payload, self.swaps = [whole], [("seq", 1)]
        yield
        self.result = (whole, self.got[0])
        self.payload = []
        yield


def advance(token, *sums):
    for s in sums:
        s.receive(token)
    payloads = lax.optimization_barrier(tuple(p for s in sums for p in s.payload))
    at = 0
    for s in sums:
        s.payload = list(payloads[at : at + len(s.payload)])
        at += len(s.payload)
        s.send()
    return payloads[0] if payloads else token


def spread_kernel(kind, count, place, mine, other, *refs):
    outs, (buf, sems) = refs[:count], refs[count:]
    here = place[1]
    rows, width = mine.shape[1:]
    slots = buf.shape[0]
    waits = []
    for n in range(2 * PARTS):
        part, piece = n // 2, n % 2
        slot = n % slots
        if n >= slots:
            for c in waits[n - slots]:
                c.wait()
        to = part ^ here
        core, x, y = to & 1, (to >> 1) & 1, (to >> 2) & 1
        at = 4 + 2 * y + x if piece else 2 * x + y
        for side, source in ((0, mine), (1, other)):

            @pl.when(core == side)
            def _(source=source, slot=slot, at=at):
                buf[slot] = source[at].astype(f32)

        pairs = []
        if kind == "up":
            down = (part % 2) * 2 * rows + piece * rows
            pairs.append((0, rows, outs[0].at[pl.ds(down, rows), pl.ds((part // 2) * width, width)]))
        elif kind == "down":
            few = width // PARTS // 2
            pairs.append((0, rows - few, outs[0].at[pl.ds(n * (rows - few), rows - few)]))
            pairs.append((rows - few, few, outs[1].at[pl.ds(n * few, few)]))
        else:
            first, last = n * rows, (n + 1) * rows
            while first < last:
                which = first // width
                size = min(last, (which + 1) * width) - first
                pairs.append((first - n * rows, size, outs[which].at[pl.ds(first - which * width, size)]))
                first += size
        waits.append([out_copy(buf.at[slot, pl.ds(a, s)], o, sems.at[slot, i]) for i, (a, s, o) in enumerate(pairs)])
    for wait in waits[-slots:]:
        for c in wait:
            c.wait()


def spread(kind, place, mine, other, after=()):
    rows, width = mine.shape[1:]
    shapes = {
        "down": [(2 * PARTS * rows - width, width), (width, width)],
        "up": [(width, 2 * PARTS * rows)],
        "rest": [(width, width)] * 3,
    }[kind]
    slots = 6
    return call(
        functools.partial(spread_kernel, kind, len(shapes)),
        out_shape=[jax.ShapeDtypeStruct(s, f32) for s in shapes],
        in_specs=[SMEM, FREE, FREE],
        out_specs=[HBM] * len(shapes),
        after=after,
        scratch_shapes=[pltpu.VMEM((slots, rows, width), f32), pltpu.SemaphoreType.DMA((slots, 2))],
        compiler_params=params(8),
        cost_estimate=cost(rows * width, 12 * PARTS * rows * width),
        name="spread_" + kind,
    )(place, mine, other)


def sum_small(vec):
    for axis in ("seq", "dp"):
        bit = 1
        while bit < lax.axis_size(axis):
            vec = vec + swap(vec, axis, bit)
            bit *= 2
    return vec


def neighbours(first, last):
    count = lax.axis_size("seq")
    up = [(i, i + 1) for i in range(count - 1)]
    low = lax.ppermute(last, "seq", up)
    high = lax.ppermute(first, "seq", [(b, a) for a, b in up])
    return low, high


def body(
    inputs, lengths, w_query, b_query, w_key, w_value, b_value, w_out, b_out, gain_one, shift_one,
    w_up, b_up, w_down, b_down, gain_two, shift_two, d_output,
):
    rows, tokens, width = inputs.shape
    reach = ITEM_MOST
    here = lax.axis_index("seq")
    place = jnp.stack([here * tokens, here & (PARTS - 1), lax.axis_index("dp")]).astype(i32)
    x = inputs.reshape(tokens, width)
    dy = d_output.reshape(tokens, width)

    xl, xr = neighbours(x[:reach], x[-reach:])
    se, spans, se_low, spans_low, q, k, v, *kept = front(
        place, lengths, x, w_query, w_key, w_value, b_query, b_value, reach
    )
    d_up, mid_low, kh, vh, output, d_one, d_attn, d_low, d_high, send1, keep1 = layer(
        place, spans, se, xl, xr, *kept, w_out, w_up, w_down, dy, b_value, b_out, gain_one, shift_one, b_up, b_down, gain_two, shift_two
    )
    one = Sum(send1, keep1, SMALL)
    token = advance(d_attn, one)
    dl, dr = neighbours(d_low, d_high)
    send2, keep2 = up_grad(place, mid_low, d_up, after=[token])
    dl, dr, send2 = lax.optimization_barrier((dl, dr, send2))
    two = Sum(send2, keep2)
    token = advance(send2, one, two)
    args = (HALVES, spans_low, se_low, q, k, v, d_attn, kh, vh, xl, xr, dl, dr, w_query, b_query)
    parts = [attend_back(0, *args, after=[token])]
    token = advance(parts[0][0], one, two)
    parts.append(attend_back(1, *args, after=[token]))
    token = advance(parts[1][0], one)
    send3, keep3 = rest_grad(place, x, parts, after=[token])
    three = Sum(send3, keep3, SMALL)
    token = advance(send3, one, two, three)
    sums = {1: one, 2: two, 3: three}
    for event in ORDER:
        if event == 0:
            (d_inputs,) = inputs_grad(d_one, parts, w_query, w_key, w_value, after=[token])
            token = d_inputs
        elif event < 0:
            kind = ("down", "up", "rest")[-event - 1]
            grads = spread(kind, place, *sums[-event].result, after=[token])
            token = grads[0]
            if kind == "down":
                g_w_down, g_w_out = grads
            elif kind == "up":
                (g_w_up,) = grads
            else:
                g_w_query, g_w_key, g_w_value = grads
        else:
            token = advance(token, *[sums[int(g)] for g in str(event)])
    small = jnp.concatenate([one.small, three.small], axis=0).astype(f32)
    ff = w_up.shape[1]
    many = ff // width
    return (
        output.reshape(rows, tokens, width),
        d_inputs.reshape(rows, tokens, width),
        g_w_query,
        small[SMALL],
        g_w_key,
        g_w_value,
        small[SMALL + 1],
        g_w_out,
        small[5],
        small[3],
        small[4],
        g_w_up,
        small[8 : 8 + many].reshape(ff),
        g_w_down,
        small[0],
        small[1],
        small[2],
    )


def solution(mesh):
    split, whole = P("dp", "seq", None), P()
    return jax.shard_map(
        body,
        mesh=mesh,
        in_specs=(split, P("dp", None)) + (whole,) * 15 + (split,),
        out_specs=(split, split) + (whole,) * 15,
        check_vma=False,
    )
```

```python
import functools

import jax
import jax.numpy as jnp
from jax import lax
from jax.experimental import pallas as pl
from jax.experimental.pallas import tpu as pltpu
from jax.sharding import PartitionSpec as P

HEADS = 12
HEAD_DIM = 64
ITEM_MOST = 256
EPS = 1e-12
SCALE = 0.125
MASKED = -1e30
FAR = 1e9
TILE = 128
PAIR = 2 * HEAD_DIM
WIDTHS = (192, 256, 384, 640)
ROWS = 256
SMALL = 16
ORDER = (3, 2, 1, 3, 2, 1, 3, 2, 1, 3, 2, 1, 23, 1, 3, 2, 3, 1, -1, 23, 0, 2, -2, 3, 3, -3)
HALVES = 2
PARTS = 8
CHUNK = 512

bf16 = jnp.bfloat16
f32 = jnp.float32
i32 = jnp.int32
ANY = pl.BlockSpec(memory_space=pl.ANY)
HBM = pl.BlockSpec(memory_space=pltpu.HBM)
KEPT = pl.BlockSpec(memory_space=pltpu.VMEM)
FREE = pl.BlockSpec(memory_space=pltpu.VMEM)
NEAR = pl.BlockSpec(memory_space=pltpu.VMEM)
SMEM = pl.BlockSpec(memory_space=pltpu.SMEM)
VMEM = pl.BlockSpec(memory_space=pltpu.VMEM)


def params(mib, **kw):
    return pltpu.CompilerParams(vmem_limit_bytes=mib * 1024 * 1024, **kw)


def cost(flops, nbytes, trans=0):
    return pl.CostEstimate(flops=int(flops), bytes_accessed=int(nbytes), transcendentals=int(trans))


def mm(a, b):
    return lax.dot_general(a, b, (((1,), (0,)), ((), ())), preferred_element_type=f32)


def mm_nt(a, b):
    return lax.dot_general(a, b, (((1,), (1,)), ((), ())), preferred_element_type=f32)


def mm_tn(a, b):
    return lax.dot_general(a, b, (((0,), (0,)), ((), ())), preferred_element_type=f32)


def large(a):
    return a.size * a.dtype.itemsize > 512 * 1024


def call(kernel, out_shape, in_specs, out_specs, after=(), anywhere=False, **kw):
    kept = lambda a, spec: pltpu.VMEM if spec is KEPT else pltpu.HBM if spec is HBM or spec is NEAR or (large(a) and spec is not FREE and spec is not ANY and not anywhere) else None
    shapes = [k(o.shape, o.dtype) if (k := kept(o, spec)) else o for o, spec in zip(out_shape, out_specs)]
    count = len(in_specs)

    def plain(*refs):
        return kernel(*refs[:count], *refs[count + len(after) :])

    specs = list(in_specs) + [ANY] * len(after)
    run = pl.pallas_call(plain, out_shape=shapes, in_specs=specs, out_specs=list(out_specs), **kw)

    def apply(*args):
        args = [
            pltpu.with_memory_space_constraint(a, k) if (k := kept(a, spec)) else a
            for a, spec in zip(args, in_specs)
        ]
        return run(*args, *[pltpu.with_memory_space_constraint(a, pltpu.HBM) if a.dtype == f32 else a for a in after])

    return apply


def loads(pairs, sems):
    copies = [pltpu.make_async_copy(a, b, sems.at[i]) for i, (a, b) in enumerate(pairs)]
    for c in copies:
        c.start()
    return lambda i: copies[i].wait()


def out_copy(source, target, sem):
    c = pltpu.make_async_copy(source, target, sem)
    c.start()
    return c


def row_blocks(tokens):
    return [slice(r, r + ROWS) for r in range(0, tokens, ROWS)]


def front_kernel(
    place, lengths, bq, bv, x, wq, wk, wv,
    se, spans, se_low, spans_low, q, k, v, qv, kv, vv, xv, wkv, wvv, wqb, sems, osems,
):
    ready = loads([(x, xv), (wq, wqb), (wk, wkv), (wv, wvv)], sems)
    slots = lengths.shape[1]
    tokens = x.shape[0]
    ext = se.shape[1]
    reach = (ext - tokens) // 2
    step = max(d for d in range(8, 129, 8) if slots % d == 0)
    start = place[0] - reach
    pos = (lax.broadcasted_iota(i32, (1, ext), 1) + start).astype(f32)
    sizes = lengths[...].astype(f32)

    def scan(c, state):
        low, high = state
        index = lax.broadcasted_iota(i32, (step, slots), 0) + c * step
        upto = lax.broadcasted_iota(i32, (step, slots), 1) <= index
        ends = jnp.sum(jnp.where(upto, sizes, 0.0), axis=1, keepdims=True)
        before = ends <= pos
        low = jnp.maximum(low, jnp.max(jnp.where(before, ends, 0.0), axis=0, keepdims=True))
        high = jnp.minimum(high, jnp.min(jnp.where(before, FAR, ends), axis=0, keepdims=True))
        return low, high

    low, high = lax.fori_loop(
        0, slots // step, scan, (jnp.zeros((1, ext), f32), jnp.full((1, ext), FAR, f32))
    )
    real = (pos >= 0.0) & (high < FAR)
    local = lax.broadcasted_iota(i32, (1, ext), 1).astype(f32)
    offset = start.astype(f32)
    own = (local >= reach) & (local < reach + tokens)
    low_e = jnp.where(real, low - offset, local)
    high_e = jnp.where(real, high - offset, local + 1.0)
    shared = real & (
        ((local < reach) & (high_e > reach)) | ((local >= reach + tokens) & (low_e < reach + tokens))
    )
    used = own | shared
    low_e = jnp.where(used, low_e, 0.0)
    high_e = jnp.where(used, high_e, 0.0)
    se[0:1, :] = low_e
    se[1:2, :] = high_e
    se[2:8, :] = jnp.zeros((6, ext), f32)
    se_copy = out_copy(se, se_low, osems.at[3])

    def note(i, value):
        spans[i] = value
        spans_low[i] = value

    note(0, jnp.sum(sizes).astype(i32))
    for t in range(ext // TILE):
        sl = slice(t * TILE, (t + 1) * TILE)
        some = high_e[:, sl] > low_e[:, sl]
        first = jnp.min(jnp.where(some, low_e[:, sl], FAR)).astype(i32)
        last = jnp.max(jnp.where(some, high_e[:, sl], -1.0)).astype(i32)
        at = first & ~15
        span = last - at
        kind = len(WIDTHS)
        begin = min(max(t * TILE - reach, 0), ext - WIDTHS[-1])
        for i in reversed(range(len(WIDTHS) - 1)):
            kind = jnp.where(span <= WIDTHS[i], i + 1, kind)
            begin = jnp.where(span <= WIDTHS[i], jnp.minimum(at, ext - WIDTHS[i]), begin)
        note(8 + 2 * t, jnp.where(last < 0, 0, kind))
        note(9 + 2 * t, begin)

    copies = [se_copy]
    ready(0)
    for i, (w, b, out, to) in enumerate(((wqb, bq, qv, q), (wkv, None, kv, k), (wvv, bv, vv, v))):
        ready(i + 1)
        for r in row_blocks(tokens):
            y = mm(xv[r, :], w[...])
            if b is not None:
                y = y + b[...]
            y = y.astype(bf16)
            out[r, :] = y * bf16(SCALE) if i == 0 else y
        copies.append(out_copy(out, to, osems.at[i]))
    for c in copies:
        c.wait()


def front(place, lengths, x, wq, wk, wv, bq, bv, reach):
    tokens, width = x.shape
    ext = tokens + 2 * reach
    like = lambda a: jax.ShapeDtypeStruct(a.shape, a.dtype)
    kept = [like(a) for a in (x, x, x, x, wk, wv)]
    return call(
        front_kernel,
        out_shape=(
            *[
                jax.ShapeDtypeStruct((8, ext), f32),
                jax.ShapeDtypeStruct((8 + 2 * (ext // TILE),), i32),
            ]
            * 2,
            like(x),
            like(x),
            like(x),
            *kept,
        ),
        in_specs=[SMEM, NEAR, NEAR, NEAR] + [HBM] * 4,
        out_specs=(KEPT, SMEM, HBM, SMEM, HBM, HBM, HBM) + (KEPT,) * len(kept),
        scratch_shapes=[
            pltpu.VMEM((width, width), bf16),
            pltpu.SemaphoreType.DMA((4,)),
            pltpu.SemaphoreType.DMA((4,)),
        ],
        compiler_params=params(8),
        cost_estimate=cost(6 * tokens * width * width, 8 * tokens * width),
        name="front",
    )(place, lengths, bq, bv, x, wq, wk, wv)


def tile_bias(se, t, at, width):
    base = pl.multiple_of(t * TILE, TILE)
    low = se[0:1, pl.ds(base, TILE)]
    high = se[1:2, pl.ds(base, TILE)]
    key = (lax.broadcasted_iota(i32, (width, TILE), 0) + at).astype(f32)
    one = jnp.where((key >= low) & (key < high), 0.0, MASKED)
    some = jnp.where(high > low, 1.0, 0.0)
    return jnp.concatenate([one, one], axis=1), jnp.concatenate([some, some], axis=1)


def stacked(pair):
    lane = lax.broadcasted_iota(i32, pair.shape, 1)
    zero = jnp.zeros_like(pair)
    return jnp.concatenate(
        [jnp.where(lane < HEAD_DIM, pair, zero), jnp.where(lane < HEAD_DIM, zero, pair)], axis=0
    )


def unstacked(both):
    own = jnp.concatenate([both[:HEAD_DIM, :TILE], both[HEAD_DIM:, TILE:]], axis=0)
    return own.T


def each_tile(spans, first, last, tile):
    def each(t, _):
        kind, at = spans[8 + 2 * t], spans[9 + 2 * t]
        for i, span in enumerate(WIDTHS):
            pl.when(kind == i + 1)(functools.partial(tile, t, at, span))
        return 0

    lax.fori_loop(first, last, each, 0)


def attend_tile(se, q, kx, vx, attn, reach, t, at, span):
    width = q.shape[1]
    bias, _ = tile_bias(se, t, at, span)
    rows = pl.ds(pl.multiple_of(t * TILE - reach, TILE), TILE)
    window = pl.ds(pl.multiple_of(at, 16), span)
    pairs = [slice(p, p + PAIR) for p in range(0, width, PAIR)]
    scores = [mm_nt(kx[window, c], stacked(q[rows, c])) for c in pairs]
    soft = []
    for s in scores:
        s = s + bias
        weights = jnp.exp(s - jnp.max(s, axis=0, keepdims=True))
        soft.append((weights.astype(bf16), jnp.sum(weights, axis=0, keepdims=True)))
    for c, (weights, total) in zip(pairs, soft):
        attn[rows, c] = unstacked(mm_tn(vx[window, c], weights) / total).astype(bf16)


def attend_back_tile(se, qx, kx, vx, dox, dkx, dvx, t, at, span):
    width = qx.shape[1]
    bias, some = tile_bias(se, t, at, span)
    rows = pl.ds(pl.multiple_of(t * TILE, TILE), TILE)
    window = pl.ds(pl.multiple_of(at, 16), span)
    pairs = [slice(p, p + PAIR) for p in range(0, width, PAIR)]
    first = []
    for c in pairs:
        query, dout = stacked(qx[rows, c]), stacked(dox[rows, c])
        first.append((query, dout, mm_nt(kx[window, c], query), mm_nt(vx[window, c], dout)))
    second = []
    for query, dout, scores, dprob in first:
        scores = scores + bias
        weights = jnp.exp(scores - jnp.max(scores, axis=0, keepdims=True))
        probs = weights * (some / jnp.sum(weights, axis=0, keepdims=True))
        delta = jnp.sum(probs * dprob, axis=0, keepdims=True)
        second.append((probs.astype(bf16), (probs * (dprob - delta)).astype(bf16)))
    for c, (query, dout, _, _), (probs, dscore) in zip(pairs, first, second):
        dvx[window, c] += mm(probs, dout)
        dkx[window, c] += mm(dscore, query)
        qx[rows, c] = (unstacked(mm_tn(kx[window, c], dscore)) * SCALE).astype(bf16)


def attend_back_kernel(
    half, spans, se, bq, q, k, v, do, kh, vh, xl, xr, dl, dr, wq,
    dq, dk, dv, qx, kx, vx, dox, dkx, dvx, dkb, dvb, wb, xb, sems, osems,
):
    tokens = q.shape[0]
    reach = xl.shape[0]
    ext, some = kx.shape
    cols = pl.ds(half * some, some)
    own, low, high = pl.ds(reach, tokens), pl.ds(0, reach), pl.ds(reach + tokens, reach)
    ready = loads(
        [
            (wq.at[:, cols], wb),
            (xl, xb.at[low]),
            (xr, xb.at[pl.ds(reach, reach)]),
            (q.at[:, cols], qx.at[own]),
            (k.at[:, cols], kx.at[own]),
            (v.at[:, cols], vx.at[own]),
            (do.at[:, cols], dox.at[own]),
            (kh.at[pl.ds(0, reach), cols], kx.at[low]),
            (kh.at[pl.ds(reach, reach), cols], kx.at[high]),
            (vh.at[pl.ds(0, reach), cols], vx.at[low]),
            (vh.at[pl.ds(reach, reach), cols], vx.at[high]),
            (dl.at[:, cols], dox.at[low]),
            (dr.at[:, cols], dox.at[high]),
        ],
        sems,
    )
    dkx[...] = jnp.zeros_like(dkx)
    dvx[...] = jnp.zeros_like(dvx)
    for i in range(3):
        ready(i)
    bias = bq[...][half * some : (half + 1) * some]
    for at, to in ((0, 0), (reach, reach + tokens)):
        y = (mm(xb[at : at + reach, :], wb[...]) + bias).astype(bf16)
        qx[to : to + reach, :] = y * bf16(SCALE)
    for i in range(3, 13):
        ready(i)
    tile = functools.partial(attend_back_tile, se, qx, kx, vx, dox, dkx, dvx)
    each_tile(spans, 0, ext // TILE, tile)
    copies = [out_copy(qx.at[own], dq, osems.at[0])]
    dkb[...] = dkx[reach : reach + tokens, :].astype(bf16)
    copies.append(out_copy(dkb, dk, osems.at[1]))
    dvb[...] = dvx[reach : reach + tokens, :].astype(bf16)
    copies.append(out_copy(dvb, dv, osems.at[2]))
    for c in copies:
        c.wait()


def attend_back(half, halves, spans, se, q, k, v, do, kh, vh, xl, xr, dl, dr, wq, bq, after=()):
    tokens, width = q.shape
    reach = xl.shape[0]
    ext = tokens + 2 * reach
    some = width // halves
    out = jax.ShapeDtypeStruct((tokens, some), bf16)
    return call(
        functools.partial(attend_back_kernel, half),
        out_shape=(out, out, out),
        in_specs=[SMEM, NEAR, VMEM] + [HBM] * 11,
        out_specs=(HBM, HBM, HBM),
        scratch_shapes=[pltpu.VMEM((ext, some), bf16)] * 4
        + [pltpu.VMEM((ext, some), f32)] * 2
        + [pltpu.VMEM((tokens, some), bf16)] * 2
        + [pltpu.VMEM((width, some), bf16), pltpu.VMEM((2 * reach, width), bf16)]
        + [pltpu.SemaphoreType.DMA((13,)), pltpu.SemaphoreType.DMA((3,))],
        after=after,
        compiler_params=params(20),
        cost_estimate=cost(16e9 / halves, 20 * tokens * some),
        name="attend_back_%d" % half,
    )(spans, se, bq, q, k, v, do, kh, vh, xl, xr, dl, dr, wq)


def piece_copies(part, place, source, sem, send, keep, stride, offset=0):
    to = part ^ place[1]
    core, x, y = to & 1, (to >> 1) & 1, (to >> 2) & 1
    rows = source(0).shape[0]

    def copies(out):
        return [
            pltpu.make_async_copy(
                source(n), out.at[pl.ds(pl.multiple_of(at * stride + offset, 16), rows)], sem.at[n]
            )
            for n, at in enumerate((2 * x + y, 4 + 2 * y + x))
        ]

    for here, out in ((1, send), (0, keep)):

        @pl.when(core == here)
        def _(out=out):
            for c in copies(out):
                c.start()

    def wait():
        for c in copies(keep):
            c.wait()

    return wait


def write_group(block, send, keep, buf, sems, place, stride):
    slots, rows = buf.shape[:2]
    half = rows // 2
    waits = []
    for part in range(PARTS):
        slot = part % slots
        value = block(part).astype(bf16)
        if part >= slots:
            waits[part - slots]()
        buf[slot] = value
        source = lambda n, slot=slot: buf.at[slot, pl.ds(n * half, half)]
        waits.append(piece_copies(part, place, source, sems.at[slot], send, keep, stride))
    for wait in waits[-slots:]:
        wait()


def group_shapes(stride, width, tail=0):
    return (jax.ShapeDtypeStruct((PARTS * stride + tail, width), bf16),) * 2


def group_scratch(rows, width, slots=PARTS):
    return [pltpu.VMEM((slots, rows // PARTS, width), bf16), pltpu.SemaphoreType.DMA((slots, 2))]


def gelu_both(z):
    u = jnp.abs(z) * 0.7071067811865476
    t = 1.0 / (1.0 + 0.3275911 * u)
    bell = jnp.exp2(z * (z * -0.7213475204444817))
    poly = t * (
        0.5 * 0.254829592
        + t * (0.5 * -0.284496736 + t * (0.5 * 1.421413741 + t * (0.5 * -1.453152027 + t * (0.5 * 1.061405429))))
    )
    tail = poly * bell
    cdf = jnp.where(z >= 0.0, 1.0 - tail, tail)
    return z * cdf, cdf + z * bell * 0.3989422804014327


def center(v):
    mean = jnp.mean(v, axis=1, keepdims=True)
    c = v - mean
    rstd = lax.rsqrt(jnp.mean(c * c, axis=1, keepdims=True) + EPS)
    return c * rstd, rstd


def center_back(e, xhat, rstd):
    return rstd * (
        e - jnp.mean(e, axis=1, keepdims=True) - xhat * jnp.mean(e * xhat, axis=1, keepdims=True)
    )


def colsum(v):
    return jnp.sum(v, axis=0, keepdims=True)


def layer_kernel(
    place, spans, se, bv, bo, g1, s1, bu, bd, g2, s2, xl, xr, q, k, v, x, wk, wv, wo_h, wu_h, wd_h, dy_h,
    d_up, mid_low, kh, vh, out, d_one, d_attn, d_low, d_high, send, keep,
    wo, wu, wd, dy, lsems, kx, vx, attb, act, xh, rstd, two, ob, dd, branch, datt, gout, line, small, buf, osems, gsems, hsems,
):
    tokens, width = x.shape
    ff = wu.shape[1]
    reach = xl.shape[0]
    own = slice(reach, reach + tokens)
    blocks = row_blocks(tokens)
    ready = loads([(wo_h, wo), (wu_h, wu), (wd_h, wd), (dy_h, dy)], lsems)
    copies = []

    def put(source, target):
        copies.append(out_copy(source, target, osems.at[len(copies)]))

    line[...] = jnp.zeros_like(line)
    kx[own, :] = k[...]
    vx[own, :] = v[...]
    for part, at in ((xl, 0), (xr, reach + tokens)):
        kx[at : at + reach, :] = mm(part[...], wk[...]).astype(bf16)
        vx[at : at + reach, :] = (mm(part[...], wv[...]) + bv[...]).astype(bf16)
    for n, at in enumerate((0, reach + tokens)):
        for ref, to in ((kx, kh), (vx, vh)):
            put(ref.at[pl.ds(at, reach)], to.at[pl.ds(n * reach, reach)])
    tile = functools.partial(attend_tile, se, q, kx, vx, attb, reach)
    each_tile(spans, reach // TILE, (reach + tokens) // TILE, tile)
    ready(0)
    for r, b in zip(blocks, [mm(attb[r, :], wo[...]) for r in blocks]):
        hat, rs = center(x[r, :].astype(f32) + b + bo[...])
        mid = hat * g1[...] + s1[...]
        xh[r, :] = hat
        rstd[r, :] = jnp.broadcast_to(rs, (ROWS, rstd.shape[1]))
        mid_low[r, :] = mid.astype(bf16)
        two[r, :] = mid + bd[...]

    ready(1)
    ready(2)

    def ups(c):
        return [mm(mid_low[r, :], wu[:, c : c + CHUNK]) for r in blocks]

    up = ups(0)
    for c in range(0, ff, CHUNK):
        cols = slice(c, c + CHUNK)
        now = up
        if c + CHUNK < ff:
            up = ups(c + CHUNK)
        for r, z in zip(blocks, now):
            a, s = gelu_both(z + bu[...][cols])
            act[r, cols] = a.astype(bf16)
            d_up[r, cols] = s.astype(bf16)
        for r in blocks:
            two[r, :] += mm(act[r, cols], wd[cols, :])

    ready(3)
    sums = [0.0] * 6
    for r in blocks:
        hat, rs = center(two[r, :])
        token = place[0] + r.start + lax.broadcasted_iota(i32, (ROWS, 1), 0)
        valid = jnp.where(token < spans[0], 1.0, 0.0)
        ob[r, :] = ((hat * g2[...] + s2[...]) * valid).astype(bf16)
        d = dy[r, :].astype(f32) * valid
        d2 = center_back(d * g2[...], hat, rs)
        two[r, :] = d2
        d2 = d2.astype(bf16)
        dd[r, :] = d2
        for i, term in enumerate((d2.astype(f32), d * hat, d)):
            sums[i] = sums[i] + colsum(term)
    put(ob, out)
    size = ff // PARTS
    stride = (send.shape[0] - SMALL) // PARTS
    write_group(lambda p: mm_tn(act[:, p * size : (p + 1) * size], dd[...]), send, keep, buf, gsems, place, stride)

    def downs(c):
        return [mm_nt(dd[r, :], wd[c : c + CHUNK, :]) for r in blocks]

    down = downs(0)
    for c in range(0, ff, CHUNK):
        cols = slice(c, c + CHUNK)
        now = down
        if c + CHUNK < ff:
            down = downs(c + CHUNK)
        total = 0.0
        for r, d in zip(blocks, now):
            du = (d_up[r, cols].astype(f32) * d).astype(bf16)
            d_up[r, cols] = du
            total = total + colsum(du.astype(f32))
        for half in range(0, CHUNK, CHUNK // 2):
            n, at = divmod(c + half, width)
            line[8 + n : 9 + n, at : at + CHUNK // 2] = total[:, half : half + CHUNK // 2]
        for r in blocks:
            two[r, :] += mm_nt(d_up[r, cols], wu[:, cols])
    for r in blocks:
        d_mid = two[r, :]
        hat = xh[r, :]
        d1 = center_back(d_mid * g1[...], hat, rstd[r, 0:1])
        two[r, :] = d1
        d1 = d1.astype(bf16)
        branch[r, :] = d1
        for i, term in enumerate((d_mid * hat, d_mid, d1.astype(f32))):
            sums[3 + i] = sums[3 + i] + colsum(term)
    put(two, d_one)
    for r in blocks:
        datt[r, :] = mm_nt(branch[r, :], wo[...]).astype(bf16)
        at = pl.ds(r.start, ROWS)
        put(datt.at[at], d_attn.at[at])
    put(datt.at[pl.ds(0, reach)], d_low)
    put(datt.at[pl.ds(tokens - reach, reach)], d_high)
    for r in range(0, width, width // 2):
        gout[r : r + width // 2, :] = mm_tn(attb[:, r : r + width // 2], branch[...]).astype(bf16)
    size = width // PARTS // 2
    waits = []
    for part in range(PARTS):
        source = lambda n, part=part: gout.at[pl.ds((2 * part + n) * size, size)]
        waits.append(piece_copies(part, place, source, hsems.at[part], send, keep, stride, stride - size))
    for i in range(6):
        line[i : i + 1, :] = sums[i]
    small[...] = line[...].astype(bf16)
    for to in (send, keep):
        put(small, to.at[pl.ds(PARTS * stride, SMALL)])
    for c in copies:
        c.wait()
    for wait in waits:
        wait()


def layer(place, spans, se, xl, xr, q, k, v, x, wk, wv, wo, wu, wd, dy, bv, bo, g1, s1, bu, bd, g2, s2):
    tokens, width = x.shape
    ff = wu.shape[1]
    reach = xl.shape[0]
    ext = tokens + 2 * reach
    shape = lambda n, t, rows=tokens: jax.ShapeDtypeStruct((rows, n), t)
    vm = lambda rows, n, t: pltpu.VMEM((rows, n), t)
    group = group_scratch(ff, width, 4)
    return call(
        layer_kernel,
        out_shape=(
            shape(ff, bf16),
            shape(width, bf16),
            shape(width, bf16, 2 * reach),
            shape(width, bf16, 2 * reach),
            shape(width, bf16),
            shape(width, f32),
            shape(width, bf16),
            shape(width, bf16, reach),
            shape(width, bf16, reach),
        )
        + group_shapes((ff + width) // PARTS // 2, width, SMALL),
        in_specs=[SMEM, SMEM, KEPT] + [VMEM] * 8 + [FREE, FREE] + [KEPT] * 6 + [HBM] * 4,
        out_specs=(KEPT, KEPT) + (HBM,) * 9,
        scratch_shapes=[
            vm(width, width, bf16),
            vm(width, ff, bf16),
            vm(ff, width, bf16),
            vm(tokens, width, bf16),
            pltpu.SemaphoreType.DMA((4,)),
            vm(ext, width, bf16),
            vm(ext, width, bf16),
            vm(tokens, width, bf16),
            vm(tokens, ff, bf16),
            vm(tokens, width, f32),
            vm(tokens, 128, f32),
            vm(tokens, width, f32),
            vm(tokens, width, bf16),
            vm(tokens, width, bf16),
            vm(tokens, width, bf16),
            vm(tokens, width, bf16),
            vm(width, width, bf16),
            vm(SMALL, width, f32),
            vm(SMALL, width, bf16),
            group[0],
            pltpu.SemaphoreType.DMA((10 + len(row_blocks(tokens)),)),
            group[1],
            pltpu.SemaphoreType.DMA((PARTS, 2)),
        ],
        compiler_params=params(46),
        cost_estimate=cost(4 * tokens * width * (width + 3 * ff) + 8e9, 40 * tokens * width, 2 * tokens * ff),
        name="layer",
    )(place, spans, se, bv, bo, g1, s1, bu, bd, g2, s2, xl, xr, q, k, v, x, wk, wv, wo, wu, wd, dy)


def up_grad_kernel(place, mid_low, d_up, send, keep, buf, gsems):
    width = mid_low.shape[1]
    size = width // 2

    def block(part):
        rows, cols = (part % 2) * size, (part // 2) * width
        return mm_tn(mid_low[:, rows : rows + size], d_up[:, cols : cols + width])

    write_group(block, send, keep, buf, gsems, place, size // 2)


def up_grad(place, mid_low, d_up, after=()):
    tokens, width = mid_low.shape
    ff = d_up.shape[1]
    return call(
        up_grad_kernel,
        out_shape=group_shapes(width // 4, width),
        in_specs=[SMEM, KEPT, KEPT],
        out_specs=(HBM, HBM),
        scratch_shapes=group_scratch(ff, width),
        after=after,
        compiler_params=params(12),
        cost_estimate=cost(2 * tokens * width * ff, 14 * tokens * width),
        name="up_grad",
    )(place, mid_low, d_up)


def rest_grad_kernel(halves, place, x, *refs):
    parts, (send, keep, xb, rhs, grad, small, gsems, sems, ssems) = refs[: 3 * halves], refs[3 * halves :]
    tokens, width = x.shape
    size = width // 2
    some = width // halves
    pairs = [(x, xb)]
    for n in range(3):
        for h in range(halves):
            pairs.append((parts[3 * h + n], rhs.at[n, :, pl.ds(h * some, some)]))
    ready = loads(pairs, sems)
    ready(0)
    stride = 3 * width // PARTS // 2
    waits = []
    for done in range(0, 3 * width, size):
        which = done // width
        if done % width == 0:
            for h in range(halves):
                ready(1 + which * halves + h)
        at = done % width
        grad[done : done + size, :] = mm_tn(xb[:, at : at + size], rhs[which]).astype(bf16)
        while 2 * stride * (len(waits) + 1) <= done + size:
            part = len(waits)
            source = lambda n, part=part: grad.at[pl.ds((2 * part + n) * stride, stride)]
            waits.append(piece_copies(part, place, source, gsems.at[part], send, keep, stride))
    ones = jnp.ones((8, tokens), bf16)
    row = lax.broadcasted_iota(i32, (8, width), 0)
    sums = jnp.where(row == 0, mm(ones, rhs[0]), jnp.where(row == 1, mm(ones, rhs[2]), 0.0))
    small[...] = jnp.concatenate([sums, jnp.zeros((SMALL - 8, width), f32)], axis=0).astype(bf16)
    end = pl.ds(PARTS * stride, SMALL)
    copies = [out_copy(small, o.at[end], ssems.at[i]) for i, o in enumerate((send, keep))]
    for c in copies:
        c.wait()
    for wait in waits:
        wait()


def rest_grad(place, x, parts, after=()):
    tokens, width = x.shape
    halves = len(parts)
    return call(
        functools.partial(rest_grad_kernel, halves),
        out_shape=group_shapes(3 * width // PARTS // 2, width, SMALL),
        in_specs=[SMEM] + [HBM] * (1 + 3 * halves),
        out_specs=(HBM, HBM),
        scratch_shapes=[
            pltpu.VMEM((tokens, width), bf16),
            pltpu.VMEM((3, tokens, width), bf16),
            pltpu.VMEM((3 * width, width), bf16),
            pltpu.VMEM((SMALL, width), bf16),
            pltpu.SemaphoreType.DMA((PARTS, 2)),
            pltpu.SemaphoreType.DMA((1 + 3 * halves,)),
            pltpu.SemaphoreType.DMA((2,)),
        ],
        after=after,
        compiler_params=params(20),
        cost_estimate=cost(6 * tokens * width * width, 20 * tokens * width),
        name="rest_grad",
    )(place, x, *sum(map(tuple, parts), ()))


def inputs_grad_kernel(halves, d_one, *refs):
    parts, (wq, wk, wv, out) = refs[: 3 * halves], refs[3 * halves :]
    total = d_one[...]
    some = wq.shape[1] // halves
    for h in range(halves):
        for g, w in zip(parts[3 * h : 3 * h + 3], (wq, wk, wv)):
            total = total + mm_nt(g[...], w[:, h * some : (h + 1) * some])
    out[...] = total


def inputs_grad(d_one, parts, wq, wk, wv, after=()):
    tokens, width = d_one.shape
    halves = len(parts)
    tok = lambda n: pl.BlockSpec((ROWS, n), lambda i: (i, 0))
    full = pl.BlockSpec((width, width), lambda i: (0, 0))
    return call(
        functools.partial(inputs_grad_kernel, halves),
        grid=(tokens // ROWS,),
        out_shape=(jax.ShapeDtypeStruct((tokens, width), f32),),
        in_specs=[tok(width)] + [tok(width // halves)] * (3 * halves) + [full] * 3,
        out_specs=(tok(width),),
        anywhere=True,
        after=after,
        compiler_params=params(16, dimension_semantics=("arbitrary",)),
        cost_estimate=cost(6 * tokens * width * width, 20 * tokens * width),
        name="inputs_grad",
    )(d_one, *sum(map(tuple, parts), ()), wq, wk, wv)


def swap(value, axis, bit):
    count = lax.axis_size(axis)
    return lax.ppermute(value, axis, [(i, i ^ bit) for i in range(count)])


def plus(a, b):
    return (a.astype(f32) + b.astype(f32)).astype(bf16)


def layer_bits():
    return list(range(1, lax.axis_size("dp")))


def far_bits():
    bit, bits = PARTS, []
    while bit < lax.axis_size("seq"):
        bits.append(bit)
        bit *= 2
    return bits


def axis_bits(axis):
    return [1 << n for n in range((lax.axis_size(axis) - 1).bit_length())]


class Sum:
    def __init__(self, send, keep, tail=0):
        self.mine, self.got, self.payload, self.tail = [keep], [], [send], tail
        self.swaps = [("seq", 1)]
        self.steps = self.run()

    def receive(self, token):
        if self.got:
            *self.got, _ = lax.optimization_barrier((*self.got, token))
            next(self.steps)

    def send(self):
        self.got = [swap(p, *s) for p, s in zip(self.payload, self.swaps)]

    def tailed(self, payloads):
        rows = [p.reshape(-1, p.shape[-1]) for p in payloads]
        if self.tail:
            rows[0] = jnp.concatenate([rows[0], self.small], axis=0)
        return rows

    def untailed(self, like):
        if self.tail:
            self.small = plus(self.small, self.got[0][-self.tail :])
            self.got[0] = self.got[0][: -self.tail]
        return [g.reshape(m.shape) for g, m in zip(self.got, like)]

    def run(self):
        keep, got = self.mine[0], self.got[0]
        width = keep.shape[-1]
        if self.tail:
            self.small = plus(keep[-self.tail :], got[-self.tail :])
            keep, got = keep[: -self.tail], got[: -self.tail]
        keep, got = (v.reshape((2, 2, 2, -1, width)) for v in (keep, got))
        keeps, gots = [keep[0], keep[1]], [got[0], got[1]]
        for bits in ((2, 4), (4, 2)):
            away = [plus(k[1], g[1]) for k, g in zip(keeps, gots)]
            keeps = [plus(k[0], g[0]) for k, g in zip(keeps, gots)]
            self.payload, self.swaps = self.tailed(away), [("seq", b) for b in bits]
            yield
            gots = self.untailed(keeps)
        parts = list(map(plus, keeps, gots))
        layers = axis_bits("dp")
        layer = lax.axis_index("dp")
        rows = parts[0].shape[0]
        part = jnp.stack(parts).reshape((2,) * len(layers) + (-1, width))
        for bit in layers:
            mine = (layer // bit) % 2
            keep = lax.dynamic_index_in_dim(part, mine, 0, keepdims=False)
            away = lax.dynamic_index_in_dim(part, 1 - mine, 0, keepdims=False)
            self.payload, self.swaps = self.tailed([away]), [("dp", bit)]
            yield
            part = plus(keep, self.untailed([keep])[0])
        for bit in far_bits():
            part = plus(part, swap(part, "seq", bit))
            if self.tail:
                self.small = plus(self.small, swap(self.small, "seq", bit))
        for bit in reversed(layers):
            self.payload, self.swaps = [part], [("dp", bit)]
            yield
            low = (layer // bit) % 2 == 0
            got = self.got[0]
            part = jnp.stack([jnp.where(low, part, got), jnp.where(low, got, part)])
        parts = list(part.reshape(2, rows, width))
        for bits in ((4, 2), (2, 4)):
            self.payload, self.swaps = parts, [("seq", b) for b in bits]
            yield
            parts = [jnp.stack(pair) for pair in zip(parts, self.got)]
        whole = jnp.stack(parts).reshape(8, -1, width)
        self.payload, self.swaps = [whole], [("seq", 1)]
        yield
        self.result = (whole, self.got[0])
        self.payload = []
        yield


def advance(token, *sums):
    for s in sums:
        s.receive(token)
    payloads = lax.optimization_barrier(tuple(p for s in sums for p in s.payload))
    at = 0
    for s in sums:
        s.payload = list(payloads[at : at + len(s.payload)])
        at += len(s.payload)
        s.send()
    return payloads[0] if payloads else token


def spread_kernel(kind, count, place, mine, other, *refs):
    outs, (buf, sems) = refs[:count], refs[count:]
    here = place[1]
    rows, width = mine.shape[1:]
    slots = buf.shape[0]
    waits = []
    for n in range(2 * PARTS):
        part, piece = n // 2, n % 2
        slot = n % slots
        if n >= slots:
            for c in waits[n - slots]:
                c.wait()
        to = part ^ here
        core, x, y = to & 1, (to >> 1) & 1, (to >> 2) & 1
        at = 4 + 2 * y + x if piece else 2 * x + y
        for side, source in ((0, mine), (1, other)):

            @pl.when(core == side)
            def _(source=source, slot=slot, at=at):
                buf[slot] = source[at].astype(f32)

        pairs = []
        if kind == "up":
            down = (part % 2) * 2 * rows + piece * rows
            pairs.append((0, rows, outs[0].at[pl.ds(down, rows), pl.ds((part // 2) * width, width)]))
        elif kind == "down":
            few = width // PARTS // 2
            pairs.append((0, rows - few, outs[0].at[pl.ds(n * (rows - few), rows - few)]))
            pairs.append((rows - few, few, outs[1].at[pl.ds(n * few, few)]))
        else:
            first, last = n * rows, (n + 1) * rows
            while first < last:
                which = first // width
                size = min(last, (which + 1) * width) - first
                pairs.append((first - n * rows, size, outs[which].at[pl.ds(first - which * width, size)]))
                first += size
        waits.append([out_copy(buf.at[slot, pl.ds(a, s)], o, sems.at[slot, i]) for i, (a, s, o) in enumerate(pairs)])
    for wait in waits[-slots:]:
        for c in wait:
            c.wait()


def spread(kind, place, mine, other, after=()):
    rows, width = mine.shape[1:]
    shapes = {
        "down": [(2 * PARTS * rows - width, width), (width, width)],
        "up": [(width, 2 * PARTS * rows)],
        "rest": [(width, width)] * 3,
    }[kind]
    slots = 6
    return call(
        functools.partial(spread_kernel, kind, len(shapes)),
        out_shape=[jax.ShapeDtypeStruct(s, f32) for s in shapes],
        in_specs=[SMEM, FREE, FREE],
        out_specs=[HBM] * len(shapes),
        after=after,
        scratch_shapes=[pltpu.VMEM((slots, rows, width), f32), pltpu.SemaphoreType.DMA((slots, 2))],
        compiler_params=params(8),
        cost_estimate=cost(rows * width, 12 * PARTS * rows * width),
        name="spread_" + kind,
    )(place, mine, other)


def sum_small(vec):
    for axis in ("seq", "dp"):
        bit = 1
        while bit < lax.axis_size(axis):
            vec = vec + swap(vec, axis, bit)
            bit *= 2
    return vec


def neighbours(first, last):
    count = lax.axis_size("seq")
    up = [(i, i + 1) for i in range(count - 1)]
    low = lax.ppermute(last, "seq", up)
    high = lax.ppermute(first, "seq", [(b, a) for a, b in up])
    return low, high


def body(
    inputs, lengths, w_query, b_query, w_key, w_value, b_value, w_out, b_out, gain_one, shift_one,
    w_up, b_up, w_down, b_down, gain_two, shift_two, d_output,
):
    rows, tokens, width = inputs.shape
    reach = ITEM_MOST
    here = lax.axis_index("seq")
    place = jnp.stack([here * tokens, here & (PARTS - 1), lax.axis_index("dp")]).astype(i32)
    x = inputs.reshape(tokens, width)
    dy = d_output.reshape(tokens, width)

    xl, xr = neighbours(x[:reach], x[-reach:])
    se, spans, se_low, spans_low, q, k, v, *kept = front(
        place, lengths, x, w_query, w_key, w_value, b_query, b_value, reach
    )
    d_up, mid_low, kh, vh, output, d_one, d_attn, d_low, d_high, send1, keep1 = layer(
        place, spans, se, xl, xr, *kept, w_out, w_up, w_down, dy, b_value, b_out, gain_one, shift_one, b_up, b_down, gain_two, shift_two
    )
    one = Sum(send1, keep1, SMALL)
    token = advance(d_attn, one)
    dl, dr = neighbours(d_low, d_high)
    send2, keep2 = up_grad(place, mid_low, d_up, after=[token])
    dl, dr, send2 = lax.optimization_barrier((dl, dr, send2))
    two = Sum(send2, keep2)
    token = advance(send2, one, two)
    args = (HALVES, spans_low, se_low, q, k, v, d_attn, kh, vh, xl, xr, dl, dr, w_query, b_query)
    parts = [attend_back(0, *args, after=[token])]
    token = advance(parts[0][0], one, two)
    parts.append(attend_back(1, *args, after=[token]))
    token = advance(parts[1][0], one)
    send3, keep3 = rest_grad(place, x, parts, after=[token])
    three = Sum(send3, keep3, SMALL)
    token = advance(send3, one, two, three)
    sums = {1: one, 2: two, 3: three}
    for event in ORDER:
        if event == 0:
            (d_inputs,) = inputs_grad(d_one, parts, w_query, w_key, w_value, after=[token])
            token = d_inputs
        elif event < 0:
            kind = ("down", "up", "rest")[-event - 1]
            grads = spread(kind, place, *sums[-event].result, after=[token])
            token = grads[0]
            if kind == "down":
                g_w_down, g_w_out = grads
            elif kind == "up":
                (g_w_up,) = grads
            else:
                g_w_query, g_w_key, g_w_value = grads
        else:
            token = advance(token, *[sums[int(g)] for g in str(event)])
    small = jnp.concatenate([one.small, three.small], axis=0).astype(f32)
    ff = w_up.shape[1]
    many = ff // width
    return (
        output.reshape(rows, tokens, width),
        d_inputs.reshape(rows, tokens, width),
        g_w_query,
        small[SMALL],
        g_w_key,
        g_w_value,
        small[SMALL + 1],
        g_w_out,
        small[5],
        small[3],
        small[4],
        g_w_up,
        small[8 : 8 + many].reshape(ff),
        g_w_down,
        small[0],
        small[1],
        small[2],
    )


def solution(mesh):
    split, whole = P("dp", "seq", None), P()
    return jax.shard_map(
        body,
        mesh=mesh,
        in_specs=(split, P("dp", None)) + (whole,) * 15 + (split,),
        out_specs=(split, split) + (whole,) * 15,
        check_vma=False,
    )
```

```python
import functools

import jax
import jax.numpy as jnp
from jax import lax
from jax.experimental import pallas as pl
from jax.experimental.pallas import tpu as pltpu
from jax.sharding import PartitionSpec as P

HEADS = 12
HEAD_DIM = 64
ITEM_MOST = 256
EPS = 1e-12
SCALE = 0.125
MASKED = -1e30
FAR = 1e9
TILE = 128
PAIR = 2 * HEAD_DIM
WIDTHS = (192, 256, 384, 640)
ROWS = 256
SMALL = 16
ORDER = (3, 2, 1, 3, 2, 1, 3, 2, 1, 3, 2, 1, 23, 1, 3, 2, 3, 1, -1, 23, 0, 2, -2, 3, 3, -3)
HALVES = 2
PARTS = 8
CHUNK = 512

bf16 = jnp.bfloat16
f32 = jnp.float32
i32 = jnp.int32
ANY = pl.BlockSpec(memory_space=pl.ANY)
HBM = pl.BlockSpec(memory_space=pltpu.HBM)
KEPT = pl.BlockSpec(memory_space=pltpu.VMEM)
FREE = pl.BlockSpec(memory_space=pltpu.VMEM)
NEAR = pl.BlockSpec(memory_space=pltpu.VMEM)
SMEM = pl.BlockSpec(memory_space=pltpu.SMEM)
VMEM = pl.BlockSpec(memory_space=pltpu.VMEM)


def params(mib, **kw):
    return pltpu.CompilerParams(vmem_limit_bytes=mib * 1024 * 1024, **kw)


def cost(flops, nbytes, trans=0):
    return pl.CostEstimate(flops=int(flops), bytes_accessed=int(nbytes), transcendentals=int(trans))


def mm(a, b):
    return lax.dot_general(a, b, (((1,), (0,)), ((), ())), preferred_element_type=f32)


def mm_nt(a, b):
    return lax.dot_general(a, b, (((1,), (1,)), ((), ())), preferred_element_type=f32)


def mm_tn(a, b):
    return lax.dot_general(a, b, (((0,), (0,)), ((), ())), preferred_element_type=f32)


def large(a):
    return a.size * a.dtype.itemsize > 512 * 1024


def call(kernel, out_shape, in_specs, out_specs, after=(), anywhere=False, **kw):
    kept = lambda a, spec: pltpu.VMEM if spec is KEPT else pltpu.HBM if spec is HBM or spec is NEAR or (large(a) and spec is not FREE and spec is not ANY and not anywhere) else None
    shapes = [k(o.shape, o.dtype) if (k := kept(o, spec)) else o for o, spec in zip(out_shape, out_specs)]
    count = len(in_specs)

    def plain(*refs):
        return kernel(*refs[:count], *refs[count + len(after) :])

    specs = list(in_specs) + [ANY] * len(after)
    run = pl.pallas_call(plain, out_shape=shapes, in_specs=specs, out_specs=list(out_specs), **kw)

    def apply(*args):
        args = [
            pltpu.with_memory_space_constraint(a, k) if (k := kept(a, spec)) else a
            for a, spec in zip(args, in_specs)
        ]
        return run(*args, *[pltpu.with_memory_space_constraint(a, pltpu.HBM) if a.dtype == f32 else a for a in after])

    return apply


def loads(pairs, sems):
    copies = [pltpu.make_async_copy(a, b, sems.at[i]) for i, (a, b) in enumerate(pairs)]
    for c in copies:
        c.start()
    return lambda i: copies[i].wait()


def out_copy(source, target, sem):
    c = pltpu.make_async_copy(source, target, sem)
    c.start()
    return c


def row_blocks(tokens):
    return [slice(r, r + ROWS) for r in range(0, tokens, ROWS)]


def front_kernel(
    place, lengths, bq, bv, x, wq, wk, wv,
    se, spans, se_low, spans_low, q, k, v, qv, kv, vv, xv, wkv, wvv, wqb, sems, osems,
):
    ready = loads([(x, xv), (wq, wqb), (wk, wkv), (wv, wvv)], sems)
    slots = lengths.shape[1]
    tokens = x.shape[0]
    ext = se.shape[1]
    reach = (ext - tokens) // 2
    step = max(d for d in range(8, 129, 8) if slots % d == 0)
    start = place[0] - reach
    pos = (lax.broadcasted_iota(i32, (1, ext), 1) + start).astype(f32)
    sizes = lengths[...].astype(f32)

    def scan(c, state):
        low, high = state
        index = lax.broadcasted_iota(i32, (step, slots), 0) + c * step
        upto = lax.broadcasted_iota(i32, (step, slots), 1) <= index
        ends = jnp.sum(jnp.where(upto, sizes, 0.0), axis=1, keepdims=True)
        before = ends <= pos
        low = jnp.maximum(low, jnp.max(jnp.where(before, ends, 0.0), axis=0, keepdims=True))
        high = jnp.minimum(high, jnp.min(jnp.where(before, FAR, ends), axis=0, keepdims=True))
        return low, high

    low, high = lax.fori_loop(
        0, slots // step, scan, (jnp.zeros((1, ext), f32), jnp.full((1, ext), FAR, f32))
    )
    real = (pos >= 0.0) & (high < FAR)
    local = lax.broadcasted_iota(i32, (1, ext), 1).astype(f32)
    offset = start.astype(f32)
    own = (local >= reach) & (local < reach + tokens)
    low_e = jnp.where(real, low - offset, local)
    high_e = jnp.where(real, high - offset, local + 1.0)
    shared = real & (
        ((local < reach) & (high_e > reach)) | ((local >= reach + tokens) & (low_e < reach + tokens))
    )
    used = own | shared
    low_e = jnp.where(used, low_e, 0.0)
    high_e = jnp.where(used, high_e, 0.0)
    se[0:1, :] = low_e
    se[1:2, :] = high_e
    se[2:8, :] = jnp.zeros((6, ext), f32)
    se_copy = out_copy(se, se_low, osems.at[3])

    def note(i, value):
        spans[i] = value
        spans_low[i] = value

    note(0, jnp.sum(sizes).astype(i32))
    for t in range(ext // TILE):
        sl = slice(t * TILE, (t + 1) * TILE)
        some = high_e[:, sl] > low_e[:, sl]
        first = jnp.min(jnp.where(some, low_e[:, sl], FAR)).astype(i32)
        last = jnp.max(jnp.where(some, high_e[:, sl], -1.0)).astype(i32)
        at = first & ~15
        span = last - at
        kind = len(WIDTHS)
        begin = min(max(t * TILE - reach, 0), ext - WIDTHS[-1])
        for i in reversed(range(len(WIDTHS) - 1)):
            kind = jnp.where(span <= WIDTHS[i], i + 1, kind)
            begin = jnp.where(span <= WIDTHS[i], jnp.minimum(at, ext - WIDTHS[i]), begin)
        note(8 + 2 * t, jnp.where(last < 0, 0, kind))
        note(9 + 2 * t, begin)

    copies = [se_copy]
    ready(0)
    for i, (w, b, out, to) in enumerate(((wqb, bq, qv, q), (wkv, None, kv, k), (wvv, bv, vv, v))):
        ready(i + 1)
        for r in row_blocks(tokens):
            y = mm(xv[r, :], w[...])
            if b is not None:
                y = y + b[...]
            y = y.astype(bf16)
            out[r, :] = y * bf16(SCALE) if i == 0 else y
        copies.append(out_copy(out, to, osems.at[i]))
    for c in copies:
        c.wait()


def front(place, lengths, x, wq, wk, wv, bq, bv, reach):
    tokens, width = x.shape
    ext = tokens + 2 * reach
    like = lambda a: jax.ShapeDtypeStruct(a.shape, a.dtype)
    kept = [like(a) for a in (x, x, x, x, wk, wv)]
    return call(
        front_kernel,
        out_shape=(
            *[
                jax.ShapeDtypeStruct((8, ext), f32),
                jax.ShapeDtypeStruct((8 + 2 * (ext // TILE),), i32),
            ]
            * 2,
            like(x),
            like(x),
            like(x),
            *kept,
        ),
        in_specs=[SMEM, NEAR, NEAR, NEAR] + [HBM] * 4,
        out_specs=(KEPT, SMEM, HBM, SMEM, HBM, HBM, HBM) + (KEPT,) * len(kept),
        scratch_shapes=[
            pltpu.VMEM((width, width), bf16),
            pltpu.SemaphoreType.DMA((4,)),
            pltpu.SemaphoreType.DMA((4,)),
        ],
        compiler_params=params(8),
        cost_estimate=cost(6 * tokens * width * width, 8 * tokens * width),
        name="front",
    )(place, lengths, bq, bv, x, wq, wk, wv)


def tile_bias(se, t, at, width):
    base = pl.multiple_of(t * TILE, TILE)
    low = se[0:1, pl.ds(base, TILE)]
    high = se[1:2, pl.ds(base, TILE)]
    key = (lax.broadcasted_iota(i32, (width, TILE), 0) + at).astype(f32)
    one = jnp.where((key >= low) & (key < high), 0.0, MASKED)
    some = jnp.where(high > low, 1.0, 0.0)
    return jnp.concatenate([one, one], axis=1), jnp.concatenate([some, some], axis=1)


def stacked(pair):
    lane = lax.broadcasted_iota(i32, pair.shape, 1)
    zero = jnp.zeros_like(pair)
    return jnp.concatenate(
        [jnp.where(lane < HEAD_DIM, pair, zero), jnp.where(lane < HEAD_DIM, zero, pair)], axis=0
    )


def unstacked(both):
    own = jnp.concatenate([both[:HEAD_DIM, :TILE], both[HEAD_DIM:, TILE:]], axis=0)
    return own.T


def each_tile(spans, first, last, tile):
    def each(t, _):
        kind, at = spans[8 + 2 * t], spans[9 + 2 * t]
        for i, span in enumerate(WIDTHS):
            pl.when(kind == i + 1)(functools.partial(tile, t, at, span))
        return 0

    lax.fori_loop(first, last, each, 0)


def attend_tile(se, q, kx, vx, attn, reach, t, at, span):
    width = q.shape[1]
    bias, _ = tile_bias(se, t, at, span)
    rows = pl.ds(pl.multiple_of(t * TILE - reach, TILE), TILE)
    window = pl.ds(pl.multiple_of(at, 16), span)
    pairs = [slice(p, p + PAIR) for p in range(0, width, PAIR)]
    scores = [mm_nt(kx[window, c], stacked(q[rows, c])) for c in pairs]
    soft = []
    for s in scores:
        s = s + bias
        weights = jnp.exp(s - jnp.max(s, axis=0, keepdims=True))
        soft.append((weights.astype(bf16), jnp.sum(weights, axis=0, keepdims=True)))
    for c, (weights, total) in zip(pairs, soft):
        attn[rows, c] = unstacked(mm_tn(vx[window, c], weights) / total).astype(bf16)


def attend_back_tile(se, qx, kx, vx, dox, dkx, dvx, t, at, span):
    width = qx.shape[1]
    bias, some = tile_bias(se, t, at, span)
    rows = pl.ds(pl.multiple_of(t * TILE, TILE), TILE)
    window = pl.ds(pl.multiple_of(at, 16), span)
    pairs = [slice(p, p + PAIR) for p in range(0, width, PAIR)]
    first = []
    for c in pairs:
        query, dout = stacked(qx[rows, c]), stacked(dox[rows, c])
        first.append((query, dout, mm_nt(kx[window, c], query), mm_nt(vx[window, c], dout)))
    second = []
    for query, dout, scores, dprob in first:
        scores = scores + bias
        weights = jnp.exp(scores - jnp.max(scores, axis=0, keepdims=True))
        probs = weights * (some / jnp.sum(weights, axis=0, keepdims=True))
        delta = jnp.sum(probs * dprob, axis=0, keepdims=True)
        second.append((probs.astype(bf16), (probs * (dprob - delta)).astype(bf16)))
    for c, (query, dout, _, _), (probs, dscore) in zip(pairs, first, second):
        dvx[window, c] += mm(probs, dout)
        dkx[window, c] += mm(dscore, query)
        qx[rows, c] = (unstacked(mm_tn(kx[window, c], dscore)) * SCALE).astype(bf16)


def attend_back_kernel(
    half, spans, se, bq, q, k, v, do, kh, vh, xl, xr, dl, dr, wq,
    dq, dk, dv, qx, kx, vx, dox, dkx, dvx, dkb, dvb, wb, xb, sems, osems,
):
    tokens = q.shape[0]
    reach = xl.shape[0]
    ext, some = kx.shape
    cols = pl.ds(half * some, some)
    own, low, high = pl.ds(reach, tokens), pl.ds(0, reach), pl.ds(reach + tokens, reach)
    ready = loads(
        [
            (wq.at[:, cols], wb),
            (xl, xb.at[low]),
            (xr, xb.at[pl.ds(reach, reach)]),
            (q.at[:, cols], qx.at[own]),
            (k.at[:, cols], kx.at[own]),
            (v.at[:, cols], vx.at[own]),
            (do.at[:, cols], dox.at[own]),
            (kh.at[pl.ds(0, reach), cols], kx.at[low]),
            (kh.at[pl.ds(reach, reach), cols], kx.at[high]),
            (vh.at[pl.ds(0, reach), cols], vx.at[low]),
            (vh.at[pl.ds(reach, reach), cols], vx.at[high]),
            (dl.at[:, cols], dox.at[low]),
            (dr.at[:, cols], dox.at[high]),
        ],
        sems,
    )
    dkx[...] = jnp.zeros_like(dkx)
    dvx[...] = jnp.zeros_like(dvx)
    for i in range(3):
        ready(i)
    bias = bq[...][half * some : (half + 1) * some]
    for at, to in ((0, 0), (reach, reach + tokens)):
        y = (mm(xb[at : at + reach, :], wb[...]) + bias).astype(bf16)
        qx[to : to + reach, :] = y * bf16(SCALE)
    for i in range(3, 13):
        ready(i)
    tile = functools.partial(attend_back_tile, se, qx, kx, vx, dox, dkx, dvx)
    each_tile(spans, 0, ext // TILE, tile)
    copies = [out_copy(qx.at[own], dq, osems.at[0])]
    dkb[...] = dkx[reach : reach + tokens, :].astype(bf16)
    copies.append(out_copy(dkb, dk, osems.at[1]))
    dvb[...] = dvx[reach : reach + tokens, :].astype(bf16)
    copies.append(out_copy(dvb, dv, osems.at[2]))
    for c in copies:
        c.wait()


def attend_back(half, halves, spans, se, q, k, v, do, kh, vh, xl, xr, dl, dr, wq, bq, after=()):
    tokens, width = q.shape
    reach = xl.shape[0]
    ext = tokens + 2 * reach
    some = width // halves
    out = jax.ShapeDtypeStruct((tokens, some), bf16)
    return call(
        functools.partial(attend_back_kernel, half),
        out_shape=(out, out, out),
        in_specs=[SMEM, NEAR, VMEM] + [HBM] * 11,
        out_specs=(HBM, HBM, HBM),
        scratch_shapes=[pltpu.VMEM((ext, some), bf16)] * 4
        + [pltpu.VMEM((ext, some), f32)] * 2
        + [pltpu.VMEM((tokens, some), bf16)] * 2
        + [pltpu.VMEM((width, some), bf16), pltpu.VMEM((2 * reach, width), bf16)]
        + [pltpu.SemaphoreType.DMA((13,)), pltpu.SemaphoreType.DMA((3,))],
        after=after,
        compiler_params=params(20),
        cost_estimate=cost(16e9 / halves, 20 * tokens * some),
        name="attend_back_%d" % half,
    )(spans, se, bq, q, k, v, do, kh, vh, xl, xr, dl, dr, wq)


def piece_copies(part, place, source, sem, send, keep, stride, offset=0):
    to = part ^ place[1]
    core, x, y = to & 1, (to >> 1) & 1, (to >> 2) & 1
    rows = source(0).shape[0]

    def copies(out):
        return [
            pltpu.make_async_copy(
                source(n), out.at[pl.ds(pl.multiple_of(at * stride + offset, 16), rows)], sem.at[n]
            )
            for n, at in enumerate((2 * x + y, 4 + 2 * y + x))
        ]

    for here, out in ((1, send), (0, keep)):

        @pl.when(core == here)
        def _(out=out):
            for c in copies(out):
                c.start()

    def wait():
        for c in copies(keep):
            c.wait()

    return wait


def write_group(block, send, keep, buf, sems, place, stride):
    slots, rows = buf.shape[:2]
    half = rows // 2
    waits = []
    for part in range(PARTS):
        slot = part % slots
        value = block(part).astype(bf16)
        if part >= slots:
            waits[part - slots]()
        buf[slot] = value
        source = lambda n, slot=slot: buf.at[slot, pl.ds(n * half, half)]
        waits.append(piece_copies(part, place, source, sems.at[slot], send, keep, stride))
    for wait in waits[-slots:]:
        wait()


def group_shapes(stride, width, tail=0):
    return (jax.ShapeDtypeStruct((PARTS * stride + tail, width), bf16),) * 2


def group_scratch(rows, width, slots=PARTS):
    return [pltpu.VMEM((slots, rows // PARTS, width), bf16), pltpu.SemaphoreType.DMA((slots, 2))]


def gelu_both(z):
    u = jnp.abs(z) * 0.7071067811865476
    t = 1.0 / (1.0 + 0.3275911 * u)
    bell = jnp.exp2(z * (z * -0.7213475204444817))
    poly = t * (
        0.5 * 0.254829592
        + t * (0.5 * -0.284496736 + t * (0.5 * 1.421413741 + t * (0.5 * -1.453152027 + t * (0.5 * 1.061405429))))
    )
    tail = poly * bell
    cdf = jnp.where(z >= 0.0, 1.0 - tail, tail)
    return z * cdf, cdf + z * bell * 0.3989422804014327


def center(v):
    mean = jnp.mean(v, axis=1, keepdims=True)
    c = v - mean
    rstd = lax.rsqrt(jnp.mean(c * c, axis=1, keepdims=True) + EPS)
    return c * rstd, rstd


def center_back(e, xhat, rstd):
    return rstd * (
        e - jnp.mean(e, axis=1, keepdims=True) - xhat * jnp.mean(e * xhat, axis=1, keepdims=True)
    )


def colsum(v):
    return jnp.sum(v, axis=0, keepdims=True)


def layer_kernel(
    place, spans, se, bv, bo, g1, s1, bu, bd, g2, s2, xl, xr, q, k, v, x, wk, wv, wo_h, wu_h, wd_h, dy_h,
    d_up, mid_low, kh, vh, out, d_one, d_attn, d_low, d_high, send, keep,
    wo, wu, wd, dy, lsems, kx, vx, attb, act, xh, rstd, two, ob, dd, branch, datt, gout, line, small, buf, osems, gsems, hsems,
):
    tokens, width = x.shape
    ff = wu.shape[1]
    reach = xl.shape[0]
    own = slice(reach, reach + tokens)
    blocks = row_blocks(tokens)
    ready = loads([(wo_h, wo), (wu_h, wu), (wd_h, wd), (dy_h, dy)], lsems)
    copies = []

    def put(source, target):
        copies.append(out_copy(source, target, osems.at[len(copies)]))

    line[...] = jnp.zeros_like(line)
    kx[own, :] = k[...]
    vx[own, :] = v[...]
    for part, at in ((xl, 0), (xr, reach + tokens)):
        kx[at : at + reach, :] = mm(part[...], wk[...]).astype(bf16)
        vx[at : at + reach, :] = (mm(part[...], wv[...]) + bv[...]).astype(bf16)
    for n, at in enumerate((0, reach + tokens)):
        for ref, to in ((kx, kh), (vx, vh)):
            put(ref.at[pl.ds(at, reach)], to.at[pl.ds(n * reach, reach)])
    tile = functools.partial(attend_tile, se, q, kx, vx, attb, reach)
    each_tile(spans, reach // TILE, (reach + tokens) // TILE, tile)
    ready(0)
    for r, b in zip(blocks, [mm(attb[r, :], wo[...]) for r in blocks]):
        hat, rs = center(x[r, :].astype(f32) + b + bo[...])
        mid = hat * g1[...] + s1[...]
        xh[r, :] = hat
        rstd[r, :] = jnp.broadcast_to(rs, (ROWS, rstd.shape[1]))
        mid_low[r, :] = mid.astype(bf16)
        two[r, :] = mid + bd[...]

    ready(1)
    ready(2)

    def ups(c):
        return [mm(mid_low[r, :], wu[:, c : c + CHUNK]) for r in blocks]

    up = ups(0)
    for c in range(0, ff, CHUNK):
        cols = slice(c, c + CHUNK)
        now = up
        if c + CHUNK < ff:
            up = ups(c + CHUNK)
        for r, z in zip(blocks, now):
            a, s = gelu_both(z + bu[...][cols])
            act[r, cols] = a.astype(bf16)
            d_up[r, cols] = s.astype(bf16)
        for r in blocks:
            two[r, :] += mm(act[r, cols], wd[cols, :])

    ready(3)
    sums = [0.0] * 6
    for r in blocks:
        hat, rs = center(two[r, :])
        token = place[0] + r.start + lax.broadcasted_iota(i32, (ROWS, 1), 0)
        valid = jnp.where(token < spans[0], 1.0, 0.0)
        ob[r, :] = ((hat * g2[...] + s2[...]) * valid).astype(bf16)
        d = dy[r, :].astype(f32) * valid
        d2 = center_back(d * g2[...], hat, rs)
        two[r, :] = d2
        d2 = d2.astype(bf16)
        dd[r, :] = d2
        for i, term in enumerate((d2.astype(f32), d * hat, d)):
            sums[i] = sums[i] + colsum(term)
    put(ob, out)
    size = ff // PARTS
    stride = (send.shape[0] - SMALL) // PARTS
    write_group(lambda p: mm_tn(act[:, p * size : (p + 1) * size], dd[...]), send, keep, buf, gsems, place, stride)

    def downs(c):
        return [mm_nt(dd[r, :], wd[c : c + CHUNK, :]) for r in blocks]

    down = downs(0)
    for c in range(0, ff, CHUNK):
        cols = slice(c, c + CHUNK)
        now = down
        if c + CHUNK < ff:
            down = downs(c + CHUNK)
        total = 0.0
        for r, d in zip(blocks, now):
            du = (d_up[r, cols].astype(f32) * d).astype(bf16)
            d_up[r, cols] = du
            total = total + colsum(du.astype(f32))
        for half in range(0, CHUNK, CHUNK // 2):
            n, at = divmod(c + half, width)
            line[8 + n : 9 + n, at : at + CHUNK // 2] = total[:, half : half + CHUNK // 2]
        for r in blocks:
            two[r, :] += mm_nt(d_up[r, cols], wu[:, cols])
    for r in blocks:
        d_mid = two[r, :]
        hat = xh[r, :]
        d1 = center_back(d_mid * g1[...], hat, rstd[r, 0:1])
        two[r, :] = d1
        d1 = d1.astype(bf16)
        branch[r, :] = d1
        for i, term in enumerate((d_mid * hat, d_mid, d1.astype(f32))):
            sums[3 + i] = sums[3 + i] + colsum(term)
    put(two, d_one)
    for r in blocks:
        datt[r, :] = mm_nt(branch[r, :], wo[...]).astype(bf16)
        at = pl.ds(r.start, ROWS)
        put(datt.at[at], d_attn.at[at])
    put(datt.at[pl.ds(0, reach)], d_low)
    put(datt.at[pl.ds(tokens - reach, reach)], d_high)
    for r in range(0, width, width // 2):
        gout[r : r + width // 2, :] = mm_tn(attb[:, r : r + width // 2], branch[...]).astype(bf16)
    size = width // PARTS // 2
    waits = []
    for part in range(PARTS):
        source = lambda n, part=part: gout.at[pl.ds((2 * part + n) * size, size)]
        waits.append(piece_copies(part, place, source, hsems.at[part], send, keep, stride, stride - size))
    for i in range(6):
        line[i : i + 1, :] = sums[i]
    small[...] = line[...].astype(bf16)
    for to in (send, keep):
        put(small, to.at[pl.ds(PARTS * stride, SMALL)])
    for c in copies:
        c.wait()
    for wait in waits:
        wait()


def layer(place, spans, se, xl, xr, q, k, v, x, wk, wv, wo, wu, wd, dy, bv, bo, g1, s1, bu, bd, g2, s2):
    tokens, width = x.shape
    ff = wu.shape[1]
    reach = xl.shape[0]
    ext = tokens + 2 * reach
    shape = lambda n, t, rows=tokens: jax.ShapeDtypeStruct((rows, n), t)
    vm = lambda rows, n, t: pltpu.VMEM((rows, n), t)
    group = group_scratch(ff, width, 4)
    return call(
        layer_kernel,
        out_shape=(
            shape(ff, bf16),
            shape(width, bf16),
            shape(width, bf16, 2 * reach),
            shape(width, bf16, 2 * reach),
            shape(width, bf16),
            shape(width, f32),
            shape(width, bf16),
            shape(width, bf16, reach),
            shape(width, bf16, reach),
        )
        + group_shapes((ff + width) // PARTS // 2, width, SMALL),
        in_specs=[SMEM, SMEM, KEPT] + [VMEM] * 8 + [FREE, FREE] + [KEPT] * 6 + [HBM] * 4,
        out_specs=(KEPT, KEPT) + (HBM,) * 9,
        scratch_shapes=[
            vm(width, width, bf16),
            vm(width, ff, bf16),
            vm(ff, width, bf16),
            vm(tokens, width, bf16),
            pltpu.SemaphoreType.DMA((4,)),
            vm(ext, width, bf16),
            vm(ext, width, bf16),
            vm(tokens, width, bf16),
            vm(tokens, ff, bf16),
            vm(tokens, width, f32),
            vm(tokens, 128, f32),
            vm(tokens, width, f32),
            vm(tokens, width, bf16),
            vm(tokens, width, bf16),
            vm(tokens, width, bf16),
            vm(tokens, width, bf16),
            vm(width, width, bf16),
            vm(SMALL, width, f32),
            vm(SMALL, width, bf16),
            group[0],
            pltpu.SemaphoreType.DMA((10 + len(row_blocks(tokens)),)),
            group[1],
            pltpu.SemaphoreType.DMA((PARTS, 2)),
        ],
        compiler_params=params(46),
        cost_estimate=cost(4 * tokens * width * (width + 3 * ff) + 8e9, 40 * tokens * width, 2 * tokens * ff),
        name="layer",
    )(place, spans, se, bv, bo, g1, s1, bu, bd, g2, s2, xl, xr, q, k, v, x, wk, wv, wo, wu, wd, dy)


def up_grad_kernel(place, mid_low, d_up, send, keep, buf, gsems):
    width = mid_low.shape[1]
    size = width // 2

    def block(part):
        rows, cols = (part % 2) * size, (part // 2) * width
        return mm_tn(mid_low[:, rows : rows + size], d_up[:, cols : cols + width])

    write_group(block, send, keep, buf, gsems, place, size // 2)


def up_grad(place, mid_low, d_up, after=()):
    tokens, width = mid_low.shape
    ff = d_up.shape[1]
    return call(
        up_grad_kernel,
        out_shape=group_shapes(width // 4, width),
        in_specs=[SMEM, KEPT, KEPT],
        out_specs=(HBM, HBM),
        scratch_shapes=group_scratch(ff, width),
        after=after,
        compiler_params=params(12),
        cost_estimate=cost(2 * tokens * width * ff, 14 * tokens * width),
        name="up_grad",
    )(place, mid_low, d_up)


def rest_grad_kernel(halves, place, x, *refs):
    parts, (send, keep, xb, rhs, grad, small, gsems, sems, ssems) = refs[: 3 * halves], refs[3 * halves :]
    tokens, width = x.shape
    size = width // 2
    some = width // halves
    pairs = [(x, xb)]
    for n in range(3):
        for h in range(halves):
            pairs.append((parts[3 * h + n], rhs.at[n, :, pl.ds(h * some, some)]))
    ready = loads(pairs, sems)
    ready(0)
    stride = 3 * width // PARTS // 2
    waits = []
    for done in range(0, 3 * width, size):
        which = done // width
        if done % width == 0:
            for h in range(halves):
                ready(1 + which * halves + h)
        at = done % width
        grad[done : done + size, :] = mm_tn(xb[:, at : at + size], rhs[which]).astype(bf16)
        while 2 * stride * (len(waits) + 1) <= done + size:
            part = len(waits)
            source = lambda n, part=part: grad.at[pl.ds((2 * part + n) * stride, stride)]
            waits.append(piece_copies(part, place, source, gsems.at[part], send, keep, stride))
    ones = jnp.ones((8, tokens), bf16)
    row = lax.broadcasted_iota(i32, (8, width), 0)
    sums = jnp.where(row == 0, mm(ones, rhs[0]), jnp.where(row == 1, mm(ones, rhs[2]), 0.0))
    small[...] = jnp.concatenate([sums, jnp.zeros((SMALL - 8, width), f32)], axis=0).astype(bf16)
    end = pl.ds(PARTS * stride, SMALL)
    copies = [out_copy(small, o.at[end], ssems.at[i]) for i, o in enumerate((send, keep))]
    for c in copies:
        c.wait()
    for wait in waits:
        wait()


def rest_grad(place, x, parts, after=()):
    tokens, width = x.shape
    halves = len(parts)
    return call(
        functools.partial(rest_grad_kernel, halves),
        out_shape=group_shapes(3 * width // PARTS // 2, width, SMALL),
        in_specs=[SMEM] + [HBM] * (1 + 3 * halves),
        out_specs=(HBM, HBM),
        scratch_shapes=[
            pltpu.VMEM((tokens, width), bf16),
            pltpu.VMEM((3, tokens, width), bf16),
            pltpu.VMEM((3 * width, width), bf16),
            pltpu.VMEM((SMALL, width), bf16),
            pltpu.SemaphoreType.DMA((PARTS, 2)),
            pltpu.SemaphoreType.DMA((1 + 3 * halves,)),
            pltpu.SemaphoreType.DMA((2,)),
        ],
        after=after,
        compiler_params=params(20),
        cost_estimate=cost(6 * tokens * width * width, 20 * tokens * width),
        name="rest_grad",
    )(place, x, *sum(map(tuple, parts), ()))


def inputs_grad_kernel(halves, d_one, *refs):
    parts, (wq, wk, wv, out) = refs[: 3 * halves], refs[3 * halves :]
    total = d_one[...]
    some = wq.shape[1] // halves
    for h in range(halves):
        for g, w in zip(parts[3 * h : 3 * h + 3], (wq, wk, wv)):
            total = total + mm_nt(g[...], w[:, h * some : (h + 1) * some])
    out[...] = total


def inputs_grad(d_one, parts, wq, wk, wv, after=()):
    tokens, width = d_one.shape
    halves = len(parts)
    tok = lambda n: pl.BlockSpec((ROWS, n), lambda i: (i, 0))
    full = pl.BlockSpec((width, width), lambda i: (0, 0))
    return call(
        functools.partial(inputs_grad_kernel, halves),
        grid=(tokens // ROWS,),
        out_shape=(jax.ShapeDtypeStruct((tokens, width), f32),),
        in_specs=[tok(width)] + [tok(width // halves)] * (3 * halves) + [full] * 3,
        out_specs=(tok(width),),
        anywhere=True,
        after=after,
        compiler_params=params(16, dimension_semantics=("arbitrary",)),
        cost_estimate=cost(6 * tokens * width * width, 20 * tokens * width),
        name="inputs_grad",
    )(d_one, *sum(map(tuple, parts), ()), wq, wk, wv)


def swap(value, axis, bit):
    count = lax.axis_size(axis)
    return lax.ppermute(value, axis, [(i, i ^ bit) for i in range(count)])


def plus(a, b):
    return (a.astype(f32) + b.astype(f32)).astype(bf16)


def layer_bits():
    return list(range(1, lax.axis_size("dp")))


def far_bits():
    bit, bits = PARTS, []
    while bit < lax.axis_size("seq"):
        bits.append(bit)
        bit *= 2
    return bits


def axis_bits(axis):
    return [1 << n for n in range((lax.axis_size(axis) - 1).bit_length())]


class Sum:
    def __init__(self, send, keep, tail=0, used=None):
        self.mine, self.got, self.payload, self.tail = [keep], [], [send], tail
        self.used = tail if used is None else used
        self.swaps = [("seq", 1)]
        self.steps = self.run()

    def receive(self, token):
        if self.got:
            *self.got, _ = lax.optimization_barrier((*self.got, token))
            next(self.steps)

    def send(self):
        self.got = [swap(p, *s) for p, s in zip(self.payload, self.swaps)]

    def tailed(self, payloads):
        rows = [p.reshape(-1, p.shape[-1]) for p in payloads]
        if self.tail:
            rows[0] = jnp.concatenate([rows[0], self.small], axis=0)
        return rows

    def untailed(self, like):
        if self.tail:
            self.small = plus(self.small, self.got[0][-self.used :])
            self.got[0] = self.got[0][: -self.used]
        return [g.reshape(m.shape) for g, m in zip(self.got, like)]

    def run(self):
        keep, got = self.mine[0], self.got[0]
        width = keep.shape[-1]
        if self.tail:
            rows = slice(keep.shape[0] - self.tail, keep.shape[0] - self.tail + self.used)
            self.small = plus(keep[rows], got[rows])
            keep, got = keep[: -self.tail], got[: -self.tail]
        keep, got = (v.reshape((2, 2, 2, -1, width)) for v in (keep, got))
        keeps, gots = [keep[0], keep[1]], [got[0], got[1]]
        for bits in ((2, 4), (4, 2)):
            away = [plus(k[1], g[1]) for k, g in zip(keeps, gots)]
            keeps = [plus(k[0], g[0]) for k, g in zip(keeps, gots)]
            self.payload, self.swaps = self.tailed(away), [("seq", b) for b in bits]
            yield
            gots = self.untailed(keeps)
        parts = list(map(plus, keeps, gots))
        layers = axis_bits("dp")
        layer = lax.axis_index("dp")
        rows = parts[0].shape[0]
        part = jnp.stack(parts).reshape((2,) * len(layers) + (-1, width))
        for bit in layers:
            mine = (layer // bit) % 2
            keep = lax.dynamic_index_in_dim(part, mine, 0, keepdims=False)
            away = lax.dynamic_index_in_dim(part, 1 - mine, 0, keepdims=False)
            self.payload, self.swaps = self.tailed([away]), [("dp", bit)]
            yield
            part = plus(keep, self.untailed([keep])[0])
        for bit in far_bits():
            part = plus(part, swap(part, "seq", bit))
            if self.tail:
                self.small = plus(self.small, swap(self.small, "seq", bit))
        for bit in reversed(layers):
            self.payload, self.swaps = [part], [("dp", bit)]
            yield
            low = (layer // bit) % 2 == 0
            got = self.got[0]
            part = jnp.stack([jnp.where(low, part, got), jnp.where(low, got, part)])
        parts = list(part.reshape(2, rows, width))
        for bits in ((4, 2), (2, 4)):
            self.payload, self.swaps = parts, [("seq", b) for b in bits]
            yield
            parts = [jnp.stack(pair) for pair in zip(parts, self.got)]
        whole = jnp.stack(parts).reshape(8, -1, width)
        self.payload, self.swaps = [whole], [("seq", 1)]
        yield
        self.result = (whole, self.got[0])
        self.payload = []
        yield


def advance(token, *sums):
    for s in sums:
        s.receive(token)
    payloads = lax.optimization_barrier(tuple(p for s in sums for p in s.payload))
    at = 0
    for s in sums:
        s.payload = list(payloads[at : at + len(s.payload)])
        at += len(s.payload)
        s.send()
    return payloads[0] if payloads else token


def spread_kernel(kind, count, place, mine, other, *refs):
    outs, (buf, sems) = refs[:count], refs[count:]
    here = place[1]
    rows, width = mine.shape[1:]
    slots = buf.shape[0]
    waits = []
    for n in range(2 * PARTS):
        part, piece = n // 2, n % 2
        slot = n % slots
        if n >= slots:
            for c in waits[n - slots]:
                c.wait()
        to = part ^ here
        core, x, y = to & 1, (to >> 1) & 1, (to >> 2) & 1
        at = 4 + 2 * y + x if piece else 2 * x + y
        for side, source in ((0, mine), (1, other)):

            @pl.when(core == side)
            def _(source=source, slot=slot, at=at):
                buf[slot] = source[at].astype(f32)

        pairs = []
        if kind == "up":
            down = (part % 2) * 2 * rows + piece * rows
            pairs.append((0, rows, outs[0].at[pl.ds(down, rows), pl.ds((part // 2) * width, width)]))
        elif kind == "down":
            few = width // PARTS // 2
            pairs.append((0, rows - few, outs[0].at[pl.ds(n * (rows - few), rows - few)]))
            pairs.append((rows - few, few, outs[1].at[pl.ds(n * few, few)]))
        else:
            first, last = n * rows, (n + 1) * rows
            while first < last:
                which = first // width
                size = min(last, (which + 1) * width) - first
                pairs.append((first - n * rows, size, outs[which].at[pl.ds(first - which * width, size)]))
                first += size
        waits.append([out_copy(buf.at[slot, pl.ds(a, s)], o, sems.at[slot, i]) for i, (a, s, o) in enumerate(pairs)])
    for wait in waits[-slots:]:
        for c in wait:
            c.wait()


def spread(kind, place, mine, other, after=()):
    rows, width = mine.shape[1:]
    shapes = {
        "down": [(2 * PARTS * rows - width, width), (width, width)],
        "up": [(width, 2 * PARTS * rows)],
        "rest": [(width, width)] * 3,
    }[kind]
    slots = 6
    return call(
        functools.partial(spread_kernel, kind, len(shapes)),
        out_shape=[jax.ShapeDtypeStruct(s, f32) for s in shapes],
        in_specs=[SMEM, FREE, FREE],
        out_specs=[HBM] * len(shapes),
        after=after,
        scratch_shapes=[pltpu.VMEM((slots, rows, width), f32), pltpu.SemaphoreType.DMA((slots, 2))],
        compiler_params=params(8),
        cost_estimate=cost(rows * width, 12 * PARTS * rows * width),
        name="spread_" + kind,
    )(place, mine, other)


def sum_small(vec):
    for axis in ("seq", "dp"):
        bit = 1
        while bit < lax.axis_size(axis):
            vec = vec + swap(vec, axis, bit)
            bit *= 2
    return vec


def neighbours(first, last):
    count = lax.axis_size("seq")
    up = [(i, i + 1) for i in range(count - 1)]
    low = lax.ppermute(last, "seq", up)
    high = lax.ppermute(first, "seq", [(b, a) for a, b in up])
    return low, high


def body(
    inputs, lengths, w_query, b_query, w_key, w_value, b_value, w_out, b_out, gain_one, shift_one,
    w_up, b_up, w_down, b_down, gain_two, shift_two, d_output,
):
    rows, tokens, width = inputs.shape
    reach = ITEM_MOST
    here = lax.axis_index("seq")
    place = jnp.stack([here * tokens, here & (PARTS - 1), lax.axis_index("dp")]).astype(i32)
    x = inputs.reshape(tokens, width)
    dy = d_output.reshape(tokens, width)

    xl, xr = neighbours(x[:reach], x[-reach:])
    se, spans, se_low, spans_low, q, k, v, *kept = front(
        place, lengths, x, w_query, w_key, w_value, b_query, b_value, reach
    )
    d_up, mid_low, kh, vh, output, d_one, d_attn, d_low, d_high, send1, keep1 = layer(
        place, spans, se, xl, xr, *kept, w_out, w_up, w_down, dy, b_value, b_out, gain_one, shift_one, b_up, b_down, gain_two, shift_two
    )
    one = Sum(send1, keep1, SMALL)
    token = advance(d_attn, one)
    dl, dr = neighbours(d_low, d_high)
    send2, keep2 = up_grad(place, mid_low, d_up, after=[token])
    dl, dr, send2 = lax.optimization_barrier((dl, dr, send2))
    two = Sum(send2, keep2)
    token = advance(send2, one, two)
    args = (HALVES, spans_low, se_low, q, k, v, d_attn, kh, vh, xl, xr, dl, dr, w_query, b_query)
    parts = [attend_back(0, *args, after=[token])]
    token = advance(parts[0][0], one, two)
    parts.append(attend_back(1, *args, after=[token]))
    token = advance(parts[1][0], one)
    send3, keep3 = rest_grad(place, x, parts, after=[token])
    three = Sum(send3, keep3, SMALL, 8)
    token = advance(send3, one, two, three)
    sums = {1: one, 2: two, 3: three}
    for event in ORDER:
        if event == 0:
            (d_inputs,) = inputs_grad(d_one, parts, w_query, w_key, w_value, after=[token])
            token = d_inputs
        elif event < 0:
            kind = ("down", "up", "rest")[-event - 1]
            grads = spread(kind, place, *sums[-event].result, after=[token])
            token = grads[0]
            if kind == "down":
                g_w_down, g_w_out = grads
            elif kind == "up":
                (g_w_up,) = grads
            else:
                g_w_query, g_w_key, g_w_value = grads
        else:
            token = advance(token, *[sums[int(g)] for g in str(event)])
    small = jnp.concatenate([one.small, three.small], axis=0).astype(f32)
    ff = w_up.shape[1]
    many = ff // width
    return (
        output.reshape(rows, tokens, width),
        d_inputs.reshape(rows, tokens, width),
        g_w_query,
        small[SMALL],
        g_w_key,
        g_w_value,
        small[SMALL + 1],
        g_w_out,
        small[5],
        small[3],
        small[4],
        g_w_up,
        small[8 : 8 + many].reshape(ff),
        g_w_down,
        small[0],
        small[1],
        small[2],
    )


def solution(mesh):
    split, whole = P("dp", "seq", None), P()
    return jax.shard_map(
        body,
        mesh=mesh,
        in_specs=(split, P("dp", None)) + (whole,) * 15 + (split,),
        out_specs=(split, split) + (whole,) * 15,
        check_vma=False,
    )
```
